32 devices in a mesh: img: 2 (over x), row: 4 (over z), col: 4 (over y, core).
Axes of the slice: x: 2, y: 2, z: 4, core: 2. Of those that a mesh axis runs over, the one named last changes fastest.
Arguments:
- tokens: bfloat16 [8, 32, 32, 1152], P('img', 'row', 'col'), may hold values from -6 to 6
- condition: bfloat16 [8, 1152], P('img'), may hold values from -6 to 6
- valid: int32 [8], P('img'), may hold values from 0 to 1, as said below
- positions: int32 [2, 8, 32, 32], P(None, 'img', 'row', 'col'), may hold values from 0 to 93, as said below
- w_qkv: bfloat16 [1152, 3456], P('img'), may hold values from -0.1875 to 0.1875
- w_out: bfloat16 [1152, 1152], P('img'), may hold values from -1.5 to 1.5
- w_up: bfloat16 [1152, 6144], P('img'), may hold values from -0.1875 to 0.1875
- w_down: bfloat16 [3072, 1152], P('img'), may hold values from -0.109375 to 0.109375
- w_ada: bfloat16 [1152, 6912], P(None, ('row', 'col')), may hold values from -0.25 to 0.25
- qk_gain: float32 [2, 72], replicated, may hold values from 0.1 to 1.9
- cotangent: bfloat16 [8, 32, 32, 1152], P('img', 'row', 'col'), may hold values from -6 to 6
Outputs:
- output: bfloat16 [8, 32, 32, 1152], P('img', 'row', 'col')
- grad_tokens: float32 [8, 32, 32, 1152], P('img', 'row', 'col')
- grad_condition: float32 [8, 1152], P('img')
- grad_w_qkv: float32 [1152, 3456], P('img')
- grad_w_out: float32 [1152, 1152], P('img')
- grad_w_up: float32 [1152, 6144], P('img')
- grad_w_down: float32 [3072, 1152], P('img')
- grad_w_ada: float32 [1152, 6912], P(None, ('row', 'col'))
- grad_qk_gain: float32 [2, 72], replicated
The draws below stay inside these ranges and needn't reach their ends.
Inputs may be any that keep to these rules, and one draw needn't show every extreme that they name: Of the 4 images that one index of img holds, 1 to 4 are valid; some group has all 4 valid. `positions`: each image has a stride of 1 to 3 for rows and one for columns; a patch's row position is its row index times the row stride, its column position its column index times the column stride. Some image has stride 3 along each.
All inputs are finite; a program needn't handle non-finite values.
Results may differ from the reference program's by a relative error of at most 0.018.
Values may be sent and summed in bfloat16 or wider, within the bound.
No kernel may reach another device: no remote copies, remote signals or barrier semaphores. Data moves between devices by JAX's collectives and lax.ppermute only.
A program may use at most 256 MiB of HBM per device.

```python
import math
import jax
import jax.numpy as jnp
from jax import lax

D = 1152
HD = 72
FF = 3072
GRID = 32
B_DEV = 4
IMAGES = 8


def draw_valid(key, part):
    key = jax.random.fold_in(key, 11)
    groups = IMAGES // B_DEV
    uniform_pick = jax.random.randint(jax.random.fold_in(key, 1), (groups,), 1, B_DEV + 1)
    counts = jnp.clip(uniform_pick * uniform_pick * uniform_pick // (B_DEV * B_DEV), 1, max(1, B_DEV - 1))
    fullest = jax.random.randint(jax.random.fold_in(key, 2), (), 0, groups)
    counts = jnp.where(jnp.arange(groups) == fullest, B_DEV, counts)
    scores = jax.random.randint(jax.random.fold_in(key, 3), (groups, B_DEV), 0, 1 << 20) * B_DEV + jnp.arange(B_DEV)[None, :]
    ranking = jnp.argsort(jnp.argsort(scores, axis=1), axis=1)
    return (ranking < counts[:, None]).astype(jnp.int32).reshape(IMAGES)


def draw_positions(key, part):
    key = jax.random.fold_in(key, 23)
    strides = jax.random.randint(jax.random.fold_in(key, 1), (2, IMAGES), 1, 4)
    chosen = jax.random.randint(jax.random.fold_in(key, 2), (2,), 0, IMAGES)
    strides = jnp.where(jnp.arange(IMAGES)[None, :] == chosen[:, None], 3, strides)
    index_line = jnp.arange(GRID)
    row_part = jnp.broadcast_to(strides[0][:, None, None] * index_line[:, None], (IMAGES, GRID, GRID))
    col_part = jnp.broadcast_to(strides[1][:, None, None] * index_line[None, :], (IMAGES, GRID, GRID))
    return jnp.stack([row_part, col_part]).astype(jnp.int32)


def steps_of(key, extent, cuts, low, largest):
    gain = 1.0
    for position, shards_of in cuts:
        heights = jax.random.uniform(jax.random.fold_in(jax.random.fold_in(key, 6), position), (shards_of,), jnp.float32, low / len(cuts), largest / len(cuts))
        gain = gain * jnp.repeat(jnp.exp(heights), extent[position] // shards_of).reshape((-1,) + (1,) * (len(extent) - 1 - position))
    return gain


def scatter_about(stream_key, shape, deviation, limit, cuts=(), kind=jnp.bfloat16):
    loudness = steps_of(stream_key, shape, cuts, -0.22, 0.18) if cuts else 1.0
    drawn = jax.random.normal(stream_key, shape, jnp.float32) * deviation * loudness
    return jnp.minimum(jnp.maximum(drawn, -limit), limit).astype(kind)


def setup_inputs(seed: int = 0) -> dict:
    keys = jax.random.split(jax.random.key(seed), 12)
    return {
        "tokens": scatter_about(keys[0], (IMAGES, GRID, GRID, D), 1.0, 6.0, ((0, 2), (1, 4), (2, 4))),
        "condition": scatter_about(keys[1], (IMAGES, D), 1.0, 6.0, ((0, 2),)),
        "valid": draw_valid(jax.random.fold_in(keys[11], 71), 0),
        "positions": draw_positions(jax.random.fold_in(keys[11], 71), 0),
        "w_qkv": scatter_about(keys[4], (D, 3 * D), D ** -0.5, 0.1875, ((0, 2),)),
        "w_out": scatter_about(keys[5], (D, D), (D // 64) ** -0.5, 1.5, ((0, 2),)),
        "w_up": scatter_about(keys[6], (D, 2 * FF), D ** -0.5, 0.1875, ((0, 2),)),
        "w_down": scatter_about(keys[7], (FF, D), FF ** -0.5, 0.109375, ((0, 2),)),
        "w_ada": scatter_about(keys[8], (D, 6 * D), (D // 2) ** -0.5, 0.25, ((1, 16),)),
        "qk_gain": jnp.clip(1.0 + 0.18 * jax.random.normal(keys[9], (2, HD), jnp.float32), 0.1, 1.9),
        "cotangent": scatter_about(keys[10], (IMAGES, GRID, GRID, D), 1.0, 6.0, ((0, 2), (1, 4), (2, 4))),
    }


@jax.custom_vjp
def low(v):
    return lax.optimization_barrier(v.astype(jnp.bfloat16)).astype(jnp.float32)

@jax.custom_vjp
def low_back(v):
    return v

def low_keep(v):
    return (low(v), None)

def low_pass(kept, grad):
    return (grad,)

def back_keep(v):
    return (v, None)

def back_low(kept, grad):
    return (low(grad),)
low.defvjp(low_keep, low_pass)
low_back.defvjp(back_keep, back_low)
epsilon = 1e-06
precise = lax.Precision.HIGHEST

def rms_norm(values):
    return values * lax.rsqrt(lax.optimization_barrier(jnp.mean(values * values, axis=-1, keepdims=True)) + epsilon)

def tables(positions, pair_count):
    frequency = jnp.exp(-math.log(10000.0) * jnp.arange(pair_count, dtype=jnp.float32) / pair_count)
    angles = jnp.moveaxis(positions.astype(jnp.float32)[..., None] * frequency, 0, -2)
    return (jnp.cos(angles), jnp.sin(angles))

def rotate(vectors, cos_table, sin_table):
    pair_count = vectors.shape[-1] // 4
    shaped = vectors.reshape(vectors.shape[:-1] + (2, 2, pair_count))
    leading = shaped[..., 0, :]
    trailing = shaped[..., 1, :]
    turned = jnp.stack([leading * cos_table - trailing * sin_table, leading * sin_table + trailing * cos_table], axis=-2)
    return turned.reshape(vectors.shape)

def prepare(joined_pair, qk_gain, cos_table, sin_table):
    normed = rms_norm(joined_pair) * qk_gain[:, None, :]
    return rotate(normed, cos_table, sin_table)

def forward(params, tokens, condition, valid_float, cos_table, sin_table):
    w_qkv, w_out, w_up, w_down, w_ada, qk_gain = params
    image_count, length, model_width = tokens.shape
    head_dim = qk_gain.shape[1]
    head_count = model_width // head_dim
    modulation = low_back(jnp.dot(low(jax.nn.silu(condition)), w_ada, precision=precise))
    offset_one, stretch_one, gate_one, offset_two, stretch_two, gate_two = jnp.split(modulation, 6, axis=1)
    gate_attn = gate_one * valid_float[:, None]
    gate_mlp = gate_two * valid_float[:, None]
    attn_in = low(rms_norm(tokens) * (1.0 + stretch_one[:, None, :]) + offset_one[:, None, :])
    joined = low_back(jnp.einsum('gtd,de->gte', attn_in, w_qkv, precision=precise))
    joined = joined.reshape(image_count, length, 3, head_count, head_dim)
    rotated = low(prepare(joined[:, :, :2], qk_gain, cos_table, sin_table))
    value_rows = low(joined[:, :, 2])
    factor = head_dim ** (-0.5)
    scores = low_back(jnp.einsum('gqhe,gkhe->ghqk', rotated[:, :, 0], rotated[:, :, 1], precision=precise) * factor)
    probability = jax.nn.softmax(scores, axis=-1)
    mixed = jnp.einsum('ghqk,gkhe->gqhe', low(probability), value_rows, precision=precise)
    mixed = low(low_back(mixed.reshape(image_count, length, model_width)))
    branch = low_back(jnp.einsum('gtd,de->gte', mixed, w_out, precision=precise))
    hidden_res = tokens + gate_attn[:, None, :] * branch
    mlp_in = low(rms_norm(hidden_res) * (1.0 + stretch_two[:, None, :]) + offset_two[:, None, :])
    gate_up = low_back(jnp.einsum('gtd,df->gtf', mlp_in, w_up, precision=precise))
    half_width = gate_up.shape[-1] // 2
    activated = low(jax.nn.silu(gate_up[..., :half_width]) * gate_up[..., half_width:])
    mlp_out = low_back(jnp.einsum('gtf,fd->gtd', activated, w_down, precision=precise))
    return hidden_res + gate_mlp[:, None, :] * mlp_out

def reference(tokens, condition, valid, positions, w_qkv, w_out, w_up, w_down, w_ada, qk_gain, cotangent):
    group = math.gcd(IMAGES, 4)
    steps = IMAGES // group
    length = GRID * GRID
    pair_count = HD // 4
    params = tuple((member.astype(jnp.float32) for member in (w_qkv, w_out, w_up, w_down, w_ada, qk_gain)))
    token_groups = tokens.astype(jnp.float32).reshape(steps, group, length, D)
    cond_groups = condition.astype(jnp.float32).reshape(steps, group, D)
    valid_groups = valid.astype(jnp.float32).reshape(steps, group)
    cos_table, sin_table = tables(positions.reshape(2, IMAGES, length), pair_count)
    cos_groups = cos_table[:, :, None, None].reshape(steps, group, length, 1, 1, 2, pair_count)
    sin_groups = sin_table[:, :, None, None].reshape(steps, group, length, 1, 1, 2, pair_count)
    cot_groups = cotangent.astype(jnp.float32).reshape(steps, group, length, D)

    def step(totals, inputs):
        token_part, cond_part, valid_part, cos_part, sin_part, cot_part = inputs

        def local_forward(weights_in, tokens_in, cond_in):
            return forward(weights_in, tokens_in, cond_in, valid_part, cos_part, sin_part)
        result, pullback = jax.vjp(local_forward, params, token_part, cond_part)
        grad_params, grad_token_part, grad_cond_part = pullback(cot_part)
        totals = jax.tree.map(lambda running, added: running + added, totals, grad_params)
        return (totals, (result.astype(jnp.bfloat16), grad_token_part, grad_cond_part))
    zeros_start = jax.tree.map(jnp.zeros_like, params)
    totals, (outputs, grad_token_all, grad_cond_all) = lax.scan(step, zeros_start, (token_groups, cond_groups, valid_groups, cos_groups, sin_groups, cot_groups))
    output = outputs.reshape(IMAGES, GRID, GRID, D)
    grad_tokens = grad_token_all.reshape(IMAGES, GRID, GRID, D)
    grad_condition = grad_cond_all.reshape(IMAGES, D)
    return (output, grad_tokens, grad_condition, totals[0], totals[1], totals[2], totals[3], totals[4], totals[5])
```

```python
import functools
import math

import jax
import jax.numpy as jnp
from jax import lax
from jax.experimental import pallas as pl
from jax.experimental.pallas import tpu as pltpu
from jax.sharding import PartitionSpec as P

LANES=128
epsilon=1e-6

def lane_iota(shape):
    return lax.broadcasted_iota(jnp.int32, shape, len(shape)-1)

def turn(x, cos, sin_a, sin_b, shift):
    return x*cos + pltpu.roll(x, LANES-shift, 1)*sin_a + pltpu.roll(x, shift, 1)*sin_b

def attn_fwd_kernel(head_dim, pairs, scale, q_ref, k_ref, v_ref, cos_ref, sa_ref, sb_ref, gain_ref, o_ref, qa_ref, ka_ref, va_ref):
    tokens = q_ref.shape[0]
    cos, sa, sb = cos_ref[...], sa_ref[...], sb_ref[...]
    def normed(x):
        return x*lax.rsqrt(jnp.sum(x*x, axis=-1, keepdims=True)*(1.0/head_dim)+epsilon)
    q = turn(normed(q_ref[...])*gain_ref[0:1,:], cos, sa, sb, pairs)*scale
    k = turn(normed(k_ref[...])*gain_ref[1:2,:], cos, sa, sb, pairs)
    lane = lane_iota((tokens, LANES))
    extra = (lane==head_dim)|(lane==head_dim+1)
    ka_ref[...] = jnp.where(extra, 1.0, k).astype(jnp.bfloat16)
    va_ref[...] = jnp.where(extra, -1.0, v_ref[...]).astype(jnp.bfloat16)
    q_low = q.astype(jnp.bfloat16)
    rows = 256
    kk = ka_ref[...]
    vv = va_ref[...]
    for s in range(tokens//rows):
        qs = q_low[s*rows:(s+1)*rows]
        scores = lax.dot_general(qs, kk, (((1,),(1,)),((),())), preferred_element_type=jnp.float32)
        weights = jnp.exp2(scores).astype(jnp.bfloat16)
        out = jnp.dot(weights, vv, preferred_element_type=jnp.float32)
        total = -out[:, head_dim:head_dim+1]
        lane_s = lane[s*rows:(s+1)*rows]
        o_ref[s*rows:(s+1)*rows, :] = jnp.where(lane_s<head_dim, out*(1.0/total), 0.0).astype(jnp.bfloat16)
        lse = -jnp.log2(total)
        hi = lse.astype(jnp.bfloat16).astype(jnp.float32)
        lo = lse-hi
        qf = q[s*rows:(s+1)*rows]
        qf = jnp.where(lane_s==head_dim, hi, jnp.where(lane_s==head_dim+1, lo, qf))
        qa_ref[s*rows:(s+1)*rows, :] = qf.astype(jnp.bfloat16)

def attn_fwd(joined, cos, sa, sb, gain, head_dim):
    tokens, width = joined.shape
    heads = width//(3*LANES)
    scale = head_dim**-0.5*math.log2(math.e)
    blk = lambda off: pl.BlockSpec((tokens, LANES), lambda h: (0, off+h))
    full = pl.BlockSpec((tokens, LANES), lambda h: (0,0))
    outs = tuple(jax.ShapeDtypeStruct((tokens, heads*LANES), jnp.bfloat16) for _ in range(4))
    return pl.pallas_call(functools.partial(attn_fwd_kernel, head_dim, head_dim//4, scale),
        grid=(heads,), in_specs=[blk(0), blk(heads), blk(2*heads), full, full, full, pl.BlockSpec((2,LANES), lambda h:(0,0))],
        out_specs=tuple(blk(0) for _ in range(4)), out_shape=outs,
        compiler_params=pltpu.CompilerParams(vmem_limit_bytes=40*1024*1024),
        cost_estimate=pl.CostEstimate(flops=4*heads*tokens*tokens*LANES, bytes_accessed=10*1024*1024, transcendentals=heads*tokens*tokens),
        name="attn_fwd")(joined, joined, joined, cos, sa, sb, gain)

def attn_bwd_kernel(head_dim, pairs, scale, q_ref, k_ref, qa_ref, ka_ref, va_ref, o_ref, do_ref, cos_ref, sa_ref, sb_ref, gain_ref, gq_ref, gk_ref, gv_ref, gg_ref, dk_acc, dv_acc, dq_acc):
    tokens = q_ref.shape[0]
    h = pl.program_id(0)
    lane = lane_iota((tokens, LANES))
    do_f = do_ref[...].astype(jnp.float32)
    delta = jnp.sum(do_f*o_ref[...].astype(jnp.float32), axis=-1, keepdims=True)
    hi = delta.astype(jnp.bfloat16).astype(jnp.float32)
    lo = delta-hi
    do_a = jnp.where(lane==head_dim, hi, jnp.where(lane==head_dim+1, lo, do_f)).astype(jnp.bfloat16)
    qa = qa_ref[...]; ka = ka_ref[...]; va = va_ref[...]
    ka_t = ka.T
    cols = 256
    for s in range(tokens//cols):
        qs = qa[s*cols:(s+1)*cols]
        ds = do_a[s*cols:(s+1)*cols]
        st = lax.dot_general(ka, qs, (((1,),(1,)),((),())), preferred_element_type=jnp.float32)
        pt = jnp.exp2(st)
        dpt = lax.dot_general(va, ds, (((1,),(1,)),((),())), preferred_element_type=jnp.float32)
        dst = (pt*dpt).astype(jnp.bfloat16)
        ptl = pt.astype(jnp.bfloat16)
        dv = jnp.dot(ptl, ds, preferred_element_type=jnp.float32)
        dk = jnp.dot(dst, qs, preferred_element_type=jnp.float32)
        if s == 0:
            dv_acc[...] = dv; dk_acc[...] = dk
        else:
            dv_acc[...] += dv; dk_acc[...] += dk
        dq_acc[:, s*cols:(s+1)*cols] = jnp.dot(ka_t, dst, preferred_element_type=jnp.float32)
    inside = lane < head_dim
    cos, sa, sb = cos_ref[...], sa_ref[...], sb_ref[...]
    def back(g, x, gain):
        g = jnp.where(inside, g, 0.0)
        g = g*cos - pltpu.roll(g, LANES-pairs, 1)*sa - pltpu.roll(g, pairs, 1)*sb
        inv = lax.rsqrt(jnp.sum(x*x, axis=-1, keepdims=True)*(1.0/head_dim)+epsilon)
        n = x*inv
        gg = jnp.sum(g*n, axis=0, keepdims=True)
        g = g*gain
        return (g - n*(jnp.sum(g*n, axis=-1, keepdims=True)*(1.0/head_dim)))*inv, gg
    gq, ggq = back(dq_acc[...].T*(head_dim**-0.5), q_ref[...], gain_ref[0:1,:])
    gk, ggk = back(dk_acc[...]*math.log(2.0), k_ref[...], gain_ref[1:2,:])
    gq_ref[...] = gq.astype(jnp.bfloat16)
    gk_ref[...] = gk.astype(jnp.bfloat16)
    gv_ref[...] = jnp.where(inside, dv_acc[...], 0.0).astype(jnp.bfloat16)
    gg = jnp.concatenate([ggq, ggk], axis=0)
    @pl.when(h==0)
    def _(): gg_ref[...] = gg
    @pl.when(h>0)
    def _(): gg_ref[...] += gg

def attn_bwd(joined, qa, ka, va, o, do, cos, sa, sb, gain, head_dim):
    tokens, width = joined.shape
    heads = width//(3*LANES)
    blk = lambda off: pl.BlockSpec((tokens, LANES), lambda h: (0, off+h))
    full = pl.BlockSpec((tokens, LANES), lambda h: (0,0))
    small = pl.BlockSpec((2,LANES), lambda h:(0,0))
    o1 = jax.ShapeDtypeStruct((tokens, heads*LANES), jnp.bfloat16)
    return pl.pallas_call(functools.partial(attn_bwd_kernel, head_dim, head_dim//4, 0.0),
        grid=(heads,), in_specs=[blk(0), blk(heads), blk(0), blk(0), blk(0), blk(0), blk(0), full, full, full, small],
        out_specs=(blk(0), blk(0), blk(0), small), out_shape=(o1, o1, o1, jax.ShapeDtypeStruct((2,LANES), jnp.float32)),
        scratch_shapes=[pltpu.VMEM((tokens,LANES),jnp.float32), pltpu.VMEM((tokens,LANES),jnp.float32), pltpu.VMEM((LANES,tokens),jnp.float32)],
        compiler_params=pltpu.CompilerParams(vmem_limit_bytes=48*1024*1024),
        cost_estimate=pl.CostEstimate(flops=10*heads*tokens*tokens*LANES, bytes_accessed=14*1024*1024, transcendentals=heads*tokens*tokens),
        name="attn_bwd")(joined, joined, qa, ka, va, o, do, cos, sa, sb, gain)


def bits_of(size):
    return [1 << b for b in reversed(range(size.bit_length() - 1))]


def swap(value, axis, size, bit):
    return lax.ppermute(value, axis, [(a, a ^ bit) for a in range(size)])


def spread(value, axis, size):
    for bit in bits_of(size):
        value = jnp.concatenate([value, swap(value, axis, size, bit)], axis=0)
    return value


def gather_sum(value, axis, size):
    for bit in reversed(bits_of(size)):
        half = value.shape[0] // 2
        other = swap(value[half:].astype(jnp.bfloat16), axis, size, bit)
        value = value[:half].astype(jnp.float32) + other.astype(jnp.float32)
    return value


def block_order(size):
    order = [0]
    for bit in bits_of(size):
        order = order + [o ^ bit for o in order]
    return order


def scatter_rows(value, axis, size, me):
    pieces = [lax.dynamic_index_in_dim(value, me ^ k, 0, keepdims=True) for k in range(size)]
    return [pieces[0]] + [swap(pieces[k], axis, size, k) for k in range(1, size)]


def total(value, axis, size):
    for bit in reversed(bits_of(size)):
        value = value + swap(value, axis, size, bit)
    return value


def assemble_columns_kernel(parts, order_ref, x_ref, o_ref):
    count, _, rows, width = x_ref.shape
    piece = width // parts
    for dest in range(count):
        block = x_ref[order_ref[dest], 0].astype(jnp.float32)
        for p in range(parts):
            start = (p * count + dest) * piece
            o_ref[:, start : start + piece] = block[:, p * piece : (p + 1) * piece]


def assemble_columns(stacked, order, parts):
    count, tiles, rows, width = stacked.shape
    return pl.pallas_call(
        functools.partial(assemble_columns_kernel, parts),
        grid_spec=pltpu.PrefetchScalarGridSpec(
            num_scalar_prefetch=1,
            grid=(tiles,),
            in_specs=[pl.BlockSpec((count, 1, rows, width), lambda z, o: (0, o[count + z], 0, 0))],
            out_specs=pl.BlockSpec((rows, count * width), lambda z, o: (z, 0)),
        ),
        out_shape=jax.ShapeDtypeStruct((tiles * rows, count * width), jnp.float32),
        compiler_params=pltpu.CompilerParams(vmem_limit_bytes=40 * 1024 * 1024),
        cost_estimate=pl.CostEstimate(flops=0, bytes_accessed=6 * stacked.size, transcendentals=0),
        name="assemble_columns",
    )(order, stacked)


def assemble_rows_kernel(order_ref, x_ref, o_ref):
    _, tiles, rows, width = x_ref.shape
    length = o_ref.shape[0]
    for z in range(tiles):
        start = z * rows
        n = min(rows, length - start)
        o_ref[start : start + n] = x_ref[0, order_ref[z], :n].astype(jnp.float32)


def assemble_rows(stacked, order, length):
    count, tiles, rows, width = stacked.shape
    return pl.pallas_call(
        lambda o, x, y: assemble_rows_kernel(o.at[pl.ds(count, tiles)], x, y),
        grid_spec=pltpu.PrefetchScalarGridSpec(
            num_scalar_prefetch=1,
            grid=(count,),
            in_specs=[pl.BlockSpec((1, tiles, rows, width), lambda c, o: (o[c], 0, 0, 0))],
            out_specs=pl.BlockSpec((length, width), lambda c, o: (c, 0)),
        ),
        out_shape=jax.ShapeDtypeStruct((count * length, width), jnp.float32),
        compiler_params=pltpu.CompilerParams(vmem_limit_bytes=40 * 1024 * 1024),
        cost_estimate=pl.CostEstimate(flops=0, bytes_accessed=6 * stacked.size, transcendentals=0),
        name="assemble_rows",
    )(order, stacked)


def program(sizes, tokens, condition, valid, positions, w_qkv, w_out, w_up, w_down, w_ada, qk_gain, cotangent):
    n_img, n_row, n_col = sizes
    images, tile_rows, tile_cols, width = tokens.shape
    assert images == n_row
    tile = tile_rows * tile_cols
    head_dim = qk_gain.shape[1]
    pairs = head_dim // 4
    heads = width // head_dim
    my_heads = heads // n_col
    hidden = w_up.shape[1] // 2
    me_img, me_row, me_col = lax.axis_index("img"), lax.axis_index("row"), lax.axis_index("col")
    order_col, order_row = block_order(n_col), list(range(n_row))
    halves = 2
    low, wide = jnp.bfloat16, jnp.float32

    def dot(a, b, dims=((1,), (0,))):
        return lax.dot_general(a, b, (dims, ((), ())), preferred_element_type=jnp.float32)

    def to_image(array):
        flat = array.reshape(images, tile, width)
        own = jnp.concatenate([p[0] for p in scatter_rows(flat, "row", n_row, me_row)], axis=0)
        return spread(own, "col", n_col)

    def from_image(own):
        blocks = own.reshape(n_row, tile, width)
        got = [blocks[0]] + [swap(blocks[k], "row", n_row, k) for k in range(1, n_row)]
        stack = jnp.stack(got, axis=0)
        return jnp.concatenate(
            [lax.dynamic_index_in_dim(stack, me_row ^ b, 0, keepdims=True) for b in range(images)], axis=0
        ).reshape(images, tile_rows, tile_cols, width)

    def cut_columns(w, parts):
        piece = w.shape[1] // (parts * n_col)
        return jnp.concatenate(
            [
                lax.dynamic_slice_in_dim(w, (p * n_col + me_col) * piece, piece, axis=1)
                for p in range(parts)
            ],
            axis=1,
        )

    def whole_rows(part):
        if n_img == 2:
            other = swap(part, "img", 2, 1)
            return jnp.where(me_img == 0, jnp.concatenate([part, other], 0), jnp.concatenate([other, part], 0))
        return lax.all_gather(part, "img", axis=0, tiled=True)

    def cut_rows(w):
        if n_img == 2:
            length = w.shape[0] // n_col
            return whole_rows(lax.dynamic_slice_in_dim(w, me_col * length, length, axis=0))
        full = lax.all_gather(w, "img", axis=0, tiled=True)
        length = full.shape[0] // (halves * n_col)
        return jnp.concatenate(
            [
                lax.dynamic_slice_in_dim(full, (h * n_col + me_col) * length, length, axis=0)
                for h in range(halves)
            ],
            axis=0,
        )

    tok = to_image(tokens)
    my_qkv = whole_rows(cut_columns(w_qkv, 3 * halves))
    cond = condition.astype(wide)
    silu_cond = jax.nn.silu(cond).astype(low)
    mod_columns = dot(silu_cond, w_ada)
    my_out = cut_rows(w_out)
    my_up = whole_rows(cut_columns(w_up, 2 * halves))
    my_down = cut_rows(w_down)
    cot = to_image(cotangent)

    mod_span = mod_columns.shape[1]
    mod_rel = jnp.concatenate(scatter_rows(mod_columns, "row", n_row, me_row), axis=0)
    mod_rel = spread(mod_rel, "col", n_col)
    source = jnp.stack(
        [(me_row ^ k) * n_col + (me_col ^ j) for j in order_col for k in order_row]
    )
    pick = source[None, :] == jnp.arange(n_row * n_col)[:, None]
    modulation = jnp.sum(jnp.where(pick[:, :, None], mod_rel[None], 0.0), axis=1).reshape(6, width)
    offset_one, stretch_one, gate_one, offset_two, stretch_two, gate_two = [modulation[g : g + 1] for g in range(6)]
    live = lax.dynamic_index_in_dim(valid, me_row, 0, keepdims=False).astype(wide)
    gate_attn = gate_one * live
    gate_mlp = gate_two * live

    steps = lax.dynamic_index_in_dim(positions, me_row, 1, keepdims=False)
    step_row = (steps[0, 1, 0] - steps[0, 0, 0]).astype(wide)
    step_col = (steps[1, 0, 1] - steps[1, 0, 0]).astype(wide)
    frequency = jnp.exp(-math.log(10000.0) * jnp.arange(pairs, dtype=wide) / pairs)
    row_index = jnp.stack([(me_row ^ k) * tile_rows + jnp.arange(tile_rows) for k in order_row])
    col_index = jnp.stack([(me_col ^ j) * tile_cols + jnp.arange(tile_cols) for j in order_col])
    row_angle = (row_index.astype(wide) * step_row)[..., None] * frequency
    col_angle = (col_index.astype(wide) * step_col)[..., None] * frequency
    shape = (n_col, n_row, tile_rows, tile_cols, pairs)

    def over(rows_part, cols_part):
        none = jnp.zeros(shape[:-1] + (LANES - head_dim,), wide)
        rows_part = [jnp.broadcast_to(a[None, :, :, None, :], shape) for a in rows_part]
        cols_part = [jnp.broadcast_to(a[:, None, None, :, :], shape) for a in cols_part]
        return jnp.concatenate(rows_part + cols_part + [none], axis=-1).reshape(-1, LANES)

    cos_r, sin_r, cos_c, sin_c = jnp.cos(row_angle), jnp.sin(row_angle), jnp.cos(col_angle), jnp.sin(col_angle)
    cos_all = over([cos_r, cos_r], [cos_c, cos_c])
    sin_a = over([-sin_r, jnp.zeros_like(sin_r)], [-sin_c, jnp.zeros_like(sin_c)])
    sin_b = over([jnp.zeros_like(sin_r), sin_r], [jnp.zeros_like(sin_c), sin_c])
    gain = jnp.pad(qk_gain, ((0, 0), (0, LANES - head_dim)))

    qkv_wide = jnp.pad(
        my_qkv.reshape(width, 3 * my_heads, head_dim), ((0, 0), (0, 0), (0, LANES - head_dim))
    ).reshape(width, 3 * my_heads * LANES)
    out_wide = jnp.pad(
        my_out.reshape(my_heads, head_dim, width), ((0, 0), (0, LANES - head_dim), (0, 0))
    ).reshape(my_heads * LANES, width)

    def inverse(v):
        return lax.rsqrt(jnp.mean(v * v, axis=-1, keepdims=True) + epsilon)

    residual = tok.astype(wide)
    attn_in = (residual * inverse(residual) * (1.0 + stretch_one) + offset_one).astype(low)
    joined = dot(attn_in, qkv_wide)
    mixed, q_aug, k_aug, v_aug = attn_fwd(joined, cos_all, sin_a, sin_b, gain, head_dim)
    branch = gather_sum(dot(mixed, out_wide), "col", n_col)
    own = branch.shape[0]
    own_tok = residual[:own]
    hidden_res = own_tok + gate_attn * branch
    inv_two = inverse(hidden_res)
    mlp_own = (hidden_res * inv_two * (1.0 + stretch_two) + offset_two).astype(low)
    mlp_in = spread(mlp_own, "col", n_col)
    gate_up = dot(mlp_in, my_up)
    half = gate_up.shape[1] // 2
    gate, up = gate_up[:, :half], gate_up[:, half:]
    sig = 1.0 / (1.0 + jnp.exp(-gate))
    act = (gate * sig * up).astype(low)
    mlp_out = gather_sum(dot(act, my_down), "col", n_col)
    output = from_image((hidden_res + gate_mlp * mlp_out).astype(low))

    grad_mlp = (gate_mlp * cot.astype(wide)).astype(low)
    cot_own = cot[:own].astype(wide)
    sums = [None] * 6
    sums[5] = live * jnp.sum(cot_own * mlp_out, axis=0, keepdims=True)
    grad_act = dot(grad_mlp, my_down, ((1,), (1,)))
    grad_gu = jnp.concatenate(
        [grad_act * up * sig * (1.0 + gate * (1.0 - sig)), grad_act * (gate * sig)], axis=1
    ).astype(low)
    grad_mlp_in = gather_sum(dot(grad_gu, my_up, ((1,), (1,))), "col", n_col)
    g_down = dot(act, grad_mlp, ((0,), (0,)))
    g_up = dot(mlp_in, grad_gu, ((0,), (0,)))

    def norm_back(v, inv, stretch, g_y):
        normed = v * inv
        g = g_y * (1.0 + stretch)
        g_v = (g - normed * jnp.mean(g * normed, axis=-1, keepdims=True)) * inv
        return g_v, jnp.sum(g_y, axis=0, keepdims=True), jnp.sum(g_y * normed, axis=0, keepdims=True)

    g_v, sums[3], sums[4] = norm_back(hidden_res, inv_two, stretch_two, grad_mlp_in)
    grad_hidden = cot_own + g_v
    sums[2] = live * jnp.sum(grad_hidden * branch, axis=0, keepdims=True)
    grad_branch = spread((gate_attn * grad_hidden).astype(low), "col", n_col)
    grad_mixed = dot(grad_branch, out_wide, ((1,), (1,))).astype(low)
    g_out = dot(mixed, grad_branch, ((0,), (0,)))
    g_out = g_out.reshape(my_heads, LANES, width)[:, :head_dim].reshape(my_heads * head_dim, width)
    gq, gk, gv, g_gain = attn_bwd(joined, q_aug, k_aug, v_aug, mixed, grad_mixed, cos_all, sin_a, sin_b, gain, head_dim)
    grad_joined = jnp.concatenate([gq, gk, gv], axis=1)
    grad_attn_in = gather_sum(dot(grad_joined, qkv_wide, ((1,), (1,))), "col", n_col)
    g_qkv = dot(attn_in, grad_joined, ((0,), (0,)))
    g_qkv = g_qkv.reshape(width, 3 * my_heads, LANES)[:, :, :head_dim].reshape(width, 3 * my_heads * head_dim)
    g_v, sums[0], sums[1] = norm_back(own_tok, inverse(own_tok), stretch_one, grad_attn_in)
    grad_tokens = from_image((grad_hidden + g_v).astype(low)).astype(wide)

    order = jnp.stack(
        [sum(jnp.where((me_col ^ d) == j, p, 0) for p, j in enumerate(order_col)) for d in range(n_col)]
        + [me_row ^ z for z in range(n_row)]
    ).astype(jnp.int32)

    def reduce_parts(partial):
        rows = partial.shape[0] // 2
        low_part = partial.astype(low)
        mine = lax.dynamic_slice_in_dim(low_part, me_img * rows, rows, axis=0)
        theirs = lax.dynamic_slice_in_dim(low_part, (1 - me_img) * rows, rows, axis=0)
        other = swap(theirs, "img", 2, 1)
        summed = (mine.astype(wide) + other.astype(wide)).astype(low)
        block = -(-rows // (8 * n_row)) * 8
        summed = jnp.pad(summed, ((0, block * n_row - rows), (0, 0))).reshape(n_row, block, -1)
        got = scatter_rows(summed, "row", n_row, me_row)
        shard = sum(g.astype(wide) for g in got).astype(low)
        around = jnp.concatenate([shard] + [swap(shard, "row", n_row, k) for k in range(1, n_row)], axis=0)
        return spread(around[None], "col", n_col), rows

    if n_img == 2:
        stack_down, rows_down = reduce_parts(g_down)
        stack_up, _ = reduce_parts(g_up)
        stack_out, rows_out = reduce_parts(g_out)
        stack_qkv, _ = reduce_parts(g_qkv)
        sum_down = assemble_rows(stack_down, order, rows_down)
        sum_up = assemble_columns(stack_up, order, 2 * halves)
        sum_out = assemble_rows(stack_out, order, rows_out)
        sum_qkv = assemble_columns(stack_qkv, order, 3 * halves)
    else:

        def reduce_columns(partial, parts):
            summed = lax.psum_scatter(
                lax.psum(partial.astype(low), "row"), "img", scatter_dimension=0, tiled=True
            )
            wholes = lax.all_gather(summed, "col", axis=0)
            rows = wholes.shape[1]
            wholes = wholes.reshape(n_col, rows, parts, -1)
            return jnp.transpose(wholes, (1, 2, 0, 3)).reshape(rows, -1).astype(wide)

        def reduce_rows(partial):
            wholes = lax.all_gather(lax.psum(partial.astype(low), "row"), "col", axis=0)
            columns = wholes.shape[2]
            wholes = jnp.transpose(wholes.reshape(n_col, halves, -1, columns), (1, 0, 2, 3)).reshape(-1, columns)
            return lax.psum_scatter(wholes, "img", scatter_dimension=0, tiled=True).astype(wide)

        sum_down, sum_up = reduce_rows(g_down), reduce_columns(g_up, 2 * halves)
        sum_out, sum_qkv = reduce_rows(g_out), reduce_columns(g_qkv, 3 * halves)

    grad_mod = total(jnp.concatenate(sums, axis=0), "col", n_col).astype(low)
    blocks = grad_mod.reshape(n_row, n_col, mod_span)
    mine = lax.dynamic_index_in_dim(blocks, me_col, 1, keepdims=False)
    share_rel = jnp.concatenate(scatter_rows(mine, "row", n_row, me_row), axis=0)
    share = jnp.concatenate(
        [lax.dynamic_index_in_dim(share_rel, me_row ^ b, 0, keepdims=True) for b in range(images)], axis=0
    )
    if n_img == 2:
        pairs_of = [(silu_cond, share), (swap(silu_cond, "img", 2, 1), swap(share, "img", 2, 1))]
    else:
        pairs_of = [
            (lax.all_gather(silu_cond, "img", axis=0, tiled=True), lax.all_gather(share, "img", axis=0, tiled=True))
        ]
    grad_ada = sum(dot(a, b, ((0,), (0,))) for a, b in pairs_of)
    back = dot(share, w_ada, ((1,), (1,)))
    flat = jnp.concatenate([back.reshape(-1), g_gain[:, :head_dim].reshape(-1)]).reshape(1, -1)
    flat = total(total(flat, "row", n_row), "col", n_col)[0]
    grad_silu = flat[: images * width].reshape(images, width)
    gains = flat[images * width :].reshape(2, head_dim)
    if n_img == 2:
        gains = gains + swap(gains, "img", 2, 1)
    else:
        gains = lax.psum(gains, "img")
    s = 1.0 / (1.0 + jnp.exp(-cond))
    grad_condition = grad_silu * (s * (1.0 + cond * (1.0 - s)))
    return output, grad_tokens, grad_condition, sum_qkv, sum_out, sum_up, sum_down, grad_ada, gains


def solution(mesh):
    sizes = tuple(mesh.shape[name] for name in ("img", "row", "col"))
    placed = (
        P("img", "row", "col", None),
        P("img", None),
        P("img"),
        P(None, "img", "row", "col"),
        P("img", None),
        P("img", None),
        P("img", None),
        P("img", None),
        P(None, ("row", "col")),
        P(),
        P("img", "row", "col", None),
    )
    return jax.shard_map(
        functools.partial(program, sizes),
        mesh=mesh,
        in_specs=placed,
        out_specs=(
            P("img", "row", "col", None),
            P("img", "row", "col", None),
            P("img", None),
            P("img", None),
            P("img", None),
            P("img", None),
            P("img", None),
            P(None, ("row", "col")),
            P(),
        ),
        check_vma=False,
    )
```

```python
import functools
import math

import jax
import jax.numpy as jnp
from jax import lax
from jax.experimental import pallas as pl
from jax.experimental.pallas import tpu as pltpu
from jax.sharding import PartitionSpec as P

LANES = 128
epsilon = 1e-06
low, wide = jnp.bfloat16, jnp.float32


def bits_of(size):
    return [1 << b for b in reversed(range(size.bit_length() - 1))]


def block_order(size):
    order = [0]
    for bit in bits_of(size):
        order = order + [o ^ bit for o in order]
    return order


def swap(value, axis, size, bit):
    return lax.ppermute(value, axis, [(a, a ^ bit) for a in range(size)])


def after(value, *earlier):
    return lax.optimization_barrier((value,) + earlier)[0]


def cat(*parts):
    return jnp.concatenate(parts, axis=0)


def dot(a, b):
    return jnp.dot(a, b, preferred_element_type=wide)


def dot_t(a, b):
    return lax.dot_general(a, b, (((1,), (1,)), ((), ())), preferred_element_type=wide)


def whole(shape):
    return pl.BlockSpec(shape, lambda *_: (0,) * len(shape))


def shape_of(shape, dtype):
    return jax.ShapeDtypeStruct(shape, dtype)


def kernel(body, name, scalars, args, grid, in_specs, out_specs, out_shape, scratch=(), megabytes=32):
    none = scalars is None
    return pl.pallas_call(
        functools.partial(body, None) if none else body,
        grid_spec=pltpu.PrefetchScalarGridSpec(
            num_scalar_prefetch=0 if none else 1, grid=grid, in_specs=in_specs, out_specs=out_specs, scratch_shapes=scratch
        ),
        out_shape=out_shape,
        compiler_params=pltpu.CompilerParams(vmem_limit_bytes=megabytes * 1024 * 1024),
        cost_estimate=pl.CostEstimate(flops=1, bytes_accessed=1, transcendentals=0),
        name=name,
    )(*([] if none else [scalars]), *args)


def pick(step, refs):
    value = refs[0][...]
    for n in range(1, len(refs)):
        value = jnp.where(step == n, refs[n][...], value)
    return value


def cut_qkv_kernel(parts, count, at, w_ref, o_ref):
    piece = o_ref.shape[1] // parts
    for c in range(count):

        @pl.when(at[0] == c)
        def _():
            for p in range(parts):
                start = (p * count + c) * piece
                o_ref[:, p * piece : (p + 1) * piece] = w_ref[:, start : start + piece]


def cut_qkv(w, at, parts, count):
    rows, width = w.shape
    step = 144
    return kernel(
        functools.partial(cut_qkv_kernel, parts, count),
        "cut_qkv",
        at,
        [w],
        (rows // step,),
        [pl.BlockSpec((step, width), lambda s, o=None: (s, 0))],
        pl.BlockSpec((step, width // count), lambda s, o=None: (s, 0)),
        shape_of((rows, width // count), w.dtype),
    )


def copy_kernel(at, *refs):
    n = len(refs) // 2
    for a, b in zip(refs[:n], refs[n:]):
        b[...] = a[...]


def cut_rest(w_up, w_out, w_down, at, parts, count):
    rows, width = w_up.shape
    piece = width // (parts * count)
    shapes = [(w.shape[0] // count, w.shape[1]) for w in (w_out, w_down)]
    return kernel(
        copy_kernel,
        "cut_rest",
        at,
        [w_up, w_out, w_down],
        (parts,),
        [pl.BlockSpec((rows, piece), lambda p, o=None: (0, p * count + o[0]))]
        + [pl.BlockSpec(s, lambda p, o=None: (o[0], 0)) for s in shapes],
        [pl.BlockSpec((rows, piece), lambda p, o=None: (0, p))] + [whole(s) for s in shapes],
        [shape_of((rows, piece * parts), w_up.dtype)] + [shape_of(s, w_up.dtype) for s in shapes],
    )


def widen_kernel(head_dim, heads, at, mine_ref, other_ref, o_ref):
    src = jnp.where(at[0] == pl.program_id(0), mine_ref[...], other_ref[...])
    none = jnp.zeros((src.shape[0], LANES - head_dim), src.dtype)
    for t in range(3):
        for n in range(heads):
            start, end = (t * heads + n) * head_dim, (n * 3 + t) * LANES
            o_ref[:, end : end + LANES] = jnp.concatenate([src[:, start : start + head_dim], none], axis=1)


def widen(mine, other, at, head_dim):
    rows, width = mine.shape
    out = width // head_dim * LANES
    return kernel(
        functools.partial(widen_kernel, head_dim, width // (3 * head_dim)),
        "widen",
        at,
        [mine, other],
        (2,),
        [whole((rows, width))] * 2,
        pl.BlockSpec((rows, out), lambda h, o=None: (h, 0)),
        shape_of((2 * rows, out), mine.dtype),
    )


def widen_rows_kernel(head_dim, at, mine_ref, other_ref, o_ref):
    src = jnp.where(at[0] == pl.program_id(0), mine_ref[...], other_ref[...]).astype(wide)
    none = jnp.zeros((LANES - head_dim, src.shape[1]), wide)
    for n in range(src.shape[0] // head_dim):
        part = jnp.concatenate([src[n * head_dim : (n + 1) * head_dim], none], axis=0)
        o_ref[n * LANES : (n + 1) * LANES] = part.astype(low)


def widen_rows(mine, other, at, head_dim):
    rows, width = mine.shape
    out = rows // head_dim * LANES
    return kernel(
        functools.partial(widen_rows_kernel, head_dim),
        "widen_rows",
        at,
        [mine, other],
        (2,),
        [whole((rows, width))] * 2,
        pl.BlockSpec((out, width), lambda h, o=None: (h, 0)),
        shape_of((2 * out, width), mine.dtype),
    )


def join_kernel(at, a_ref, b_ref, c_ref, d_ref, x_ref, y_ref):
    mine = at[0] == pl.program_id(0)
    x_ref[...] = jnp.where(mine, a_ref[...], b_ref[...])
    y_ref[...] = jnp.where(mine, c_ref[...], d_ref[...])


def join(mine_up, other_up, mine_down, other_down, at):
    specs = [whole(a.shape) for a in (mine_up, other_up, mine_down, other_down)]
    return kernel(
        join_kernel,
        "join",
        at,
        [mine_up, other_up, mine_down, other_down],
        (2,),
        specs,
        [pl.BlockSpec(a.shape, lambda h, o=None: (h, 0)) for a in (mine_up, mine_down)],
        [shape_of((2 * a.shape[0], a.shape[1]), low) for a in (mine_up, mine_down)],
    )


def tables_kernel(n_row, tile, tile_cols, head_dim, at, cos_ref, a_ref, b_ref):
    shape = cos_ref.shape
    pairs = head_dim // 4
    pos = lax.broadcasted_iota(jnp.int32, shape, 0)
    lane = lax.broadcasted_iota(jnp.int32, shape, 1)
    block = pos // tile
    row_block, col_block = block % n_row, block // n_row
    row_at = jnp.zeros(shape, jnp.int32)
    for k in range(n_row):
        row_at = jnp.where(row_block == k, at[2 + k], row_at)
    col_at = jnp.zeros(shape, jnp.int32)
    for j in range(shape[0] // (tile * n_row)):
        col_at = jnp.where(col_block == j, at[2 + n_row + j], col_at)
    inside = pos % tile
    row = (row_at * (tile // tile_cols) + inside // tile_cols) * at[0]
    col = (col_at * tile_cols + inside % tile_cols) * at[1]
    half = 2 * pairs
    within = jnp.where(lane < half, lane, lane - half)
    first = within < pairs
    step = jnp.where(first, within, within - pairs).astype(wide)
    frequency = jnp.exp(step * (-math.log(10000.0) / pairs))
    angle = jnp.where(lane < half, row, col).astype(wide) * frequency
    live = lane < head_dim
    cos, sin = jnp.cos(angle), jnp.sin(angle)
    cos_ref[...] = jnp.where(live, cos, 0.0)
    a_ref[...] = jnp.where(live & first, -sin, 0.0)
    b_ref[...] = jnp.where(live & jnp.logical_not(first), sin, 0.0)


def tables(at, n_row, n_col, tile, tile_cols, head_dim):
    shape = (n_row * n_col * tile, LANES)
    return kernel(
        functools.partial(tables_kernel, n_row, tile, tile_cols, head_dim),
        "tables",
        at,
        [],
        (1,),
        [],
        [whole(shape)] * 3,
        [shape_of(shape, wide)] * 3,
    )


def place_modulation_kernel(at, *refs):
    o_ref = refs[-1]
    rows = refs[0].shape[0]
    for j, ref in enumerate(refs[:-1]):
        for k in range(rows):
            o_ref[pl.ds(at[j * rows + k], 1), :] = ref[k : k + 1, :]


def place_modulation(parts, at):
    rows, width = parts[0].shape
    shape = (rows * len(parts), width)
    return kernel(
        place_modulation_kernel,
        "place_modulation",
        at,
        parts,
        (1,),
        [whole(p.shape) for p in parts],
        whole(shape),
        shape_of(shape, wide),
    )


def inverse(v):
    return lax.rsqrt(jnp.mean(v * v, axis=-1, keepdims=True) + epsilon)


def norm_back(v, inv, stretch, g_y):
    normed = v * inv
    g = g_y * (1.0 + stretch)
    g_v = (g - normed * jnp.mean(g * normed, axis=-1, keepdims=True)) * inv
    return g_v, jnp.sum(g_y, axis=0, keepdims=True), jnp.sum(g_y * normed, axis=0, keepdims=True)


def put_rows(ref, **rows):
    ref[...] = jnp.zeros_like(ref)
    for name, row in rows.items():
        n = int(name[1:])
        ref[n : n + 1, :] = row


def turn(x, cos, sin_a, sin_b, shift):
    return x * cos + pltpu.roll(x, LANES - shift, 1) * sin_a + pltpu.roll(x, shift, 1) * sin_b


def project_qkv_kernel(at, *refs):
    toks, (mod_ref, w_ref, in_ref, joined_ref) = refs[:-4], refs[-4:]
    x = pick(pl.program_id(0), toks).astype(wide)
    attn_in = (x * inverse(x) * (1.0 + mod_ref[1:2, :]) + mod_ref[0:1, :]).astype(low)
    in_ref[...] = attn_in
    joined_ref[...] = dot(attn_in, w_ref[...])


def project_qkv(toks, modulation, w):
    rows, width = toks[0].shape
    n, columns = len(toks), w.shape[1]
    return kernel(
        project_qkv_kernel,
        "project_qkv",
        None,
        [*toks, modulation, w],
        (n,),
        [whole(t.shape) for t in toks] + [whole(modulation.shape), whole(w.shape)],
        [pl.BlockSpec((rows, width), lambda s, o=None: (s, 0)), pl.BlockSpec((rows, columns), lambda s, o=None: (s, 0))],
        [shape_of((n * rows, width), low), shape_of((n * rows, columns), wide)],
    )


def attn_fwd_kernel(head_dim, at, x_ref, cos_ref, a_ref, b_ref, gain_ref, o_ref, aug_ref):
    tokens = x_ref.shape[0]
    pairs, scale = head_dim // 4, head_dim**-0.5 * math.log2(math.e)
    cos, sa, sb = cos_ref[...], a_ref[...], b_ref[...]

    def normed(x):
        return x * lax.rsqrt(jnp.sum(x * x, axis=-1, keepdims=True) * (1.0 / head_dim) + epsilon)

    q = turn(normed(x_ref[:, :LANES]) * gain_ref[0:1, :], cos, sa, sb, pairs) * scale
    k = turn(normed(x_ref[:, LANES : 2 * LANES]) * gain_ref[1:2, :], cos, sa, sb, pairs)
    lane = lax.broadcasted_iota(jnp.int32, (tokens, LANES), 1)
    extra = (lane == head_dim) | (lane == head_dim + 1)
    kk = jnp.where(extra, 1.0, k).astype(low)
    vv = jnp.where(extra, -1.0, x_ref[:, 2 * LANES :]).astype(low)
    aug_ref[:, LANES : 2 * LANES] = kk
    aug_ref[:, 2 * LANES :] = vv
    q_low = q.astype(low)
    rows = 256
    for s in range(tokens // rows):
        span = slice(s * rows, (s + 1) * rows)
        out = dot(jnp.exp2(dot_t(q_low[span], kk)).astype(low), vv)
        total = -out[:, head_dim : head_dim + 1]
        lane_s = lane[span]
        o_ref[span, :] = jnp.where(lane_s < head_dim, out * (1.0 / total), 0.0).astype(low)
        lse = -jnp.log2(total)
        high = lse.astype(low).astype(wide)
        aug = jnp.where(lane_s == head_dim, high, jnp.where(lane_s == head_dim + 1, lse - high, q[span]))
        aug_ref[span, :LANES] = aug.astype(low)


def attn_fwd(joined, cos, sa, sb, gain, head_dim):
    tokens, columns = joined.shape
    heads = columns // (3 * LANES)
    block = pl.BlockSpec((tokens, 3 * LANES), lambda h, o=None: (0, h))
    return kernel(
        functools.partial(attn_fwd_kernel, head_dim),
        "attn_fwd",
        None,
        [joined, cos, sa, sb, gain],
        (heads,),
        [block, whole(cos.shape), whole(cos.shape), whole(cos.shape), whole(gain.shape)],
        [pl.BlockSpec((tokens, LANES), lambda h, o=None: (0, h)), block],
        [shape_of((tokens, heads * LANES), low), shape_of((tokens, columns), low)],
        megabytes=60,
    )


def attn_bwd_kernel(head_dim, at, *refs):
    n = len(refs) - 14
    gbs = refs[:n]
    x_ref, aug_ref, o_ref, w_ref, cos_ref, a_ref, b_ref, gain_ref, g_ref, gg_ref = refs[n : n + 10]
    dk_acc, dv_acc, dq_acc, do_acc = refs[n + 10 :]
    tokens = x_ref.shape[0]
    pairs = head_dim // 4
    h = pl.program_id(0)
    rows = tokens // n
    for j in range(n):
        do_acc[j * rows : (j + 1) * rows, :] = dot_t(gbs[j][...], w_ref[...]).astype(low)
    lane = lax.broadcasted_iota(jnp.int32, (tokens, LANES), 1)
    do_f = do_acc[...].astype(wide)
    delta = jnp.sum(do_f * o_ref[...].astype(wide), axis=-1, keepdims=True)
    high = delta.astype(low).astype(wide)
    do_a = jnp.where(lane == head_dim, high, jnp.where(lane == head_dim + 1, delta - high, do_f)).astype(low)
    qa, ka, va = aug_ref[:, :LANES], aug_ref[:, LANES : 2 * LANES], aug_ref[:, 2 * LANES :]
    ka_t = ka.T
    cols = 256
    for s in range(tokens // cols):
        qs = qa[s * cols : (s + 1) * cols]
        ds = do_a[s * cols : (s + 1) * cols]
        p = jnp.exp2(dot_t(ka, qs))
        grad_s = (p * dot_t(va, ds)).astype(low)
        dv, dk = dot(p.astype(low), ds), dot(grad_s, qs)
        if s == 0:
            dv_acc[...] = dv
            dk_acc[...] = dk
        else:
            dv_acc[...] += dv
            dk_acc[...] += dk
        dq_acc[:, s * cols : (s + 1) * cols] = dot(ka_t, grad_s)
    inside = lane < head_dim
    cos, sa, sb = cos_ref[...], a_ref[...], b_ref[...]

    def back(g, x, gain):
        g = jnp.where(inside, g, 0.0)
        g = g * cos - pltpu.roll(g, LANES - pairs, 1) * sa - pltpu.roll(g, pairs, 1) * sb
        inv = lax.rsqrt(jnp.sum(x * x, axis=-1, keepdims=True) * (1.0 / head_dim) + epsilon)
        normed = x * inv
        gain_part = jnp.sum(g * normed, axis=0, keepdims=True)
        g = g * gain
        return (g - normed * (jnp.sum(g * normed, axis=-1, keepdims=True) * (1.0 / head_dim))) * inv, gain_part

    gq, ggq = back(dq_acc[...].T * (head_dim**-0.5), x_ref[:, :LANES], gain_ref[0:1, :])
    gk, ggk = back(dk_acc[...] * math.log(2.0), x_ref[:, LANES : 2 * LANES], gain_ref[1:2, :])
    g_ref[:, :LANES] = gq.astype(low)
    g_ref[:, LANES : 2 * LANES] = gk.astype(low)
    g_ref[:, 2 * LANES :] = jnp.where(inside, dv_acc[...], 0.0).astype(low)
    gg = jnp.concatenate([ggq, ggk], axis=0)

    @pl.when(h == 0)
    def _():
        gg_ref[...] = gg

    @pl.when(h > 0)
    def _():
        gg_ref[...] += gg


def attn_bwd(grads, joined, aug, mixed, w_out, cos, sa, sb, gain, head_dim, first, heads):
    tokens = joined.shape[0]
    block = pl.BlockSpec((tokens, 3 * LANES), lambda h, o=None: (0, first + h))
    return kernel(
        functools.partial(attn_bwd_kernel, head_dim),
        "attn_bwd",
        None,
        [*grads, joined, aug, mixed, w_out, cos, sa, sb, gain],
        (heads,),
        [whole(g.shape) for g in grads]
        + [block, block, pl.BlockSpec((tokens, LANES), lambda h, o=None: (0, first + h))]
        + [pl.BlockSpec((LANES, w_out.shape[1]), lambda h, o=None: (first + h, 0))]
        + [whole(cos.shape), whole(cos.shape), whole(cos.shape), whole(gain.shape)],
        [pl.BlockSpec((tokens, 3 * LANES), lambda h, o=None: (0, h)), whole(gain.shape)],
        [shape_of((tokens, heads * 3 * LANES), low), shape_of(gain.shape, wide)],
        scratch=[
            pltpu.VMEM((tokens, LANES), wide),
            pltpu.VMEM((tokens, LANES), wide),
            pltpu.VMEM((LANES, tokens), wide),
            pltpu.VMEM((tokens, LANES), low),
        ],
        megabytes=60,
    )


def project_kernel(at, x_ref, w_ref, o_ref):
    o_ref[...] = dot(x_ref[...], w_ref[...]).astype(o_ref.dtype)


def project_back_kernel(at, *refs):
    xs, (w_ref, o_ref) = refs[:-2], refs[-2:]
    width = xs[0].shape[1]
    value = sum(dot_t(x[...], w_ref[:, n * width : (n + 1) * width]) for n, x in enumerate(xs))
    o_ref[...] = value.astype(o_ref.dtype)


def project(xs, w, first, count, rows, dtype):
    columns = w.shape[1] if len(xs) == 1 else w.shape[0]
    return kernel(
        project_kernel if len(xs) == 1 else project_back_kernel,
        "project",
        None,
        [*xs, w],
        (count,),
        [pl.BlockSpec((rows, x.shape[1]), lambda s, o=None: (first + s, 0)) for x in xs] + [whole(w.shape)],
        pl.BlockSpec((rows, columns), lambda s, o=None: (s, 0)),
        shape_of((count * rows, columns), dtype),
    )


def add_kernel(at, a_ref, b_ref, o_ref):
    o_ref[...] = (a_ref[...].astype(wide) + b_ref[...].astype(wide)).astype(low)


def add_second(a, b):
    rows, columns = a.shape[0] // 2, a.shape[1]
    return kernel(
        add_kernel,
        "add_second",
        None,
        [a, b],
        (1,),
        [pl.BlockSpec((rows, columns), lambda s, o=None: (1, 0))] * 2,
        whole((rows, columns)),
        shape_of((rows, columns), low),
    )


def middle_kernel(live, keep_ref, core_ref, y_ref, tok_ref, mod_ref, hidden_ref, branch_ref, mlp_ref):
    branch = keep_ref[...] + core_ref[...].astype(wide) + y_ref[...].astype(wide)
    gate = mod_ref[2:3, :] * live[0].astype(wide)
    hidden = tok_ref[...].astype(wide) + gate * branch
    hidden_ref[...] = hidden
    branch_ref[...] = branch
    mlp_ref[...] = (hidden * inverse(hidden) * (1.0 + mod_ref[4:5, :]) + mod_ref[3:4, :]).astype(low)


def middle(keep, core, y, tok, modulation, live):
    shape = y.shape
    first = pl.BlockSpec(shape, lambda s, o=None: (0, 0))
    return kernel(
        middle_kernel,
        "middle",
        live,
        [keep, core, y, tok, modulation],
        (1,),
        [first, first, first, first, whole(modulation.shape)],
        [first] * 3,
        [shape_of(shape, wide), shape_of(shape, wide), shape_of(shape, low)],
    )


def middle_back_kernel(live, keep_ref, core_ref, y_ref, hidden_ref, branch_ref, cot_ref, mod_ref, grad_ref, gb_ref, s_ref):
    g_y = keep_ref[...] + core_ref[...].astype(wide) + y_ref[...].astype(wide)
    hidden = hidden_ref[...]
    on = live[0].astype(wide)
    g_v, g_o, g_a = norm_back(hidden, inverse(hidden), mod_ref[4:5, :], g_y)
    grad = cot_ref[...].astype(wide) + g_v
    grad_ref[...] = grad
    gb_ref[...] = (mod_ref[2:3, :] * on * grad).astype(low)
    put_rows(s_ref, r2=on * jnp.sum(grad * branch_ref[...], axis=0, keepdims=True), r3=g_o, r4=g_a)


def middle_back(keep, core, y, hidden, branch, cot, modulation, live):
    shape = y.shape
    first = pl.BlockSpec(shape, lambda s, o=None: (0, 0))
    sums = (8, shape[1])
    return kernel(
        middle_back_kernel,
        "middle_back",
        live,
        [keep, core, y, hidden, branch, cot, modulation],
        (1,),
        [first] * 6 + [whole(modulation.shape)],
        [first, first, whole(sums)],
        [shape_of(shape, wide), shape_of(shape, low), shape_of(sums, wide)],
    )


def result_kernel(live, keep_ref, core_ref, y_ref, hidden_ref, cot_ref, mod_ref, *outs):
    mlp_out = keep_ref[...] + core_ref[...].astype(wide) + y_ref[...].astype(wide)
    on = live[0].astype(wide)
    result = (hidden_ref[...] + mod_ref[5:6, :] * on * mlp_out).astype(low)
    put_rows(outs[-1], r5=on * jnp.sum(cot_ref[...].astype(wide) * mlp_out, axis=0, keepdims=True))
    outs[0][...] = result


def result(keep, core, y, hidden, cot, modulation, live):
    shape = y.shape
    first = pl.BlockSpec(shape, lambda s, o=None: (0, 0))
    sums = (8, shape[1])
    return kernel(
        result_kernel,
        "result",
        live,
        [keep, core, y, hidden, cot, modulation],
        (1,),
        [first] * 5 + [whole(modulation.shape)],
        [first, whole(sums)],
        [shape_of(shape, low), shape_of(sums, wide)],
    )


def last_back_kernel(live, keep_ref, core_ref, y_ref, tok_ref, grad_ref, mod_ref, *outs):
    g_y = keep_ref[...] + core_ref[...].astype(wide) + y_ref[...].astype(wide)
    tok = tok_ref[...].astype(wide)
    g_v, g_o, g_a = norm_back(tok, inverse(tok), mod_ref[1:2, :], g_y)
    grad = (grad_ref[...] + g_v).astype(low)
    put_rows(outs[-1], r0=g_o, r1=g_a)
    outs[0][...] = grad


def last_back(keep, core, y, tok, grad, modulation, live):
    shape = y.shape
    first = pl.BlockSpec(shape, lambda s, o=None: (0, 0))
    sums = (8, shape[1])
    return kernel(
        last_back_kernel,
        "last_back",
        live,
        [keep, core, y, tok, grad, modulation],
        (1,),
        [first] * 5 + [whole(modulation.shape)],
        [first, whole(sums)],
        [shape_of(shape, low), shape_of(sums, wide)],
    )


def feed_forward_kernel(n, live, *refs):
    xs, cots = refs[:n], refs[n : 2 * n]
    mod_ref, up_ref, down_ref, act_ref, gu_ref, gm_ref, send_ref, keep_ref = refs[2 * n :]
    s = pl.program_id(0)
    block = (s + n // 2) % n
    x, cot = pick(block, xs), pick(block, cots)
    w_up = up_ref[...]
    gate_up = dot(x, w_up)
    half = gate_up.shape[1] // 2
    gate, up = gate_up[:, :half], gate_up[:, half:]
    sig = 1.0 / (1.0 + jnp.exp(-gate))
    silu = gate * sig
    act_ref[...] = (silu * up).astype(low)
    grad = (mod_ref[5:6, :] * live[0].astype(wide) * cot.astype(wide)).astype(low)
    gm_ref[...] = grad
    grad_act = dot_t(grad, down_ref[...])
    gu_ref[:, :half] = (grad_act * up * sig * (1.0 + gate * (1.0 - sig))).astype(low)
    gu_ref[:, half:] = (grad_act * silu).astype(low)
    grad_in = dot_t(gu_ref[...], w_up)

    @pl.when(s < n // 2)
    def _():
        send_ref[...] = grad_in.astype(low)

    @pl.when(s >= n // 2)
    def _():
        keep_ref[...] = grad_in


def feed_forward(xs, cots, modulation, w_up, w_down, live):
    n = len(xs)
    rows, width = xs[0].shape
    hidden = w_down.shape[0]
    half = n // 2

    def by_block(columns):
        return pl.BlockSpec((rows, columns), lambda s, o=None: ((s + half) % n, 0))

    return kernel(
        functools.partial(feed_forward_kernel, n),
        "feed_forward",
        live,
        [*xs, *cots, modulation, w_up, w_down],
        (n,),
        [whole(x.shape) for x in (*xs, *cots, modulation, w_up, w_down)],
        [
            by_block(hidden),
            by_block(2 * hidden),
            by_block(width),
            pl.BlockSpec((rows, width), lambda s, o=None: (jnp.minimum(s, half - 1), 0)),
            pl.BlockSpec((rows, width), lambda s, o=None: (jnp.maximum(s - half, 0), 0)),
        ],
        [
            shape_of((n * rows, hidden), low),
            shape_of((n * rows, 2 * hidden), low),
            shape_of((n * rows, width), low),
            shape_of((half * rows, width), low),
            shape_of((half * rows, width), wide),
        ],
        megabytes=48,
    )


def halves_of(acc_ref, at):
    rows = acc_ref.shape[0] // 2
    return [acc_ref[pl.ds(pl.multiple_of(i * rows, 8), rows), :] for i in (1 - at[0], at[0])]


def turned(xs, xt_ref):
    @pl.when(pl.program_id(0) == 0)
    def _():
        rows = xs[0].shape[0]
        for j, x in enumerate(xs):
            xt_ref[:, j * rows : (j + 1) * rows] = x[...].T


def turn_kernel(at, *refs):
    n = len(refs) // 2
    for a, b in zip(refs[:n], refs[n:]):
        b[...] = a[...].T


def turn_blocks(arrays, rows):
    tokens = arrays[0].shape[0]
    return kernel(
        turn_kernel,
        "turn_blocks",
        None,
        arrays,
        (tokens // rows,),
        [pl.BlockSpec((rows, a.shape[1]), lambda s, o=None: (s, 0)) for a in arrays],
        [pl.BlockSpec((a.shape[1], rows), lambda s, o=None: (0, s)) for a in arrays],
        [shape_of((a.shape[1], tokens), a.dtype) for a in arrays],
    )


def grad_part_kernel(n, at, *refs):
    xs, (b_ref, theirs, mine, xt_ref, acc_ref) = refs[:n], refs[n:]
    turned(xs, xt_ref)
    acc_ref[...] = dot(xt_ref[...], b_ref[...])
    for ref, value in zip((theirs, mine), halves_of(acc_ref, at)):
        ref[...] = value.astype(low)


def grad_part(xs, b, at, first, columns, chunk):
    tokens, width = len(xs) * xs[0].shape[0], xs[0].shape[1]
    out = pl.BlockSpec((width // 2, chunk), lambda s, o=None: (0, s))
    return kernel(
        functools.partial(grad_part_kernel, len(xs)),
        "grad_part",
        at,
        [*xs, b],
        (columns // chunk,),
        [whole(x.shape) for x in xs] + [pl.BlockSpec((tokens, chunk), lambda s, o=None: (0, first // chunk + s))],
        [out, out],
        [shape_of((width // 2, columns), low)] * 2,
        scratch=[pltpu.VMEM((width, tokens), low), pltpu.VMEM((width, chunk), wide)],
        megabytes=36,
    )


def grad_last_kernel(n, head_dim, cut, columns, at, *refs):
    xt_ref, mt_ref = refs[:2]
    parts, gbs = refs[2 : 2 + n], refs[2 + n : 2 + 2 * n]
    outs = refs[2 + 2 * n : 6 + 2 * n]
    acc_ref, out_ref = refs[6 + 2 * n :]
    s = pl.program_id(0)

    @pl.when(s == 0)
    def _():
        for ref in outs:
            ref[:, columns:] = jnp.zeros((ref.shape[0], ref.shape[1] - columns), low)

    acc_ref[...] = dot(xt_ref[...], pick(s, parts))
    for half, value in enumerate(halves_of(acc_ref, at)):
        joined = [value[:, h * LANES : h * LANES + head_dim] for h in range(value.shape[1] // LANES)]
        value = jnp.concatenate(joined, axis=1).astype(low)
        width, rows = value.shape[1], value.shape[0] - cut
        for c in range(n):

            @pl.when(s == c)
            def _():
                outs[half][:, c * width : (c + 1) * width] = value[:cut]
                outs[2 + half][:rows, c * width : (c + 1) * width] = value[cut:]

    @pl.when(s == n - 1)
    def _():
        rows = gbs[0].shape[0]
        out_ref[...] = sum(dot(mt_ref[:, j * rows : (j + 1) * rows], gbs[j][...]) for j in range(n))
        for half, value in enumerate(halves_of(out_ref, at)):
            ref = outs[2 + half]
            heads = [value[h * LANES : h * LANES + head_dim] for h in range(value.shape[0] // LANES)]
            value = jnp.concatenate(heads, axis=0)
            length, width = value.shape[0], columns
            start = xt_ref.shape[0] // 2 - cut
            side, third = value.shape[1] - width, length // 3
            ref[start : start + length, :width] = value[:, :width].astype(low)
            rest = [value[k * third : (k + 1) * third, width:] for k in range(3)]
            ref[start + length :, :width] = jnp.concatenate(rest, axis=1).astype(low)


def grad_last(xt, parts, mixed_t, gbs, at, head_dim, cut):
    n = len(parts)
    width = xt.shape[0]
    columns = n * parts[0].shape[1] // LANES * head_dim
    length = mixed_t.shape[0] // LANES * head_dim // 2
    assert gbs[0].shape[1] - columns == columns // 3 and length % 3 == 0
    padded = -(-columns // LANES) * LANES
    shapes = [(cut, padded), (width // 2 - cut + length + length // 3, padded)]
    return kernel(
        functools.partial(grad_last_kernel, n, head_dim, cut, columns),
        "grad_last",
        at,
        [xt, mixed_t, *parts, *gbs],
        (n,),
        [whole(a.shape) for a in (xt, mixed_t, *parts, *gbs)],
        [whole(a) for a in shapes for _ in range(2)],
        [shape_of(a, low) for a in shapes for _ in range(2)],
        scratch=[
            pltpu.VMEM((width, parts[0].shape[1]), wide),
            pltpu.VMEM((mixed_t.shape[0], gbs[0].shape[1]), wide),
        ],
        megabytes=52,
    )


def add_halves_kernel(at, a_ref, b_ref, send_ref, keep_ref):
    value = a_ref[...].astype(wide) + b_ref[...].astype(wide)

    @pl.when(pl.program_id(0) == 0)
    def _():
        send_ref[...] = value.astype(low)

    @pl.when(pl.program_id(0) == 1)
    def _():
        keep_ref[...] = value


def add_halves(a, b, at):
    rows, columns = a.shape[0] // 2, a.shape[1]
    block = pl.BlockSpec((rows, columns), lambda s, o=None: (o[s], 0))
    return kernel(
        add_halves_kernel,
        "add_halves",
        at,
        [a, b],
        (2,),
        [block, block],
        [whole((rows, columns))] * 2,
        [shape_of((rows, columns), low), shape_of((rows, columns), wide)],
    )


def join_halves_kernel(at, a_ref, b_ref, o_ref):
    o_ref[...] = jnp.where(pl.program_id(0) == at[1], a_ref[...], b_ref[...])


def join_halves(mine, other, at):
    rows, columns = mine.shape
    return kernel(
        join_halves_kernel,
        "join_halves",
        at,
        [mine, other],
        (2,),
        [whole(mine.shape)] * 2,
        pl.BlockSpec((rows, columns), lambda s, o=None: (s, 0)),
        shape_of((2 * rows, columns), low),
    )


def place_columns(srcs, at, start, step, parts, up_ref):
    width = srcs[0].shape[1]
    piece, count = width // parts, len(srcs)

    def put(d, block):
        for p in range(parts):
            end = (p * count + d) * piece
            up_ref[:, end : end + piece] = block[:, p * piece : (p + 1) * piece]

    for j in range(count):
        block = srcs[j][pl.ds(start, step), :].astype(wide)
        for d in range(count):
            pl.when(at[j] == d)(functools.partial(put, d, block))


def place_first_kernel(parts, at, *refs):
    srcs, up_ref = refs[:-1], refs[-1]
    step = up_ref.shape[0]
    place_columns(srcs, at, pl.multiple_of(pl.program_id(0) * step, 16), step, parts, up_ref)


def place_first(blocks, at, parts):
    count = len(blocks)
    rows, width = blocks[0].shape
    step = 144
    return kernel(
        functools.partial(place_first_kernel, parts),
        "place_first",
        at,
        blocks,
        (rows // step,),
        [whole(b.shape) for b in blocks],
        pl.BlockSpec((step, width * count), lambda s, o=None: (s, 0)),
        shape_of((rows, 2 * width * count), wide),
    )


def place_second_kernel(count, parts, at, *refs):
    srcs, up_ref = refs[:count], refs[-1]
    step = up_ref.shape[0]
    place_columns(srcs, at, pl.multiple_of(pl.program_id(0) * step, 16), step, parts, up_ref)


def place_second(blocks, first, at, parts):
    count = len(blocks)
    width = blocks[0].shape[1]
    rows = first.shape[0]
    step = 144
    return pl.pallas_call(
        functools.partial(place_second_kernel, count, parts),
        grid_spec=pltpu.PrefetchScalarGridSpec(
            num_scalar_prefetch=1,
            grid=(rows // step,),
            in_specs=[whole(b.shape) for b in blocks] + [pl.BlockSpec(memory_space=pl.ANY)],
            out_specs=pl.BlockSpec((step, width * count), lambda s, o: (s, 1)),
        ),
        out_shape=shape_of(first.shape, wide),
        input_output_aliases={count + 1: 0},
        compiler_params=pltpu.CompilerParams(vmem_limit_bytes=32 * 1024 * 1024),
        cost_estimate=pl.CostEstimate(flops=1, bytes_accessed=1, transcendentals=0),
        name="place_second",
    )(at, *blocks, first)


def place_rows_kernel(at, *refs):
    srcs, o_ref = refs[:-1], refs[-1]
    rows = srcs[0].shape[0]
    for j, ref in enumerate(srcs):
        o_ref[pl.ds(pl.multiple_of(at[j] * rows, 8), rows), :] = ref[...].astype(wide)


def place_rows(blocks, at, chunk):
    rows, width = blocks[0].shape
    n = len(blocks)
    return kernel(
        place_rows_kernel,
        "place_rows",
        at,
        blocks,
        (width // chunk,),
        [pl.BlockSpec((rows, chunk), lambda s, o=None: (0, s))] * n,
        pl.BlockSpec((n * rows, chunk), lambda s, o=None: (0, s)),
        shape_of((n * rows, width), wide),
    )


def place_last_kernel(count, halves, head_dim, steps, columns, at, *refs):
    firsts, seconds, lasts = refs[:count], refs[count : 2 * count], refs[2 * count : 3 * count]
    o_ref, out_ref = refs[3 * count :]
    heads = columns // (3 * head_dim) // halves
    s = pl.program_id(0)

    def put(d, block):
        for t in range(3):
            for h in range(halves):
                for u in range(heads):
                    end = ((t * halves + h) * count + d) * heads + u
                    start = (h * heads + u) * 3 + t
                    o_ref[:, end * head_dim : (end + 1) * head_dim] = block[
                        :, start * head_dim : (start + 1) * head_dim
                    ]

    for j in range(count):
        block = jnp.where(s < steps, firsts[j][...], seconds[j][...]).astype(wide)
        for d in range(count):
            pl.when(at[j] == d)(functools.partial(put, d, block))

    @pl.when(s == 0)
    def _():
        length = out_ref.shape[0] // count
        for j in range(count):
            value = lasts[j][...].astype(wide)
            width, side = columns, columns // 3
            at_row = pl.multiple_of(at[j] * length, 8)
            out_ref[pl.ds(at_row, length), :width] = value[:length, :width]
            rest = [value[length:, k * side : (k + 1) * side] for k in range(3)]
            out_ref[pl.ds(at_row, length), width:] = jnp.concatenate(rest, axis=0)


def place_last(firsts, seconds, at, halves, head_dim, rows, length, columns):
    count = len(firsts)
    cut, width = firsts[0].shape
    step = 96
    steps, total = cut // step, rows // step
    last = seconds[0].shape[0] - (rows - cut)
    assert last == rows - cut
    outs = [(rows, columns * count), (count * length, columns // 3 * 4)]
    return kernel(
        functools.partial(place_last_kernel, count, halves, head_dim, steps, columns),
        "place_last",
        at,
        [*firsts, *seconds, *seconds],
        (total,),
        [pl.BlockSpec((step, width), lambda s, o: (jnp.minimum(s, steps - 1), 0))] * count
        + [pl.BlockSpec((step, width), lambda s, o: (jnp.maximum(s - steps, 0), 0))] * count
        + [pl.BlockSpec((last, width), lambda s, o: (1, 0))] * count,
        [pl.BlockSpec((step, columns * count), lambda s, o: (s, 0)), whole(outs[1])],
        [shape_of(a, wide) for a in outs],
        megabytes=40,
    )


def program(sizes, tokens, condition, valid, positions, w_qkv, w_out, w_up, w_down, w_ada, qk_gain, cotangent):
    n_img, n_row, n_col = sizes
    images, tile_rows, tile_cols, width = tokens.shape
    assert images == n_row == 4 and n_col == 4
    tile = tile_rows * tile_cols
    own = n_row * tile
    head_dim = qk_gain.shape[1]
    my_heads = width // head_dim // n_col
    me_img, me_row, me_col = lax.axis_index("img"), lax.axis_index("row"), lax.axis_index("col")
    order_col, order_row = block_order(n_col), block_order(n_row)
    halves = 2
    paired = n_img == 2

    def integers(*values):
        return jnp.stack(values).astype(jnp.int32)

    steps = lax.dynamic_index_in_dim(positions, me_row, 1, keepdims=False)
    bit = me_row % 2
    at_col, at_img, at_columns, at_halves, live, at_tables, source = lax.optimization_barrier(
        (
            integers(me_col),
            integers(me_img if paired else jnp.zeros_like(me_img)),
            integers(*[me_col ^ j for j in order_col]),
            integers(1 - bit, bit),
            lax.dynamic_slice_in_dim(valid, me_row, 1, axis=0),
            jnp.concatenate(
                [
                    integers(steps[0, 1, 0] - steps[0, 0, 0], steps[1, 0, 1] - steps[1, 0, 0]),
                    jnp.arange(n_row, dtype=jnp.int32),
                    integers(*[me_col ^ j for j in order_col]),
                ]
            ),
            integers(*[(me_row ^ k) * n_col + (me_col ^ j) for j in order_col for k in order_row]),
        )
    )

    def x_swap(v):
        return swap(v, "img", 2, 1)

    def y_swap(v):
        return swap(v, "col", n_col, 2)

    def core_swap(v):
        return swap(v, "col", n_col, 1)

    def z_swaps(parts):
        return [parts[0]] + [swap(p, "row", n_row, k) for p, k in zip(parts[1:], order_row[1:])]

    def over_rows(v):
        return lax.all_to_all(v, "row", split_axis=0, concat_axis=0, tiled=True)

    if paired:
        part_qkv = cut_qkv(w_qkv, at_col, 3 * halves, n_col)
        other_qkv = x_swap(part_qkv)
    else:
        full = cut_qkv(lax.all_gather(w_qkv, "img", axis=0, tiled=True), at_col, 3 * halves, n_col)
        part_qkv, other_qkv = full[: width // 2], full[width // 2 :]
    tok_row = over_rows(after(tokens, part_qkv).reshape(images * tile, width))
    cond = condition.astype(wide)
    silu_cond = jax.nn.silu(cond).astype(low)
    mod_columns = jnp.dot(after(silu_cond, part_qkv), w_ada, preferred_element_type=wide)
    mod_span = mod_columns.shape[1]
    mod_z = z_swaps([lax.dynamic_slice_in_dim(mod_columns, me_row ^ k, 1, axis=0) for k in order_row])
    cos_all, sin_a, sin_b = tables(after(at_tables, mod_columns), n_row, n_col, tile, tile_cols, head_dim)
    gain = after(jnp.pad(qk_gain, ((0, 0), (0, LANES - head_dim))), at_col)
    t = cos_all
    if paired:
        part_up, part_out, part_down = cut_rest(w_up, w_out, w_down, after(at_col, mod_columns), 2 * halves, n_col)
        other_out, other_down = x_swap(part_out), x_swap(part_down)
        other_silu = x_swap(after(silu_cond, mod_columns))
        t = part_down
    mod_row = cat(*[after(m, cos_all, t) for m in mod_z])
    mod_y, mod_core = y_swap(mod_row), core_swap(mod_row)
    t = mod_row
    mod_y, mod_core = lax.optimization_barrier((mod_y, mod_core, t))[:2]
    mod_last = core_swap(mod_y)
    tok_row = after(tok_row, mod_y)
    tok_y, tok_core = y_swap(tok_row), core_swap(tok_row)
    cot_row = over_rows(after(cotangent, tok_row).reshape(images * tile, width))
    modulation = place_modulation([mod_row, mod_y, mod_core, after(mod_last, tok_row)], source).reshape(6, width)
    tok_core = after(tok_core, modulation)
    if paired:
        other_qkv = after(other_qkv, tok_core)
    w_qkv_mine = widen(part_qkv, other_qkv, at_img, head_dim)
    tok_y = after(tok_y, w_qkv_mine)
    if paired:
        other_out, other_down, tok_y, other_silu = lax.optimization_barrier((other_out, other_down, tok_y, other_silu))
        other_up = x_swap(after(part_up, other_down))
    tok_last = core_swap(tok_y)
    toks = [tok_row, tok_y, tok_core, tok_last]

    attn_in, joined = project_qkv(toks, modulation, w_qkv_mine)
    cot_row = after(cot_row, joined)
    cot_y, cot_core = y_swap(cot_row), core_swap(cot_row)
    mixed, aug = attn_fwd(after(joined, cot_row), cos_all, sin_a, sin_b, gain, head_dim)
    if paired:
        w_out_mine = widen_rows(part_out, after(other_out, joined), at_img, head_dim)
    else:

        def cut_rows(w):
            full = lax.all_gather(w, "img", axis=0, tiled=True)
            length = full.shape[0] // (halves * n_col)
            return [
                lax.dynamic_slice_in_dim(full, (h * n_col + me_col) * length, length, axis=0) for h in range(halves)
            ]

        w_out_mine = widen_rows(*cut_rows(w_out), at_img, head_dim)
        w_down_mine = cat(*cut_rows(w_down))
        full_up = lax.all_gather(w_up, "img", axis=0, tiled=True)
        piece = full_up.shape[1] // (2 * halves * n_col)
        w_up_mine = jnp.concatenate(
            [
                lax.dynamic_slice_in_dim(full_up, (p * n_col + me_col) * piece, piece, axis=1)
                for p in range(2 * halves)
            ],
            axis=1,
        )
    cot_y, cot_core, mixed = lax.optimization_barrier((cot_y, cot_core, mixed))
    if paired:
        mixed, other_up = lax.optimization_barrier((mixed, other_up))
    sent = project([mixed], w_out_mine, 2, 2, own, low)
    got = core_swap(sent)
    cot_last = core_swap(after(cot_y, sent))
    keep = project([after(mixed, sent)], w_out_mine, 0, 2, own, wide)
    got = after(got, keep)
    sent = add_second(keep, got)
    got_y = y_swap(sent)
    cots = [cot_row, cot_y, cot_core, after(cot_last, sent)]
    t = cots[3]
    if paired:
        w_up_mine, w_down_mine = join(part_up, after(other_up, t), part_down, after(other_down, t), at_img)
        t = w_up_mine
    attn_t, mixed_t = turn_blocks([after(attn_in, t), mixed], own)
    hidden, branch, mlp_own = middle(keep, got, after(got_y, attn_t), tok_row, modulation, live)
    mlp_y, mlp_core = y_swap(mlp_own), core_swap(mlp_own)
    mlp_y, mlp_core = lax.optimization_barrier((mlp_y, mlp_core))
    xs = [mlp_own, mlp_y, mlp_core, core_swap(mlp_y)]

    act, grad_gu, grad_mlp, sent, keep = feed_forward(xs, cots, modulation, w_up_mine, w_down_mine, live)
    got = core_swap(sent)

    class Piece:
        def __init__(self, theirs, mine):
            self.sent = theirs
            self.value, self.got = mine, x_swap(theirs)

        def z_one(self, *earlier):
            self.sent, self.keep = add_halves(self.value, after(self.got, *earlier), at_halves)
            self.got = swap(self.sent, "row", n_row, 1)
            return self.sent

        def z_two(self, *earlier):
            self.sent = (self.keep + after(self.got, *earlier).astype(wide)).astype(low)
            self.got = swap(self.sent, "row", n_row, 2)
            return self.sent

        def z_three(self, *earlier):
            other = after(self.got, *earlier)
            self.keep = (self.sent.astype(wide) + other.astype(wide)).astype(low)
            self.got = swap(self.keep, "row", n_row, 1)
            return self.keep

        def y(self, *earlier):
            self.value = join_halves(self.keep, after(self.got, *earlier), at_halves)
            self.got, self.core = y_swap(self.value), core_swap(self.value)
            return self.value

        def end(self, *earlier):
            self.got, self.core = lax.optimization_barrier((self.got, self.core) + earlier)[:2]
            self.last = core_swap(self.got)
            return self.got

        def blocks(self, *earlier):
            return [self.value, self.got, self.core, after(self.last, *earlier)]

    got = after(got, keep)
    sent = add_second(keep, got)
    got_y = y_swap(sent)
    t = sent
    if paired:
        d = Piece(*grad_part([after(act, t)], grad_mlp, at_img, 0, width, 384))
        half_up = grad_gu.shape[1] // 2
        u_one = Piece(*grad_part(xs, after(grad_gu, d.sent), at_img, 0, half_up, 384))
        u_two = Piece(*grad_part(xs, after(grad_gu, u_one.sent), at_img, half_up, half_up, 384))
        t = u_two.sent
    grad_hidden, gb_own, sums_two = middle_back(
        keep, got, after(got_y, t), hidden, branch, cot_row, modulation, live
    )
    gb_y, gb_core = y_swap(gb_own), core_swap(gb_own)
    mlp_sent = project([after(act, gb_own)], w_down_mine, 2, 2, own, low)
    mlp_got = core_swap(mlp_sent)
    mlp_keep = project([after(act, mlp_sent)], w_down_mine, 0, 2, own, wide)
    t = mlp_keep
    if paired:
        t = d.z_one(t)
    gb_y, gb_core = lax.optimization_barrier((gb_y, gb_core, t))[:2]
    gb_last = core_swap(gb_y)
    mlp_got = after(mlp_got, gb_y)
    mlp_next = add_second(mlp_keep, mlp_got)
    mlp_y = y_swap(mlp_next)
    gbs = [gb_own, gb_y, gb_core, after(gb_last, mlp_next)]
    heads_back = []

    def back_of(head, *earlier):
        heads_back.append(
            attn_bwd(
                gbs, after(joined, *earlier), aug, mixed, w_out_mine, cos_all, sin_a, sin_b, gain, head_dim, head, 1
            )
        )
        return heads_back[-1][0]

    t = back_of(0)
    if paired:
        t = d.z_two(t)
        t = u_one.z_one(t)
    t = back_of(1, t)
    out_own, sums_out = result(mlp_keep, mlp_got, after(mlp_y, t), hidden, cot_row, modulation, live)
    output = over_rows(out_own)
    t = out_own
    if paired:
        t = u_one.z_two(t)
        t = d.z_three(t)
        t = u_two.z_one(t)
    t = back_of(2, t)
    if paired:
        t = d.y(t)
    t = back_of(3, t)
    assert my_heads == 4
    if paired:
        t = u_one.z_three(t)
        t = u_two.z_two(t)
    grad_heads = [g for g, _ in heads_back]
    g_gain = sum(g for _, g in heads_back)
    if paired:
        rows = width // 2
        length = my_heads * head_dim // halves
        cut = (rows + length + length // 3) // 2
        g = grad_last(attn_t, grad_heads[:3] + [after(grad_heads[3], t)], mixed_t, gbs, at_img, head_dim, cut)
        q_one, q_two = Piece(g[0], g[1]), Piece(g[2], g[3])
        t = d.end(g[0])
    sent = project(grad_heads[:3] + [after(grad_heads[3], t)], w_qkv_mine, 2, 2, own, low)
    got = core_swap(sent)
    t = sent
    if paired:
        t = u_one.y(t)
    keep = project(grad_heads[:3] + [after(grad_heads[3], t)], w_qkv_mine, 0, 2, own, wide)
    got = after(got, keep)
    sent = add_second(keep, got)
    got_y = y_swap(sent)
    t = sent
    if paired:
        t = u_two.z_three(t)
        t = q_one.z_one(t)
    output = after(output, t)
    grad_own, sums_last = last_back(keep, got, after(got_y, output), tok_row, grad_hidden, modulation, live)
    t = grad_own
    if paired:
        t = u_two.y(t)
    grad_tokens = over_rows(after(grad_own, t))
    vector = (sums_two + sums_last + sums_out)[:6]
    got = core_swap(vector)
    t = vector
    if paired:
        t = q_one.z_two(t)
        t = q_two.z_one(t)
        t = u_one.end(t)
    vector = vector + after(got, t)
    got = y_swap(vector)
    t = vector
    if paired:
        sum_down = place_rows(d.blocks(t), at_columns, 384)
        t = sum_down
    grad_mod = (vector + after(got, t)).astype(low)
    blocks = grad_mod.reshape(n_row, n_col, mod_span)
    mine = lax.dynamic_slice_in_dim(blocks, at_col[0], 1, axis=1)[:, 0]
    share = over_rows(after(mine, grad_tokens))
    t = mine
    if paired:
        t = q_two.z_two(t)
        t = q_one.z_three(t)
        sum_up = place_first(u_one.blocks(t), at_columns, halves)
        t = sum_up
    share = after(share, t)
    back = lax.dot_general(share, w_ada, (((1,), (1,)), ((), ())), preferred_element_type=wide)
    flat = jnp.concatenate([back.reshape(-1), g_gain[:, :head_dim].reshape(-1)]).reshape(1, -1)
    got = swap(flat, "row", n_row, 1)
    t = flat
    if paired:
        other_share = x_swap(share)
        t = u_two.end(t)
        t = q_one.y(t)
    flat = flat + after(got, t)
    got = swap(flat, "row", n_row, 2)
    t = flat

    def outer_product(a, b):
        return lax.dot_general(a, b, (((0,), (0,)), ((), ())), preferred_element_type=wide)

    if paired:
        grad_ada = outer_product(silu_cond, share) + outer_product(other_silu, after(other_share, t))
        t = grad_ada
    else:
        grad_ada = outer_product(
            lax.all_gather(silu_cond, "img", axis=0, tiled=True), lax.all_gather(share, "img", axis=0, tiled=True)
        )
    flat = flat + after(got, t)
    got = core_swap(flat)
    t = flat
    if paired:
        t = q_two.z_three(t)
    flat = flat + after(got, t)
    got = y_swap(flat)
    t = flat
    grad_tokens = after(grad_tokens, t).astype(wide).reshape(tokens.shape)
    output = output.reshape(tokens.shape)
    t = grad_tokens
    if paired:
        sum_up = place_second(u_two.blocks(t), sum_up, at_columns, halves)
        t = sum_up
    flat = (flat + after(got, t))[0]
    grad_silu = flat[: images * width].reshape(images, width)
    gains = flat[images * width :].reshape(2, head_dim)
    s = 1.0 / (1.0 + jnp.exp(-cond))
    grad_condition = grad_silu * (s * (1.0 + cond * (1.0 - s)))
    if paired:
        gains_other = x_swap(gains)
        t = q_two.y(grad_condition)
        t = q_one.end(t)
        gains = gains + after(gains_other, t)
        t = q_two.end(gains)
        sum_qkv, sum_out = place_last(
            q_one.blocks(t),
            q_two.blocks(t),
            at_columns,
            halves,
            head_dim,
            rows,
            length,
            3 * my_heads * head_dim,
        )
    else:
        gains = lax.psum(gains, "img")

        def weight_grad(a, b):
            return lax.dot_general(a, b, (((0,), (0,)), ((), ())), preferred_element_type=wide).astype(low)

        def reduce_columns(partial, parts):
            summed = lax.psum_scatter(lax.psum(partial, "row"), "img", scatter_dimension=0, tiled=True)
            wholes = lax.all_gather(summed, "col", axis=0)
            rows = wholes.shape[1]
            wholes = wholes.reshape(n_col, rows, parts, -1)
            return jnp.transpose(wholes, (1, 2, 0, 3)).reshape(rows, -1).astype(wide)

        def reduce_rows(partial):
            wholes = lax.all_gather(lax.psum(partial, "row"), "col", axis=0)
            columns = wholes.shape[2]
            wholes = jnp.transpose(wholes.reshape(n_col, halves, -1, columns), (1, 0, 2, 3)).reshape(-1, columns)
            return lax.psum_scatter(wholes, "img", scatter_dimension=0, tiled=True).astype(wide)

        g_qkv = weight_grad(attn_in, jnp.concatenate(grad_heads, axis=1)).reshape(width, my_heads, 3, LANES)[..., :head_dim]
        g_qkv = jnp.swapaxes(g_qkv, 1, 2).reshape(width, -1)
        g_out = weight_grad(mixed, cat(*gbs)).reshape(my_heads, LANES, width)[:, :head_dim].reshape(-1, width)
        sum_up = reduce_columns(weight_grad(cat(*xs), grad_gu), 2 * halves)
        sum_down = reduce_rows(weight_grad(act, grad_mlp))
        sum_out = reduce_rows(g_out)
        sum_qkv = reduce_columns(g_qkv, 3 * halves)
    return output, grad_tokens, grad_condition, sum_qkv, sum_out, sum_up, sum_down, grad_ada, gains


def solution(mesh):
    sizes = tuple(mesh.shape[name] for name in ("img", "row", "col"))
    placed = (
        P("img", "row", "col", None),
        P("img", None),
        P("img"),
        P(None, "img", "row", "col"),
        P("img", None),
        P("img", None),
        P("img", None),
        P("img", None),
        P(None, ("row", "col")),
        P(),
        P("img", "row", "col", None),
    )
    return jax.shard_map(
        functools.partial(program, sizes),
        mesh=mesh,
        in_specs=placed,
        out_specs=(
            P("img", "row", "col", None),
            P("img", "row", "col", None),
            P("img", None),
            P("img", None),
            P("img", None),
            P("img", None),
            P("img", None),
            P(None, ("row", "col")),
            P(),
        ),
        check_vma=False,
    )
```

```python
import functools
import math

import jax
import jax.numpy as jnp
from jax import lax
from jax.experimental import pallas as pl
from jax.experimental.pallas import tpu as pltpu
from jax.sharding import PartitionSpec as P

LANES = 128
epsilon = 1e-06
low, wide = jnp.bfloat16, jnp.float32


def bits_of(size):
    return [1 << b for b in reversed(range(size.bit_length() - 1))]


def block_order(size):
    order = [0]
    for bit in bits_of(size):
        order = order + [o ^ bit for o in order]
    return order


def swap(value, axis, size, bit):
    return lax.ppermute(value, axis, [(a, a ^ bit) for a in range(size)])


def after(value, *earlier):
    return lax.optimization_barrier((value,) + earlier)[0]


def cat(*parts):
    return jnp.concatenate(parts, axis=0)


def dot(a, b):
    return jnp.dot(a, b, preferred_element_type=wide)


def dot_t(a, b):
    return lax.dot_general(a, b, (((1,), (1,)), ((), ())), preferred_element_type=wide)


def whole(shape):
    return pl.BlockSpec(shape, lambda *_: (0,) * len(shape))


def shape_of(shape, dtype):
    return jax.ShapeDtypeStruct(shape, dtype)


def kernel(body, name, scalars, args, grid, in_specs, out_specs, out_shape, scratch=(), megabytes=32):
    none = scalars is None
    return pl.pallas_call(
        functools.partial(body, None) if none else body,
        grid_spec=pltpu.PrefetchScalarGridSpec(
            num_scalar_prefetch=0 if none else 1, grid=grid, in_specs=in_specs, out_specs=out_specs, scratch_shapes=scratch
        ),
        out_shape=out_shape,
        compiler_params=pltpu.CompilerParams(vmem_limit_bytes=megabytes * 1024 * 1024),
        cost_estimate=pl.CostEstimate(flops=1, bytes_accessed=1, transcendentals=0),
        name=name,
    )(*([] if none else [scalars]), *args)


def pick(step, refs):
    value = refs[0][...]
    for n in range(1, len(refs)):
        value = jnp.where(step == n, refs[n][...], value)
    return value


def cut_qkv_kernel(parts, count, at, w_ref, o_ref):
    piece = o_ref.shape[1] // parts
    for c in range(count):

        @pl.when(at[0] == c)
        def _():
            for p in range(parts):
                start = (p * count + c) * piece
                o_ref[:, p * piece : (p + 1) * piece] = w_ref[:, start : start + piece]


def cut_qkv(w, at, parts, count):
    rows, width = w.shape
    step = 144
    return kernel(
        functools.partial(cut_qkv_kernel, parts, count),
        "cut_qkv",
        at,
        [w],
        (rows // step,),
        [pl.BlockSpec((step, width), lambda s, o=None: (s, 0))],
        pl.BlockSpec((step, width // count), lambda s, o=None: (s, 0)),
        shape_of((rows, width // count), w.dtype),
    )


def copy_kernel(at, *refs):
    n = len(refs) // 2
    for a, b in zip(refs[:n], refs[n:]):
        b[...] = a[...]


def cut_rest(w_up, w_out, w_down, at, parts, count):
    rows, width = w_up.shape
    piece = width // (parts * count)
    shapes = [(w.shape[0] // count, w.shape[1]) for w in (w_out, w_down)]
    return kernel(
        copy_kernel,
        "cut_rest",
        at,
        [w_up, w_out, w_down],
        (parts,),
        [pl.BlockSpec((rows, piece), lambda p, o=None: (0, p * count + o[0]))]
        + [pl.BlockSpec(s, lambda p, o=None: (o[0], 0)) for s in shapes],
        [pl.BlockSpec((rows, piece), lambda p, o=None: (0, p))] + [whole(s) for s in shapes],
        [shape_of((rows, piece * parts), w_up.dtype)] + [shape_of(s, w_up.dtype) for s in shapes],
    )


def widen_kernel(head_dim, heads, at, mine_ref, other_ref, o_ref):
    src = jnp.where(at[0] == pl.program_id(0), mine_ref[...], other_ref[...])
    none = jnp.zeros((src.shape[0], LANES - head_dim), src.dtype)
    for t in range(3):
        for n in range(heads):
            start, end = (t * heads + n) * head_dim, (n * 3 + t) * LANES
            o_ref[:, end : end + LANES] = jnp.concatenate([src[:, start : start + head_dim], none], axis=1)


def widen(mine, other, at, head_dim):
    rows, width = mine.shape
    out = width // head_dim * LANES
    return kernel(
        functools.partial(widen_kernel, head_dim, width // (3 * head_dim)),
        "widen",
        at,
        [mine, other],
        (2,),
        [whole((rows, width))] * 2,
        pl.BlockSpec((rows, out), lambda h, o=None: (h, 0)),
        shape_of((2 * rows, out), mine.dtype),
    )


def widen_rows_kernel(head_dim, at, mine_ref, other_ref, o_ref):
    src = jnp.where(at[0] == pl.program_id(0), mine_ref[...], other_ref[...]).astype(wide)
    none = jnp.zeros((LANES - head_dim, src.shape[1]), wide)
    for n in range(src.shape[0] // head_dim):
        part = jnp.concatenate([src[n * head_dim : (n + 1) * head_dim], none], axis=0)
        o_ref[n * LANES : (n + 1) * LANES] = part.astype(low)


def widen_rows(mine, other, at, head_dim):
    rows, width = mine.shape
    out = rows // head_dim * LANES
    return kernel(
        functools.partial(widen_rows_kernel, head_dim),
        "widen_rows",
        at,
        [mine, other],
        (2,),
        [whole((rows, width))] * 2,
        pl.BlockSpec((out, width), lambda h, o=None: (h, 0)),
        shape_of((2 * out, width), mine.dtype),
    )


def join_kernel(at, a_ref, b_ref, c_ref, d_ref, x_ref, y_ref):
    mine = at[0] == pl.program_id(0)
    x_ref[...] = jnp.where(mine, a_ref[...], b_ref[...])
    y_ref[...] = jnp.where(mine, c_ref[...], d_ref[...])


def join(mine_up, other_up, mine_down, other_down, at):
    specs = [whole(a.shape) for a in (mine_up, other_up, mine_down, other_down)]
    return kernel(
        join_kernel,
        "join",
        at,
        [mine_up, other_up, mine_down, other_down],
        (2,),
        specs,
        [pl.BlockSpec(a.shape, lambda h, o=None: (h, 0)) for a in (mine_up, mine_down)],
        [shape_of((2 * a.shape[0], a.shape[1]), low) for a in (mine_up, mine_down)],
    )


def copied(a):
    return kernel(copy_kernel, "copied", None, [a], (1,), [whole(a.shape)], whole(a.shape), shape_of(a.shape, a.dtype))


def tables_kernel(n_row, tile, tile_cols, head_dim, at, cos_ref, a_ref, b_ref):
    shape = cos_ref.shape
    pairs = head_dim // 4
    pos = lax.broadcasted_iota(jnp.int32, shape, 0)
    lane = lax.broadcasted_iota(jnp.int32, shape, 1)
    block = pos // tile
    row_block, col_block = block % n_row, block // n_row
    row_at = jnp.zeros(shape, jnp.int32)
    for k in range(n_row):
        row_at = jnp.where(row_block == k, at[2 + k], row_at)
    col_at = jnp.zeros(shape, jnp.int32)
    for j in range(shape[0] // (tile * n_row)):
        col_at = jnp.where(col_block == j, at[2 + n_row + j], col_at)
    inside = pos % tile
    row = (row_at * (tile // tile_cols) + inside // tile_cols) * at[0]
    col = (col_at * tile_cols + inside % tile_cols) * at[1]
    half = 2 * pairs
    within = jnp.where(lane < half, lane, lane - half)
    first = within < pairs
    step = jnp.where(first, within, within - pairs).astype(wide)
    frequency = jnp.exp(step * (-math.log(10000.0) / pairs))
    angle = jnp.where(lane < half, row, col).astype(wide) * frequency
    live = lane < head_dim
    cos, sin = jnp.cos(angle), jnp.sin(angle)
    cos_ref[...] = jnp.where(live, cos, 0.0)
    a_ref[...] = jnp.where(live & first, -sin, 0.0)
    b_ref[...] = jnp.where(live & jnp.logical_not(first), sin, 0.0)


def tables(at, n_row, n_col, tile, tile_cols, head_dim):
    shape = (n_row * n_col * tile, LANES)
    return kernel(
        functools.partial(tables_kernel, n_row, tile, tile_cols, head_dim),
        "tables",
        at,
        [],
        (1,),
        [],
        [whole(shape)] * 3,
        [shape_of(shape, wide)] * 3,
    )


def place_modulation_kernel(at, *refs):
    o_ref = refs[-1]
    rows = refs[0].shape[0]
    for j, ref in enumerate(refs[:-1]):
        for k in range(rows):
            o_ref[pl.ds(at[j * rows + k], 1), :] = ref[k : k + 1, :]


def place_modulation(parts, at):
    rows, width = parts[0].shape
    shape = (rows * len(parts), width)
    return kernel(
        place_modulation_kernel,
        "place_modulation",
        at,
        parts,
        (1,),
        [whole(p.shape) for p in parts],
        whole(shape),
        shape_of(shape, wide),
    )


def inverse(v):
    return lax.rsqrt(jnp.mean(v * v, axis=-1, keepdims=True) + epsilon)


def norm_back(v, inv, stretch, g_y):
    normed = v * inv
    g = g_y * (1.0 + stretch)
    g_v = (g - normed * jnp.mean(g * normed, axis=-1, keepdims=True)) * inv
    return g_v, jnp.sum(g_y, axis=0, keepdims=True), jnp.sum(g_y * normed, axis=0, keepdims=True)


def put_rows(ref, **rows):
    ref[...] = jnp.zeros_like(ref)
    for name, row in rows.items():
        n = int(name[1:])
        ref[n : n + 1, :] = row


def turn(x, cos, sin_a, sin_b, shift):
    return x * cos + pltpu.roll(x, LANES - shift, 1) * sin_a + pltpu.roll(x, shift, 1) * sin_b


def project_qkv_kernel(at, *refs):
    toks, (mod_ref, w_ref, in_ref, joined_ref) = refs[:-4], refs[-4:]
    x = pick(pl.program_id(0), toks).astype(wide)
    attn_in = (x * inverse(x) * (1.0 + mod_ref[1:2, :]) + mod_ref[0:1, :]).astype(low)
    in_ref[...] = attn_in
    joined_ref[...] = dot(attn_in, w_ref[...])


def project_qkv(toks, modulation, w):
    rows, width = toks[0].shape
    n, columns = len(toks), w.shape[1]
    return kernel(
        project_qkv_kernel,
        "project_qkv",
        None,
        [*toks, modulation, w],
        (n,),
        [whole(t.shape) for t in toks] + [whole(modulation.shape), whole(w.shape)],
        [pl.BlockSpec((rows, width), lambda s, o=None: (s, 0)), pl.BlockSpec((rows, columns), lambda s, o=None: (s, 0))],
        [shape_of((n * rows, width), low), shape_of((n * rows, columns), wide)],
    )


def attn_fwd_kernel(head_dim, at, x_ref, cos_ref, a_ref, b_ref, gain_ref, o_ref, aug_ref):
    tokens = x_ref.shape[0]
    pairs, scale = head_dim // 4, head_dim**-0.5 * math.log2(math.e)
    cos, sa, sb = cos_ref[...], a_ref[...], b_ref[...]

    def normed(x):
        return x * lax.rsqrt(jnp.sum(x * x, axis=-1, keepdims=True) * (1.0 / head_dim) + epsilon)

    q = turn(normed(x_ref[:, :LANES]) * gain_ref[0:1, :], cos, sa, sb, pairs) * scale
    k = turn(normed(x_ref[:, LANES : 2 * LANES]) * gain_ref[1:2, :], cos, sa, sb, pairs)
    lane = lax.broadcasted_iota(jnp.int32, (tokens, LANES), 1)
    extra = (lane == head_dim) | (lane == head_dim + 1)
    kk = jnp.where(extra, 1.0, k).astype(low)
    vv = jnp.where(extra, -1.0, x_ref[:, 2 * LANES :]).astype(low)
    aug_ref[:, LANES : 2 * LANES] = kk
    aug_ref[:, 2 * LANES :] = vv
    q_low = q.astype(low)
    rows = 256
    for s in range(tokens // rows):
        span = slice(s * rows, (s + 1) * rows)
        out = dot(jnp.exp2(dot_t(q_low[span], kk)).astype(low), vv)
        total = -out[:, head_dim : head_dim + 1]
        lane_s = lane[span]
        o_ref[span, :] = jnp.where(lane_s < head_dim, out * (1.0 / total), 0.0).astype(low)
        lse = -jnp.log2(total)
        high = lse.astype(low).astype(wide)
        aug = jnp.where(lane_s == head_dim, high, jnp.where(lane_s == head_dim + 1, lse - high, q[span]))
        aug_ref[span, :LANES] = aug.astype(low)


def attn_fwd(joined, cos, sa, sb, gain, head_dim):
    tokens, columns = joined.shape
    heads = columns // (3 * LANES)
    block = pl.BlockSpec((tokens, 3 * LANES), lambda h, o=None: (0, h))
    return kernel(
        functools.partial(attn_fwd_kernel, head_dim),
        "attn_fwd",
        None,
        [joined, cos, sa, sb, gain],
        (heads,),
        [block, whole(cos.shape), whole(cos.shape), whole(cos.shape), whole(gain.shape)],
        [pl.BlockSpec((tokens, LANES), lambda h, o=None: (0, h)), block],
        [shape_of((tokens, heads * LANES), low), shape_of((tokens, columns), low)],
        megabytes=32,
    )


def attn_bwd_kernel(head_dim, at, *refs):
    n = len(refs) - 14
    gbs = refs[:n]
    x_ref, aug_ref, o_ref, w_ref, cos_ref, a_ref, b_ref, gain_ref, g_ref, gg_ref = refs[n : n + 10]
    dk_acc, dv_acc, dq_acc, do_acc = refs[n + 10 :]
    tokens = x_ref.shape[0]
    pairs = head_dim // 4
    h = pl.program_id(0)
    rows = tokens // n
    for j in range(n):
        do_acc[j * rows : (j + 1) * rows, :] = dot_t(gbs[j][...], w_ref[...]).astype(low)
    lane = lax.broadcasted_iota(jnp.int32, (tokens, LANES), 1)
    do_f = do_acc[...].astype(wide)
    delta = jnp.sum(do_f * o_ref[...].astype(wide), axis=-1, keepdims=True)
    high = delta.astype(low).astype(wide)
    do_a = jnp.where(lane == head_dim, high, jnp.where(lane == head_dim + 1, delta - high, do_f)).astype(low)
    qa, ka, va = aug_ref[:, :LANES], aug_ref[:, LANES : 2 * LANES], aug_ref[:, 2 * LANES :]
    ka_t = ka.T
    cols = 256
    for s in range(tokens // cols):
        qs = qa[s * cols : (s + 1) * cols]
        ds = do_a[s * cols : (s + 1) * cols]
        p = jnp.exp2(dot_t(ka, qs))
        grad_s = (p * dot_t(va, ds)).astype(low)
        dv, dk = dot(p.astype(low), ds), dot(grad_s, qs)
        if s == 0:
            dv_acc[...] = dv
            dk_acc[...] = dk
        else:
            dv_acc[...] += dv
            dk_acc[...] += dk
        dq_acc[:, s * cols : (s + 1) * cols] = dot(ka_t, grad_s)
    inside = lane < head_dim
    cos, sa, sb = cos_ref[...], a_ref[...], b_ref[...]

    def back(g, x, gain):
        g = jnp.where(inside, g, 0.0)
        g = g * cos - pltpu.roll(g, LANES - pairs, 1) * sa - pltpu.roll(g, pairs, 1) * sb
        inv = lax.rsqrt(jnp.sum(x * x, axis=-1, keepdims=True) * (1.0 / head_dim) + epsilon)
        normed = x * inv
        gain_part = jnp.sum(g * normed, axis=0, keepdims=True)
        g = g * gain
        return (g - normed * (jnp.sum(g * normed, axis=-1, keepdims=True) * (1.0 / head_dim))) * inv, gain_part

    gq, ggq = back(dq_acc[...].T * (head_dim**-0.5), x_ref[:, :LANES], gain_ref[0:1, :])
    gk, ggk = back(dk_acc[...] * math.log(2.0), x_ref[:, LANES : 2 * LANES], gain_ref[1:2, :])
    g_ref[:, :LANES] = gq.astype(low)
    g_ref[:, LANES : 2 * LANES] = gk.astype(low)
    g_ref[:, 2 * LANES :] = jnp.where(inside, dv_acc[...], 0.0).astype(low)
    gg = jnp.concatenate([ggq, ggk], axis=0)

    @pl.when(h == 0)
    def _():
        gg_ref[...] = gg

    @pl.when(h > 0)
    def _():
        gg_ref[...] += gg


def attn_bwd(grads, joined, aug, mixed, w_out, cos, sa, sb, gain, head_dim, first, heads):
    tokens = joined.shape[0]
    block = pl.BlockSpec((tokens, 3 * LANES), lambda h, o=None: (0, first + h))
    return kernel(
        functools.partial(attn_bwd_kernel, head_dim),
        "attn_bwd",
        None,
        [*grads, joined, aug, mixed, w_out, cos, sa, sb, gain],
        (heads,),
        [whole(g.shape) for g in grads]
        + [block, block, pl.BlockSpec((tokens, LANES), lambda h, o=None: (0, first + h))]
        + [pl.BlockSpec((LANES, w_out.shape[1]), lambda h, o=None: (first + h, 0))]
        + [whole(cos.shape), whole(cos.shape), whole(cos.shape), whole(gain.shape)],
        [pl.BlockSpec((tokens, 3 * LANES), lambda h, o=None: (0, h)), whole(gain.shape)],
        [shape_of((tokens, heads * 3 * LANES), low), shape_of(gain.shape, wide)],
        scratch=[
            pltpu.VMEM((tokens, LANES), wide),
            pltpu.VMEM((tokens, LANES), wide),
            pltpu.VMEM((LANES, tokens), wide),
            pltpu.VMEM((tokens, LANES), low),
        ],
        megabytes=32,
    )


def project_kernel(product, at, x_ref, w_ref, send_ref, keep_ref):
    value = product(x_ref[...], w_ref[...])
    half = pl.num_programs(0) // 2

    @pl.when(pl.program_id(0) < half)
    def _():
        send_ref[...] = value.astype(low)

    @pl.when(pl.program_id(0) >= half)
    def _():
        keep_ref[...] = value


def project(x, w, rows, product=dot):
    columns = w.shape[1] if product is dot else w.shape[0]
    count = x.shape[0] // rows
    half = count // 2
    return kernel(
        functools.partial(project_kernel, product),
        "project",
        None,
        [x, w],
        (count,),
        [pl.BlockSpec((rows, x.shape[1]), lambda s, o=None: ((s + half) % count, 0)), whole(w.shape)],
        [
            pl.BlockSpec((rows, columns), lambda s, o=None: (jnp.minimum(s, half - 1), 0)),
            pl.BlockSpec((rows, columns), lambda s, o=None: (jnp.maximum(s - half, 0), 0)),
        ],
        [shape_of((half * rows, columns), low), shape_of((half * rows, columns), wide)],
        megabytes=36,
    )


def add_kernel(at, a_ref, b_ref, o_ref):
    o_ref[...] = (a_ref[...].astype(wide) + b_ref[...].astype(wide)).astype(low)


def add_second(a, b):
    rows, columns = a.shape[0] // 2, a.shape[1]
    return kernel(
        add_kernel,
        "add_second",
        None,
        [a, b],
        (1,),
        [pl.BlockSpec((rows, columns), lambda s, o=None: (1, 0))] * 2,
        whole((rows, columns)),
        shape_of((rows, columns), low),
    )


def middle_kernel(live, keep_ref, core_ref, y_ref, tok_ref, mod_ref, hidden_ref, branch_ref, mlp_ref):
    branch = keep_ref[...] + core_ref[...].astype(wide) + y_ref[...].astype(wide)
    gate = mod_ref[2:3, :] * live[0].astype(wide)
    hidden = tok_ref[...].astype(wide) + gate * branch
    hidden_ref[...] = hidden
    branch_ref[...] = branch
    mlp_ref[...] = (hidden * inverse(hidden) * (1.0 + mod_ref[4:5, :]) + mod_ref[3:4, :]).astype(low)


def middle(keep, core, y, tok, modulation, live):
    shape = y.shape
    first = pl.BlockSpec(shape, lambda s, o=None: (0, 0))
    return kernel(
        middle_kernel,
        "middle",
        live,
        [keep, core, y, tok, modulation],
        (1,),
        [first, first, first, first, whole(modulation.shape)],
        [first] * 3,
        [shape_of(shape, wide), shape_of(shape, wide), shape_of(shape, low)],
    )


def middle_back_kernel(live, keep_ref, core_ref, y_ref, hidden_ref, branch_ref, cot_ref, mod_ref, grad_ref, gb_ref, s_ref):
    g_y = keep_ref[...] + core_ref[...].astype(wide) + y_ref[...].astype(wide)
    hidden = hidden_ref[...]
    on = live[0].astype(wide)
    g_v, g_o, g_a = norm_back(hidden, inverse(hidden), mod_ref[4:5, :], g_y)
    grad = cot_ref[...].astype(wide) + g_v
    grad_ref[...] = grad
    gb_ref[...] = (mod_ref[2:3, :] * on * grad).astype(low)
    put_rows(s_ref, r2=on * jnp.sum(grad * branch_ref[...], axis=0, keepdims=True), r3=g_o, r4=g_a)


def middle_back(keep, core, y, hidden, branch, cot, modulation, live):
    shape = y.shape
    first = pl.BlockSpec(shape, lambda s, o=None: (0, 0))
    sums = (8, shape[1])
    return kernel(
        middle_back_kernel,
        "middle_back",
        live,
        [keep, core, y, hidden, branch, cot, modulation],
        (1,),
        [first] * 6 + [whole(modulation.shape)],
        [first, first, whole(sums)],
        [shape_of(shape, wide), shape_of(shape, low), shape_of(sums, wide)],
    )


def result_kernel(live, keep_ref, core_ref, y_ref, hidden_ref, cot_ref, mod_ref, *outs):
    mlp_out = keep_ref[...] + core_ref[...].astype(wide) + y_ref[...].astype(wide)
    on = live[0].astype(wide)
    result = (hidden_ref[...] + mod_ref[5:6, :] * on * mlp_out).astype(low)
    put_rows(outs[-1], r5=on * jnp.sum(cot_ref[...].astype(wide) * mlp_out, axis=0, keepdims=True))
    outs[0][...] = result


def result(keep, core, y, hidden, cot, modulation, live):
    shape = y.shape
    first = pl.BlockSpec(shape, lambda s, o=None: (0, 0))
    sums = (8, shape[1])
    return kernel(
        result_kernel,
        "result",
        live,
        [keep, core, y, hidden, cot, modulation],
        (1,),
        [first] * 5 + [whole(modulation.shape)],
        [first, whole(sums)],
        [shape_of(shape, low), shape_of(sums, wide)],
    )


def last_back_kernel(live, keep_ref, core_ref, y_ref, tok_ref, grad_ref, mod_ref, *outs):
    g_y = keep_ref[...] + core_ref[...].astype(wide) + y_ref[...].astype(wide)
    tok = tok_ref[...].astype(wide)
    g_v, g_o, g_a = norm_back(tok, inverse(tok), mod_ref[1:2, :], g_y)
    grad = (grad_ref[...] + g_v).astype(low)
    put_rows(outs[-1], r0=g_o, r1=g_a)
    outs[0][...] = grad


def last_back(keep, core, y, tok, grad, modulation, live):
    shape = y.shape
    first = pl.BlockSpec(shape, lambda s, o=None: (0, 0))
    sums = (8, shape[1])
    return kernel(
        last_back_kernel,
        "last_back",
        live,
        [keep, core, y, tok, grad, modulation],
        (1,),
        [first] * 5 + [whole(modulation.shape)],
        [first, whole(sums)],
        [shape_of(shape, low), shape_of(sums, wide)],
    )


def feed_forward_kernel(n, live, *refs):
    xs, cots = refs[:n], refs[n : 2 * n]
    mod_ref, up_ref, down_ref, act_ref, gu_ref, gm_ref, send_ref, keep_ref = refs[2 * n :]
    s = pl.program_id(0)
    block = (s + n // 2) % n
    x, cot = pick(block, xs), pick(block, cots)
    w_up = up_ref[...]
    gate_up = dot(x, w_up)
    half = gate_up.shape[1] // 2
    gate, up = gate_up[:, :half], gate_up[:, half:]
    sig = 1.0 / (1.0 + jnp.exp(-gate))
    silu = gate * sig
    act_ref[...] = (silu * up).astype(low)
    grad = (mod_ref[5:6, :] * live[0].astype(wide) * cot.astype(wide)).astype(low)
    gm_ref[...] = grad
    grad_act = dot_t(grad, down_ref[...])
    gu_ref[:, :half] = (grad_act * up * sig * (1.0 + gate * (1.0 - sig))).astype(low)
    gu_ref[:, half:] = (grad_act * silu).astype(low)
    grad_in = dot_t(gu_ref[...], w_up)

    @pl.when(s < n // 2)
    def _():
        send_ref[...] = grad_in.astype(low)

    @pl.when(s >= n // 2)
    def _():
        keep_ref[...] = grad_in


def feed_forward(xs, cots, modulation, w_up, w_down, live):
    n = len(xs)
    rows, width = xs[0].shape
    hidden = w_down.shape[0]
    half = n // 2

    def by_block(columns):
        return pl.BlockSpec((rows, columns), lambda s, o=None: ((s + half) % n, 0))

    return kernel(
        functools.partial(feed_forward_kernel, n),
        "feed_forward",
        live,
        [*xs, *cots, modulation, w_up, w_down],
        (n,),
        [whole(x.shape) for x in (*xs, *cots, modulation, w_up, w_down)],
        [
            by_block(hidden),
            by_block(2 * hidden),
            by_block(width),
            pl.BlockSpec((rows, width), lambda s, o=None: (jnp.minimum(s, half - 1), 0)),
            pl.BlockSpec((rows, width), lambda s, o=None: (jnp.maximum(s - half, 0), 0)),
        ],
        [
            shape_of((n * rows, hidden), low),
            shape_of((n * rows, 2 * hidden), low),
            shape_of((n * rows, width), low),
            shape_of((half * rows, width), low),
            shape_of((half * rows, width), wide),
        ],
        megabytes=48,
    )


def halves_of(acc_ref, at):
    rows = acc_ref.shape[0] // 2
    return [acc_ref[pl.ds(pl.multiple_of(i * rows, 8), rows), :] for i in (1 - at[0], at[0])]


def turned(xs, xt_ref):
    @pl.when(pl.program_id(0) == 0)
    def _():
        rows = xs[0].shape[0]
        for j, x in enumerate(xs):
            xt_ref[:, j * rows : (j + 1) * rows] = x[...].T


def turn_kernel(at, *refs):
    n = len(refs) // 2
    for a, b in zip(refs[:n], refs[n:]):
        b[...] = a[...].T


def turn_blocks(arrays, rows):
    tokens = arrays[0].shape[0]
    return kernel(
        turn_kernel,
        "turn_blocks",
        None,
        arrays,
        (tokens // rows,),
        [pl.BlockSpec((rows, a.shape[1]), lambda s, o=None: (s, 0)) for a in arrays],
        [pl.BlockSpec((a.shape[1], rows), lambda s, o=None: (0, s)) for a in arrays],
        [shape_of((a.shape[1], tokens), a.dtype) for a in arrays],
    )


def grad_part_kernel(n, at, *refs):
    xs, (b_ref, theirs, mine, xt_ref, acc_ref) = refs[:n], refs[n:]
    turned(xs, xt_ref)
    acc_ref[...] = dot(xt_ref[...], b_ref[...])
    for ref, value in zip((theirs, mine), halves_of(acc_ref, at)):
        ref[...] = value.astype(low)


def grad_part(xs, b, at, first, columns, chunk):
    tokens, width = len(xs) * xs[0].shape[0], xs[0].shape[1]
    out = pl.BlockSpec((width // 2, chunk), lambda s, o=None: (0, s))
    return kernel(
        functools.partial(grad_part_kernel, len(xs)),
        "grad_part",
        at,
        [*xs, b],
        (columns // chunk,),
        [whole(x.shape) for x in xs] + [pl.BlockSpec((tokens, chunk), lambda s, o=None: (0, first // chunk + s))],
        [out, out],
        [shape_of((width // 2, columns), low)] * 2,
        scratch=[pltpu.VMEM((width, tokens), low), pltpu.VMEM((width, chunk), wide)],
        megabytes=36,
    )


def grad_last_kernel(n, head_dim, cut, columns, at, *refs):
    xt_ref, mt_ref = refs[:2]
    parts, gbs = refs[2 : 2 + n], refs[2 + n : 2 + 2 * n]
    outs = refs[2 + 2 * n : 6 + 2 * n]
    acc_ref, out_ref = refs[6 + 2 * n :]
    padded = outs[0].shape[1]
    wide_columns = parts[0].shape[1]
    lane = lax.broadcasted_iota(jnp.int32, (wide_columns, padded), 0)
    target = (lane // LANES) * head_dim + lane % LANES
    column = lax.broadcasted_iota(jnp.int32, (wide_columns, padded), 1)
    inside = lane % LANES < head_dim
    per = columns // n
    narrow = sum(
        dot(part[...], jnp.where(inside & (column == target + p * per), 1.0, 0.0).astype(low))
        for p, part in enumerate(parts)
    ).astype(low)
    acc_ref[...] = dot(xt_ref[...], narrow)
    for half, value in enumerate(halves_of(acc_ref, at)):
        outs[half][...] = value[:cut].astype(low)
        outs[2 + half][: value.shape[0] - cut] = value[cut:].astype(low)

    rows = gbs[0].shape[0]
    out_ref[...] = sum(dot(mt_ref[:, j * rows : (j + 1) * rows], gbs[j][...]) for j in range(n))
    for half, value in enumerate(halves_of(out_ref, at)):
        ref = outs[2 + half]
        heads = [value[h * LANES : h * LANES + head_dim] for h in range(value.shape[0] // LANES)]
        value = jnp.concatenate(heads, axis=0)
        length, third = value.shape[0], value.shape[0] // 3
        start = xt_ref.shape[0] // 2 - cut
        spare = jnp.zeros((third, padded - columns), wide)
        ref[start : start + length] = jnp.where(
            lax.broadcasted_iota(jnp.int32, (length, padded), 1) < columns, value[:, :padded], 0.0
        ).astype(low)
        rest = [value[k * third : (k + 1) * third, columns:] for k in range(3)]
        ref[start + length :] = jnp.concatenate(rest + [spare], axis=1).astype(low)


def grad_last(xt, joined, mixed_t, gbs, at, head_dim, cut):
    n = joined.shape[1] // (3 * LANES)
    assert n == len(gbs)
    tokens, part = joined.shape[0], 3 * LANES
    width = xt.shape[0]
    columns = n * 3 * head_dim
    length = mixed_t.shape[0] // LANES * head_dim // 2
    assert gbs[0].shape[1] - columns == columns // 3 and length % 3 == 0
    padded = -(-columns // LANES) * LANES
    shapes = [(cut, padded), (width // 2 - cut + length + length // 3, padded)]
    return kernel(
        functools.partial(grad_last_kernel, n, head_dim, cut, columns),
        "grad_last",
        at,
        [xt, mixed_t, *[joined] * n, *gbs],
        (1,),
        [whole(xt.shape), whole(mixed_t.shape)]
        + [pl.BlockSpec((tokens, part), lambda s, o=None, h=h: (0, h)) for h in range(n)]
        + [whole(b.shape) for b in gbs],
        [whole(a) for a in shapes for _ in range(2)],
        [shape_of(a, low) for a in shapes for _ in range(2)],
        scratch=[
            pltpu.VMEM((width, padded), wide),
            pltpu.VMEM((mixed_t.shape[0], gbs[0].shape[1]), wide),
        ],
        megabytes=50,
    )


def add_halves_kernel(at, a_ref, b_ref, send_ref, keep_ref):
    value = a_ref[...].astype(wide) + b_ref[...].astype(wide)

    @pl.when(pl.program_id(0) == 0)
    def _():
        send_ref[...] = value.astype(low)

    @pl.when(pl.program_id(0) == 1)
    def _():
        keep_ref[...] = value


def add_halves(a, b, at):
    rows, columns = a.shape[0] // 2, a.shape[1]
    block = pl.BlockSpec((rows, columns), lambda s, o=None: (o[s], 0))
    return kernel(
        add_halves_kernel,
        "add_halves",
        at,
        [a, b],
        (2,),
        [block, block],
        [whole((rows, columns))] * 2,
        [shape_of((rows, columns), low), shape_of((rows, columns), wide)],
    )


def join_halves_kernel(at, a_ref, b_ref, o_ref):
    o_ref[...] = jnp.where(pl.program_id(0) == at[1], a_ref[...], b_ref[...])


def join_halves(mine, other, at):
    rows, columns = mine.shape
    return kernel(
        join_halves_kernel,
        "join_halves",
        at,
        [mine, other],
        (2,),
        [whole(mine.shape)] * 2,
        pl.BlockSpec((rows, columns), lambda s, o=None: (s, 0)),
        shape_of((2 * rows, columns), low),
    )


def place_columns(srcs, at, start, step, parts, up_ref):
    width = srcs[0].shape[1]
    piece, count = width // parts, len(srcs)

    def put(d, block):
        for p in range(parts):
            end = (p * count + d) * piece
            up_ref[:, end : end + piece] = block[:, p * piece : (p + 1) * piece]

    for j in range(count):
        block = srcs[j][pl.ds(start, step), :].astype(wide)
        for d in range(count):
            pl.when(at[j] == d)(functools.partial(put, d, block))


def place_first_kernel(parts, at, *refs):
    srcs, up_ref = refs[:-1], refs[-1]
    step = up_ref.shape[0]
    place_columns(srcs, at, pl.multiple_of(pl.program_id(0) * step, 16), step, parts, up_ref)


def place_first(blocks, at, parts):
    count = len(blocks)
    rows, width = blocks[0].shape
    step = 144
    return kernel(
        functools.partial(place_first_kernel, parts),
        "place_first",
        at,
        blocks,
        (rows // step,),
        [whole(b.shape) for b in blocks],
        pl.BlockSpec((step, width * count), lambda s, o=None: (s, 0)),
        shape_of((rows, 2 * width * count), wide),
    )


def place_second_kernel(count, parts, at, *refs):
    srcs, up_ref = refs[:count], refs[-1]
    step = up_ref.shape[0]
    place_columns(srcs, at, pl.multiple_of(pl.program_id(0) * step, 16), step, parts, up_ref)


def place_second(blocks, first, at, parts):
    count = len(blocks)
    width = blocks[0].shape[1]
    rows = first.shape[0]
    step = 144
    return pl.pallas_call(
        functools.partial(place_second_kernel, count, parts),
        grid_spec=pltpu.PrefetchScalarGridSpec(
            num_scalar_prefetch=1,
            grid=(rows // step,),
            in_specs=[whole(b.shape) for b in blocks] + [pl.BlockSpec(memory_space=pl.ANY)],
            out_specs=pl.BlockSpec((step, width * count), lambda s, o: (s, 1)),
        ),
        out_shape=shape_of(first.shape, wide),
        input_output_aliases={count + 1: 0},
        compiler_params=pltpu.CompilerParams(vmem_limit_bytes=32 * 1024 * 1024),
        cost_estimate=pl.CostEstimate(flops=1, bytes_accessed=1, transcendentals=0),
        name="place_second",
    )(at, *blocks, first)


def place_rows_kernel(at, *refs):
    srcs, o_ref = refs[:-1], refs[-1]
    rows = srcs[0].shape[0]
    for j, ref in enumerate(srcs):
        o_ref[pl.ds(pl.multiple_of(at[j] * rows, 8), rows), :] = ref[...].astype(wide)


def place_rows(blocks, at, chunk):
    rows, width = blocks[0].shape
    n = len(blocks)
    return kernel(
        place_rows_kernel,
        "place_rows",
        at,
        blocks,
        (width // chunk,),
        [pl.BlockSpec((rows, chunk), lambda s, o=None: (0, s))] * n,
        pl.BlockSpec((n * rows, chunk), lambda s, o=None: (0, s)),
        shape_of((n * rows, width), wide),
    )


def place_rows_of(srcs, at, halves, head_dim, columns, o_ref):
    count = len(srcs)
    heads = columns // (3 * head_dim) // halves

    def put(d, block):
        for t in range(3):
            for h in range(halves):
                for u in range(heads):
                    end = ((t * halves + h) * count + d) * heads + u
                    start = (h * heads + u) * 3 + t
                    o_ref[:, end * head_dim : (end + 1) * head_dim] = block[
                        :, start * head_dim : (start + 1) * head_dim
                    ]

    for j in range(count):
        block = srcs[j][...].astype(wide)
        for d in range(count):
            pl.when(at[j] == d)(functools.partial(put, d, block))


def place_top_kernel(halves, head_dim, columns, at, *refs):
    place_rows_of(refs[:-1], at, halves, head_dim, columns, refs[-1])


def place_top(blocks, at, halves, head_dim, rows, columns):
    count = len(blocks)
    cut, width = blocks[0].shape
    step = 96
    return kernel(
        functools.partial(place_top_kernel, halves, head_dim, columns),
        "place_top",
        at,
        blocks,
        (cut // step,),
        [pl.BlockSpec((step, width), lambda s, o: (s, 0))] * count,
        pl.BlockSpec((step, columns * count), lambda s, o: (s, 0)),
        shape_of((rows, columns * count), wide),
    )


def place_last_kernel(count, halves, head_dim, columns, at, *refs):
    seconds, lasts = refs[:count], refs[count : 2 * count]
    _, o_ref, out_ref = refs[2 * count :]
    place_rows_of(seconds, at, halves, head_dim, columns, o_ref)

    @pl.when(pl.program_id(0) == 0)
    def _():
        length = out_ref.shape[0] // count
        for j in range(count):
            value = lasts[j][...].astype(wide)
            width, side = columns, columns // 3
            at_row = pl.multiple_of(at[j] * length, 8)
            out_ref[pl.ds(at_row, length), :width] = value[:length, :width]
            rest = [value[length:, k * side : (k + 1) * side] for k in range(3)]
            out_ref[pl.ds(at_row, length), width:] = jnp.concatenate(rest, axis=0)


def place_last(blocks, top, at, halves, head_dim, length, columns):
    count = len(blocks)
    step, width = 96, blocks[0].shape[1]
    rows = top.shape[0]
    last = blocks[0].shape[0] // 2
    steps = last // step
    skip = rows // step - steps
    outs = [top.shape, (count * length, columns // 3 * 4)]
    return pl.pallas_call(
        functools.partial(place_last_kernel, count, halves, head_dim, columns),
        grid_spec=pltpu.PrefetchScalarGridSpec(
            num_scalar_prefetch=1,
            grid=(steps,),
            in_specs=[pl.BlockSpec((step, width), lambda s, o: (s, 0))] * count
            + [pl.BlockSpec((last, width), lambda s, o: (1, 0))] * count
            + [pl.BlockSpec(memory_space=pl.ANY)],
            out_specs=[pl.BlockSpec((step, columns * count), lambda s, o: (skip + s, 0)), whole(outs[1])],
        ),
        out_shape=[shape_of(a, wide) for a in outs],
        input_output_aliases={2 * count + 1: 0},
        compiler_params=pltpu.CompilerParams(vmem_limit_bytes=32 * 1024 * 1024),
        cost_estimate=pl.CostEstimate(flops=1, bytes_accessed=1, transcendentals=0),
        name="place_last",
    )(at, *blocks, *blocks, top)


def program(sizes, tokens, condition, valid, positions, w_qkv, w_out, w_up, w_down, w_ada, qk_gain, cotangent):
    n_img, n_row, n_col = sizes
    images, tile_rows, tile_cols, width = tokens.shape
    assert images == n_row == 4 and n_col == 4
    tile = tile_rows * tile_cols
    own = n_row * tile
    head_dim = qk_gain.shape[1]
    my_heads = width // head_dim // n_col
    me_img, me_row, me_col = lax.axis_index("img"), lax.axis_index("row"), lax.axis_index("col")
    order_col, order_row = block_order(n_col), block_order(n_row)
    halves = 2
    paired = n_img == 2

    def integers(*values):
        return jnp.stack(values).astype(jnp.int32)

    steps = lax.dynamic_index_in_dim(positions, me_row, 1, keepdims=False)
    bit = me_row % 2
    at_col, at_img, at_columns, at_halves, live, at_tables, source = lax.optimization_barrier(
        (
            integers(me_col),
            integers(me_img if paired else jnp.zeros_like(me_img)),
            integers(*[me_col ^ j for j in order_col]),
            integers(1 - bit, bit),
            lax.dynamic_slice_in_dim(valid, me_row, 1, axis=0),
            jnp.concatenate(
                [
                    integers(steps[0, 1, 0] - steps[0, 0, 0], steps[1, 0, 1] - steps[1, 0, 0]),
                    jnp.arange(n_row, dtype=jnp.int32),
                    integers(*[me_col ^ j for j in order_col]),
                ]
            ),
            integers(*[(me_row ^ k) * n_col + (me_col ^ j) for j in order_col for k in order_row]),
        )
    )

    def x_swap(v):
        return swap(v, "img", 2, 1)

    def y_swap(v):
        return swap(v, "col", n_col, 2)

    def core_swap(v):
        return swap(v, "col", n_col, 1)

    def z_swaps(parts):
        return [parts[0]] + [swap(p, "row", n_row, k) for p, k in zip(parts[1:], order_row[1:])]

    def over_rows(v):
        return lax.all_to_all(v, "row", split_axis=0, concat_axis=0, tiled=True)

    if paired:
        part_qkv = cut_qkv(w_qkv, at_col, 3 * halves, n_col)
        other_qkv = x_swap(part_qkv)
    else:
        full = cut_qkv(lax.all_gather(w_qkv, "img", axis=0, tiled=True), at_col, 3 * halves, n_col)
        part_qkv, other_qkv = full[: width // 2], full[width // 2 :]
    tok_row = over_rows(after(tokens, part_qkv).reshape(images * tile, width))
    cond = condition.astype(wide)
    silu_cond = jax.nn.silu(cond).astype(low)
    mod_columns = jnp.dot(after(silu_cond, part_qkv), w_ada, preferred_element_type=wide)
    mod_span = mod_columns.shape[1]
    mod_z = z_swaps([lax.dynamic_slice_in_dim(mod_columns, me_row ^ k, 1, axis=0) for k in order_row])
    cos_all, sin_a, sin_b = tables(after(at_tables, mod_columns), n_row, n_col, tile, tile_cols, head_dim)
    gain = after(jnp.pad(qk_gain, ((0, 0), (0, LANES - head_dim))), at_col)
    t = cos_all
    if paired:
        part_up, part_out, part_down = cut_rest(w_up, w_out, w_down, after(at_col, mod_columns), 2 * halves, n_col)
        other_out, other_down = x_swap(part_out), x_swap(part_down)
        other_silu = x_swap(after(silu_cond, mod_columns))
        t = part_down
    mod_row = cat(*[after(m, cos_all, t) for m in mod_z])
    mod_y, mod_core = y_swap(mod_row), core_swap(mod_row)
    t = mod_row
    mod_y, mod_core = lax.optimization_barrier((mod_y, mod_core, t))[:2]
    mod_last = core_swap(mod_y)
    tok_row = after(tok_row, mod_y)
    tok_y, tok_core = y_swap(tok_row), core_swap(tok_row)
    cot_row = over_rows(after(cotangent, tok_row).reshape(images * tile, width))
    modulation = place_modulation([mod_row, mod_y, mod_core, after(mod_last, tok_row)], source).reshape(6, width)
    tok_core = after(tok_core, modulation)
    if paired:
        other_qkv = after(other_qkv, tok_core)
    w_qkv_mine = widen(part_qkv, other_qkv, at_img, head_dim)
    tok_y = after(tok_y, w_qkv_mine)
    if paired:
        other_out, other_down, tok_y, other_silu = lax.optimization_barrier((other_out, other_down, tok_y, other_silu))
        other_up = x_swap(after(part_up, other_down))
    tok_last = core_swap(tok_y)
    toks = [tok_row, tok_y, tok_core, tok_last]

    attn_in, joined = project_qkv(toks, modulation, w_qkv_mine)
    cot_row = after(cot_row, joined)
    cot_y, cot_core = y_swap(cot_row), core_swap(cot_row)
    mixed, aug = attn_fwd(after(joined, cot_row), cos_all, sin_a, sin_b, gain, head_dim)
    if paired:
        w_out_mine = widen_rows(part_out, after(other_out, joined), at_img, head_dim)
    else:

        def cut_rows(w):
            full = lax.all_gather(w, "img", axis=0, tiled=True)
            length = full.shape[0] // (halves * n_col)
            return [
                lax.dynamic_slice_in_dim(full, (h * n_col + me_col) * length, length, axis=0) for h in range(halves)
            ]

        w_out_mine = widen_rows(*cut_rows(w_out), at_img, head_dim)
        w_down_mine = cat(*cut_rows(w_down))
        full_up = lax.all_gather(w_up, "img", axis=0, tiled=True)
        piece = full_up.shape[1] // (2 * halves * n_col)
        w_up_mine = jnp.concatenate(
            [
                lax.dynamic_slice_in_dim(full_up, (p * n_col + me_col) * piece, piece, axis=1)
                for p in range(2 * halves)
            ],
            axis=1,
        )
    cot_y, cot_core, mixed = lax.optimization_barrier((cot_y, cot_core, mixed))
    if paired:
        mixed, other_up = lax.optimization_barrier((mixed, other_up))
    sent, keep = project(mixed, w_out_mine, own)
    got = core_swap(sent)
    cot_last = core_swap(after(cot_y, sent))
    got = after(got, keep)
    sent = add_second(keep, got)
    got_y = y_swap(sent)
    cots = [cot_row, cot_y, cot_core, after(cot_last, sent)]
    t = cots[3]
    if paired:
        w_up_mine, w_down_mine = join(part_up, after(other_up, t), part_down, after(other_down, t), at_img)
        t = w_up_mine
    attn_t, mixed_t = turn_blocks([after(attn_in, t), mixed], own)
    hidden, branch, mlp_own = middle(keep, got, after(got_y, attn_t), tok_row, modulation, live)
    mlp_y, mlp_core = y_swap(mlp_own), core_swap(mlp_own)
    mlp_y, mlp_core = lax.optimization_barrier((mlp_y, mlp_core))
    xs = [mlp_own, mlp_y, mlp_core, core_swap(mlp_y)]

    act, grad_gu, grad_mlp, sent, keep = feed_forward(xs, cots, modulation, w_up_mine, w_down_mine, live)
    got = core_swap(sent)

    class Piece:
        def __init__(self, theirs, mine):
            self.sent = theirs
            self.value, self.got = mine, x_swap(theirs)

        def z_one(self, *earlier):
            self.sent, self.keep = add_halves(self.value, after(self.got, *earlier), at_halves)
            self.got = swap(self.sent, "row", n_row, 1)
            return self.sent

        def z_two(self, *earlier):
            self.sent = (self.keep + after(self.got, *earlier).astype(wide)).astype(low)
            self.got = swap(self.sent, "row", n_row, 2)
            return self.sent

        def z_three(self, *earlier):
            other = after(self.got, *earlier)
            self.keep = (self.sent.astype(wide) + other.astype(wide)).astype(low)
            self.got = swap(self.keep, "row", n_row, 1)
            return self.keep

        def y(self, *earlier):
            self.value = join_halves(self.keep, after(self.got, *earlier), at_halves)
            self.got, self.core = y_swap(self.value), core_swap(self.value)
            return self.value

        def rows_in(self, *earlier):
            other = after(self.got, *earlier)
            self.sent = (self.value.astype(wide) + other.astype(wide)).astype(low)
            self.got = over_rows(self.sent)
            return self.sent

        def rows_out(self, *earlier):
            parts = after(self.got, *earlier).reshape(n_row, -1, self.got.shape[1])
            shard = jnp.sum(parts.astype(wide), axis=0).astype(low)
            self.sent = cat(*[shard] * n_row)
            self.got = over_rows(self.sent)
            return self.sent

        def y_rows(self, *earlier):
            self.value = after(self.got, *earlier)
            self.got, self.core = y_swap(self.value), core_swap(self.value)
            return self.value

        def end(self, *earlier):
            self.got, self.core = lax.optimization_barrier((self.got, self.core) + earlier)[:2]
            self.last = core_swap(self.got)
            return self.got

        def blocks(self, *earlier):
            return [self.value, self.got, self.core, after(self.last, *earlier)]

    got = after(got, keep)
    sent = add_second(keep, got)
    got_y = y_swap(sent)
    t = sent
    if paired:
        d = Piece(*grad_part([after(act, t)], grad_mlp, at_img, 0, width, 384))
        half_up = grad_gu.shape[1] // 2
        u_one = Piece(*grad_part(xs, after(grad_gu, d.sent), at_img, 0, half_up, 384))
        u_two = Piece(*grad_part(xs, after(grad_gu, u_one.sent), at_img, half_up, half_up, 384))
        t = u_two.sent
    grad_hidden, gb_own, sums_two = middle_back(
        keep, got, after(got_y, t), hidden, branch, cot_row, modulation, live
    )
    gb_y, gb_core = y_swap(gb_own), core_swap(gb_own)
    mlp_sent, mlp_keep = project(after(act, gb_own), w_down_mine, own)
    mlp_got = core_swap(mlp_sent)
    t = mlp_keep
    if paired:
        t = d.z_one(t)
    gb_y, gb_core = lax.optimization_barrier((gb_y, gb_core, t))[:2]
    gb_last = core_swap(gb_y)
    mlp_got = after(mlp_got, gb_y)
    mlp_next = add_second(mlp_keep, mlp_got)
    mlp_y = y_swap(mlp_next)
    gbs = [gb_own, gb_y, gb_core, after(gb_last, mlp_next)]
    joined_back, g_gain = attn_bwd(
        gbs, joined, aug, mixed, w_out_mine, cos_all, sin_a, sin_b, gain, head_dim, 0, my_heads
    )
    t = joined_back
    if paired:
        t = d.z_two(t)
        t = u_one.z_one(t)
    sent, keep = project(after(joined_back, t), w_qkv_mine, own, dot_t)
    got = core_swap(sent)
    t = sent
    if paired:
        rows = width // 2
        length = my_heads * head_dim // halves
        cut = (rows + length + length // 3) // 2
        g = grad_last(attn_t, after(joined_back, t), mixed_t, gbs, at_img, head_dim, cut)
        q_one, q_two = Piece(g[0], g[1]), Piece(g[2], g[3])
        t = g[0]
    got = after(got, t)
    sent = add_second(keep, got)
    got_y = y_swap(sent)
    t = sent
    if paired:
        t = u_two.z_one(t)
        t = d.z_three(t)
    out_own, sums_out = result(mlp_keep, mlp_got, after(mlp_y, t), hidden, cot_row, modulation, live)
    output = over_rows(out_own)
    t = out_own
    if paired:
        t = u_one.z_two(t)
    grad_own, sums_last = last_back(keep, got, after(got_y, t), tok_row, grad_hidden, modulation, live)
    vector = (sums_two + sums_last + sums_out)[:6]
    got = core_swap(vector)
    t = vector
    if paired:
        t = d.y(t)
        t = q_one.z_one(t)
    vector = vector + after(got, t)
    got = y_swap(vector)
    t = vector
    if paired:
        t = u_two.z_two(t)
        t = u_one.z_three(t)
        t = q_two.z_one(t)
        t = d.end(t)
    grad_mod = (vector + after(got, t)).astype(low)
    blocks = grad_mod.reshape(n_row, n_col, mod_span)
    mine = lax.dynamic_slice_in_dim(blocks, at_col[0], 1, axis=1)[:, 0]
    share_z = z_swaps([lax.dynamic_slice_in_dim(mine, me_row ^ k, 1, axis=0) for k in order_row])
    t = mine
    if paired:
        t = u_one.y(t)
        t = q_one.z_two(t)
    output = copied(after(output, t))
    grad_tokens = over_rows(after(grad_own, output))
    t = output
    if paired:
        sum_down = place_rows(d.blocks(t), at_columns, 384)
        t = u_two.z_three(sum_down)
        t = q_two.z_two(t)
    at_image = [jnp.argmax(jnp.stack([(me_row ^ b) == k for k in order_row])) for b in range(images)]
    share_rel = cat(*[after(v, t) for v in share_z])
    share = cat(*[lax.dynamic_slice_in_dim(share_rel, a, 1, axis=0) for a in at_image])
    back = lax.dot_general(share, w_ada, (((1,), (1,)), ((), ())), preferred_element_type=wide)
    flat = jnp.concatenate([back.reshape(-1), g_gain[:, :head_dim].reshape(-1)]).reshape(1, -1)
    got = swap(flat, "row", n_row, 1)
    t = flat
    if paired:
        other_share = x_swap(share)
        t = u_one.end(t)
        t = u_two.y(t)
        t = q_one.z_three(t)
    flat = flat + after(got, t)
    got = swap(flat, "row", n_row, 2)
    t = flat
    if paired:
        sum_up = place_first(u_one.blocks(t), at_columns, halves)
        t = q_two.z_three(sum_up)

    def outer_product(a, b):
        return lax.dot_general(a, b, (((0,), (0,)), ((), ())), preferred_element_type=wide)

    if paired:
        grad_ada = outer_product(silu_cond, share) + outer_product(other_silu, after(other_share, t))
        t = grad_ada
    else:
        grad_ada = outer_product(
            lax.all_gather(silu_cond, "img", axis=0, tiled=True), lax.all_gather(share, "img", axis=0, tiled=True)
        )
    flat = flat + after(got, t)
    got = core_swap(flat)
    t = flat
    if paired:
        t = q_one.y(t)
        t = u_two.end(t)
    flat = flat + after(got, t)
    got = y_swap(flat)
    t = flat
    grad_tokens = after(grad_tokens, t).astype(wide).reshape(tokens.shape)
    output = output.reshape(tokens.shape)
    t = grad_tokens
    if paired:
        t = q_two.y(t)
        sum_up = place_second(u_two.blocks(t), sum_up, at_columns, halves)
        t = sum_up
    flat = (flat + after(got, t))[0]
    grad_silu = flat[: images * width].reshape(images, width)
    gains = flat[images * width :].reshape(2, head_dim)
    s = 1.0 / (1.0 + jnp.exp(-cond))
    grad_condition = grad_silu * (s * (1.0 + cond * (1.0 - s)))
    if paired:
        gains_other = x_swap(gains)
        t = q_one.end(grad_condition)
        gains = gains + after(gains_other, t)
        columns = 3 * my_heads * head_dim
        top = place_top(q_one.blocks(gains), at_columns, halves, head_dim, rows, columns)
        t = q_two.end(top)
        sum_qkv, sum_out = place_last(q_two.blocks(t), top, at_columns, halves, head_dim, length, columns)
    else:
        gains = lax.psum(gains, "img")

        def weight_grad(a, b):
            return lax.dot_general(a, b, (((0,), (0,)), ((), ())), preferred_element_type=wide).astype(low)

        def reduce_columns(partial, parts):
            summed = lax.psum_scatter(lax.psum(partial, "row"), "img", scatter_dimension=0, tiled=True)
            wholes = lax.all_gather(summed, "col", axis=0)
            rows = wholes.shape[1]
            wholes = wholes.reshape(n_col, rows, parts, -1)
            return jnp.transpose(wholes, (1, 2, 0, 3)).reshape(rows, -1).astype(wide)

        def reduce_rows(partial):
            wholes = lax.all_gather(lax.psum(partial, "row"), "col", axis=0)
            columns = wholes.shape[2]
            wholes = jnp.transpose(wholes.reshape(n_col, halves, -1, columns), (1, 0, 2, 3)).reshape(-1, columns)
            return lax.psum_scatter(wholes, "img", scatter_dimension=0, tiled=True).astype(wide)

        g_qkv = weight_grad(attn_in, joined_back).reshape(width, my_heads, 3, LANES)[..., :head_dim]
        g_qkv = jnp.swapaxes(g_qkv, 1, 2).reshape(width, -1)
        g_out = weight_grad(mixed, cat(*gbs)).reshape(my_heads, LANES, width)[:, :head_dim].reshape(-1, width)
        sum_up = reduce_columns(weight_grad(cat(*xs), grad_gu), 2 * halves)
        sum_down = reduce_rows(weight_grad(act, grad_mlp))
        sum_out = reduce_rows(g_out)
        sum_qkv = reduce_columns(g_qkv, 3 * halves)
    return output, grad_tokens, grad_condition, sum_qkv, sum_out, sum_up, sum_down, grad_ada, gains


def solution(mesh):
    sizes = tuple(mesh.shape[name] for name in ("img", "row", "col"))
    placed = (
        P("img", "row", "col", None),
        P("img", None),
        P("img"),
        P(None, "img", "row", "col"),
        P("img", None),
        P("img", None),
        P("img", None),
        P("img", None),
        P(None, ("row", "col")),
        P(),
        P("img", "row", "col", None),
    )
    return jax.shard_map(
        functools.partial(program, sizes),
        mesh=mesh,
        in_specs=placed,
        out_specs=(
            P("img", "row", "col", None),
            P("img", "row", "col", None),
            P("img", None),
            P("img", None),
            P("img", None),
            P("img", None),
            P("img", None),
            P(None, ("row", "col")),
            P(),
        ),
        check_vma=False,
    )
```

```python
import functools
import math

import jax
import jax.numpy as jnp
from jax import lax
from jax.experimental import pallas as pl
from jax.experimental.pallas import tpu as pltpu
from jax.sharding import PartitionSpec as P

LANES = 128
epsilon = 1e-06
low, wide = jnp.bfloat16, jnp.float32


def bits_of(size):
    return [1 << b for b in reversed(range(size.bit_length() - 1))]


def block_order(size):
    order = [0]
    for bit in bits_of(size):
        order = order + [o ^ bit for o in order]
    return order


def swap(value, axis, size, bit):
    return lax.ppermute(value, axis, [(a, a ^ bit) for a in range(size)])


def after(value, *earlier):
    return lax.optimization_barrier((value,) + earlier)[0]


def cat(*parts):
    return jnp.concatenate(parts, axis=0)


def dot(a, b):
    return jnp.dot(a, b, preferred_element_type=wide)


def dot_t(a, b):
    return lax.dot_general(a, b, (((1,), (1,)), ((), ())), preferred_element_type=wide)


def whole(shape):
    return pl.BlockSpec(shape, lambda *_: (0,) * len(shape))


def shape_of(shape, dtype):
    return jax.ShapeDtypeStruct(shape, dtype)


def kernel(body, name, scalars, args, grid, in_specs, out_specs, out_shape, scratch=(), megabytes=32):
    none = scalars is None
    return pl.pallas_call(
        functools.partial(body, None) if none else body,
        grid_spec=pltpu.PrefetchScalarGridSpec(
            num_scalar_prefetch=0 if none else 1, grid=grid, in_specs=in_specs, out_specs=out_specs, scratch_shapes=scratch
        ),
        out_shape=out_shape,
        compiler_params=pltpu.CompilerParams(vmem_limit_bytes=megabytes * 1024 * 1024),
        cost_estimate=pl.CostEstimate(flops=1, bytes_accessed=1, transcendentals=0),
        name=name,
    )(*([] if none else [scalars]), *args)


def pick(step, refs):
    value = refs[0][...]
    for n in range(1, len(refs)):
        value = jnp.where(step == n, refs[n][...], value)
    return value


def cut_qkv_kernel(parts, count, at, w_ref, o_ref):
    piece = o_ref.shape[1] // parts
    for c in range(count):

        @pl.when(at[0] == c)
        def _():
            for p in range(parts):
                start = (p * count + c) * piece
                o_ref[:, p * piece : (p + 1) * piece] = w_ref[:, start : start + piece]


def cut_qkv(w, at, parts, count):
    rows, width = w.shape
    step = 144
    return kernel(
        functools.partial(cut_qkv_kernel, parts, count),
        "cut_qkv",
        at,
        [w],
        (rows // step,),
        [pl.BlockSpec((step, width), lambda s, o=None: (s, 0))],
        pl.BlockSpec((step, width // count), lambda s, o=None: (s, 0)),
        shape_of((rows, width // count), w.dtype),
    )


def copy_kernel(at, *refs):
    n = len(refs) // 2
    for a, b in zip(refs[:n], refs[n:]):
        b[...] = a[...]


def cut_rest(w_up, w_out, w_down, at, parts, count):
    rows, width = w_up.shape
    piece = width // (parts * count)
    shapes = [(w.shape[0] // count, w.shape[1]) for w in (w_out, w_down)]
    return kernel(
        copy_kernel,
        "cut_rest",
        at,
        [w_up, w_out, w_down],
        (parts,),
        [pl.BlockSpec((rows, piece), lambda p, o=None: (0, p * count + o[0]))]
        + [pl.BlockSpec(s, lambda p, o=None: (o[0], 0)) for s in shapes],
        [pl.BlockSpec((rows, piece), lambda p, o=None: (0, p))] + [whole(s) for s in shapes],
        [shape_of((rows, piece * parts), w_up.dtype)] + [shape_of(s, w_up.dtype) for s in shapes],
    )


def widen_kernel(head_dim, heads, at, mine_ref, other_ref, o_ref):
    src = jnp.where(at[0] == pl.program_id(0), mine_ref[...], other_ref[...])
    none = jnp.zeros((src.shape[0], LANES - head_dim), src.dtype)
    for t in range(3):
        for n in range(heads):
            start, end = (t * heads + n) * head_dim, (n * 3 + t) * LANES
            o_ref[:, end : end + LANES] = jnp.concatenate([src[:, start : start + head_dim], none], axis=1)


def widen(mine, other, at, head_dim):
    rows, width = mine.shape
    out = width // head_dim * LANES
    return kernel(
        functools.partial(widen_kernel, head_dim, width // (3 * head_dim)),
        "widen",
        at,
        [mine, other],
        (2,),
        [whole((rows, width))] * 2,
        pl.BlockSpec((rows, out), lambda h, o=None: (h, 0)),
        shape_of((2 * rows, out), mine.dtype),
    )


def widen_rows_kernel(head_dim, at, mine_ref, other_ref, o_ref):
    src = jnp.where(at[0] == pl.program_id(0), mine_ref[...], other_ref[...]).astype(wide)
    none = jnp.zeros((LANES - head_dim, src.shape[1]), wide)
    for n in range(src.shape[0] // head_dim):
        part = jnp.concatenate([src[n * head_dim : (n + 1) * head_dim], none], axis=0)
        o_ref[n * LANES : (n + 1) * LANES] = part.astype(low)


def widen_rows(mine, other, at, head_dim):
    rows, width = mine.shape
    out = rows // head_dim * LANES
    return kernel(
        functools.partial(widen_rows_kernel, head_dim),
        "widen_rows",
        at,
        [mine, other],
        (2,),
        [whole((rows, width))] * 2,
        pl.BlockSpec((out, width), lambda h, o=None: (h, 0)),
        shape_of((2 * out, width), mine.dtype),
    )


def join_kernel(at, a_ref, b_ref, c_ref, d_ref, x_ref, y_ref):
    mine = at[0] == pl.program_id(0)
    x_ref[...] = jnp.where(mine, a_ref[...], b_ref[...])
    y_ref[...] = jnp.where(mine, c_ref[...], d_ref[...])


def join(mine_up, other_up, mine_down, other_down, at):
    specs = [whole(a.shape) for a in (mine_up, other_up, mine_down, other_down)]
    return kernel(
        join_kernel,
        "join",
        at,
        [mine_up, other_up, mine_down, other_down],
        (2,),
        specs,
        [pl.BlockSpec(a.shape, lambda h, o=None: (h, 0)) for a in (mine_up, mine_down)],
        [shape_of((2 * a.shape[0], a.shape[1]), low) for a in (mine_up, mine_down)],
    )


def copied(a):
    return kernel(copy_kernel, "copied", None, [a], (1,), [whole(a.shape)], whole(a.shape), shape_of(a.shape, a.dtype))


def tables_kernel(n_row, tile, tile_cols, head_dim, at, cos_ref, a_ref, b_ref):
    shape = cos_ref.shape
    pairs = head_dim // 4
    pos = lax.broadcasted_iota(jnp.int32, shape, 0)
    lane = lax.broadcasted_iota(jnp.int32, shape, 1)
    block = pos // tile
    row_block, col_block = block % n_row, block // n_row
    row_at = jnp.zeros(shape, jnp.int32)
    for k in range(n_row):
        row_at = jnp.where(row_block == k, at[2 + k], row_at)
    col_at = jnp.zeros(shape, jnp.int32)
    for j in range(shape[0] // (tile * n_row)):
        col_at = jnp.where(col_block == j, at[2 + n_row + j], col_at)
    inside = pos % tile
    row = (row_at * (tile // tile_cols) + inside // tile_cols) * at[0]
    col = (col_at * tile_cols + inside % tile_cols) * at[1]
    half = 2 * pairs
    within = jnp.where(lane < half, lane, lane - half)
    first = within < pairs
    step = jnp.where(first, within, within - pairs).astype(wide)
    frequency = jnp.exp(step * (-math.log(10000.0) / pairs))
    angle = jnp.where(lane < half, row, col).astype(wide) * frequency
    live = lane < head_dim
    cos, sin = jnp.cos(angle), jnp.sin(angle)
    cos_ref[...] = jnp.where(live, cos, 0.0)
    a_ref[...] = jnp.where(live & first, -sin, 0.0)
    b_ref[...] = jnp.where(live & jnp.logical_not(first), sin, 0.0)


def tables(at, n_row, n_col, tile, tile_cols, head_dim):
    shape = (n_row * n_col * tile, LANES)
    return kernel(
        functools.partial(tables_kernel, n_row, tile, tile_cols, head_dim),
        "tables",
        at,
        [],
        (1,),
        [],
        [whole(shape)] * 3,
        [shape_of(shape, wide)] * 3,
    )


def place_modulation_kernel(at, *refs):
    o_ref = refs[-1]
    rows = refs[0].shape[0]
    for j, ref in enumerate(refs[:-1]):
        for k in range(rows):
            o_ref[pl.ds(at[j * rows + k], 1), :] = ref[k : k + 1, :]


def place_modulation(parts, at):
    rows, width = parts[0].shape
    shape = (rows * len(parts), width)
    return kernel(
        place_modulation_kernel,
        "place_modulation",
        at,
        parts,
        (1,),
        [whole(p.shape) for p in parts],
        whole(shape),
        shape_of(shape, wide),
    )


def inverse(v):
    return lax.rsqrt(jnp.mean(v * v, axis=-1, keepdims=True) + epsilon)


def norm_back(v, inv, stretch, g_y):
    normed = v * inv
    g = g_y * (1.0 + stretch)
    g_v = (g - normed * jnp.mean(g * normed, axis=-1, keepdims=True)) * inv
    return g_v, jnp.sum(g_y, axis=0, keepdims=True), jnp.sum(g_y * normed, axis=0, keepdims=True)


def put_rows(ref, **rows):
    ref[...] = jnp.zeros_like(ref)
    for name, row in rows.items():
        n = int(name[1:])
        ref[n : n + 1, :] = row


def turn(x, cos, sin_a, sin_b, shift):
    return x * cos + pltpu.roll(x, LANES - shift, 1) * sin_a + pltpu.roll(x, shift, 1) * sin_b


def project_qkv_kernel(at, *refs):
    toks, (mod_ref, w_ref, in_ref, joined_ref) = refs[:-4], refs[-4:]
    x = pick(pl.program_id(0), toks).astype(wide)
    attn_in = (x * inverse(x) * (1.0 + mod_ref[1:2, :]) + mod_ref[0:1, :]).astype(low)
    in_ref[...] = attn_in
    joined_ref[...] = dot(attn_in, w_ref[...])


def project_qkv(toks, modulation, w):
    rows, width = toks[0].shape
    n, columns = len(toks), w.shape[1]
    return kernel(
        project_qkv_kernel,
        "project_qkv",
        None,
        [*toks, modulation, w],
        (n,),
        [whole(t.shape) for t in toks] + [whole(modulation.shape), whole(w.shape)],
        [pl.BlockSpec((rows, width), lambda s, o=None: (s, 0)), pl.BlockSpec((rows, columns), lambda s, o=None: (s, 0))],
        [shape_of((n * rows, width), low), shape_of((n * rows, columns), wide)],
    )


def attn_fwd_kernel(head_dim, at, x_ref, cos_ref, a_ref, b_ref, gain_ref, o_ref, aug_ref):
    tokens = x_ref.shape[0]
    pairs, scale = head_dim // 4, head_dim**-0.5 * math.log2(math.e)
    cos, sa, sb = cos_ref[...], a_ref[...], b_ref[...]

    def normed(x):
        return x * lax.rsqrt(jnp.sum(x * x, axis=-1, keepdims=True) * (1.0 / head_dim) + epsilon)

    q = turn(normed(x_ref[:, :LANES]) * gain_ref[0:1, :], cos, sa, sb, pairs) * scale
    k = turn(normed(x_ref[:, LANES : 2 * LANES]) * gain_ref[1:2, :], cos, sa, sb, pairs)
    lane = lax.broadcasted_iota(jnp.int32, (tokens, LANES), 1)
    extra = (lane == head_dim) | (lane == head_dim + 1)
    kk = jnp.where(extra, 1.0, k).astype(low)
    vv = jnp.where(extra, -1.0, x_ref[:, 2 * LANES :]).astype(low)
    aug_ref[:, LANES : 2 * LANES] = kk
    aug_ref[:, 2 * LANES :] = vv
    q_low = q.astype(low)
    rows = 256
    for s in range(tokens // rows):
        span = slice(s * rows, (s + 1) * rows)
        out = dot(jnp.exp2(dot_t(q_low[span], kk)).astype(low), vv)
        total = -out[:, head_dim : head_dim + 1]
        lane_s = lane[span]
        o_ref[span, :] = jnp.where(lane_s < head_dim, out * (1.0 / total), 0.0).astype(low)
        lse = -jnp.log2(total)
        high = lse.astype(low).astype(wide)
        aug = jnp.where(lane_s == head_dim, high, jnp.where(lane_s == head_dim + 1, lse - high, q[span]))
        aug_ref[span, :LANES] = aug.astype(low)


def attn_fwd(joined, cos, sa, sb, gain, head_dim):
    tokens, columns = joined.shape
    heads = columns // (3 * LANES)
    block = pl.BlockSpec((tokens, 3 * LANES), lambda h, o=None: (0, h))
    return kernel(
        functools.partial(attn_fwd_kernel, head_dim),
        "attn_fwd",
        None,
        [joined, cos, sa, sb, gain],
        (heads,),
        [block, whole(cos.shape), whole(cos.shape), whole(cos.shape), whole(gain.shape)],
        [pl.BlockSpec((tokens, LANES), lambda h, o=None: (0, h)), block],
        [shape_of((tokens, heads * LANES), low), shape_of((tokens, columns), low)],
        megabytes=32,
    )


def attn_bwd_kernel(head_dim, at, *refs):
    n = len(refs) - 14
    gbs = refs[:n]
    x_ref, aug_ref, o_ref, w_ref, cos_ref, a_ref, b_ref, gain_ref, g_ref, gg_ref = refs[n : n + 10]
    dk_acc, dv_acc, dq_acc, do_acc = refs[n + 10 :]
    tokens = x_ref.shape[0]
    pairs = head_dim // 4
    h = pl.program_id(0)
    rows = tokens // n
    for j in range(n):
        do_acc[j * rows : (j + 1) * rows, :] = dot_t(gbs[j][...], w_ref[...]).astype(low)
    lane = lax.broadcasted_iota(jnp.int32, (tokens, LANES), 1)
    do_f = do_acc[...].astype(wide)
    delta = jnp.sum(do_f * o_ref[...].astype(wide), axis=-1, keepdims=True)
    high = delta.astype(low).astype(wide)
    do_a = jnp.where(lane == head_dim, high, jnp.where(lane == head_dim + 1, delta - high, do_f)).astype(low)
    qa, ka, va = aug_ref[:, :LANES], aug_ref[:, LANES : 2 * LANES], aug_ref[:, 2 * LANES :]
    ka_t = ka.T
    cols = 256
    for s in range(tokens // cols):
        qs = qa[s * cols : (s + 1) * cols]
        ds = do_a[s * cols : (s + 1) * cols]
        p = jnp.exp2(dot_t(ka, qs))
        grad_s = (p * dot_t(va, ds)).astype(low)
        dv, dk = dot(p.astype(low), ds), dot(grad_s, qs)
        if s == 0:
            dv_acc[...] = dv
            dk_acc[...] = dk
        else:
            dv_acc[...] += dv
            dk_acc[...] += dk
        dq_acc[:, s * cols : (s + 1) * cols] = dot(ka_t, grad_s)
    inside = lane < head_dim
    cos, sa, sb = cos_ref[...], a_ref[...], b_ref[...]

    def back(g, x, gain):
        g = jnp.where(inside, g, 0.0)
        g = g * cos - pltpu.roll(g, LANES - pairs, 1) * sa - pltpu.roll(g, pairs, 1) * sb
        inv = lax.rsqrt(jnp.sum(x * x, axis=-1, keepdims=True) * (1.0 / head_dim) + epsilon)
        normed = x * inv
        gain_part = jnp.sum(g * normed, axis=0, keepdims=True)
        g = g * gain
        return (g - normed * (jnp.sum(g * normed, axis=-1, keepdims=True) * (1.0 / head_dim))) * inv, gain_part

    gq, ggq = back(dq_acc[...].T * (head_dim**-0.5), x_ref[:, :LANES], gain_ref[0:1, :])
    gk, ggk = back(dk_acc[...] * math.log(2.0), x_ref[:, LANES : 2 * LANES], gain_ref[1:2, :])
    g_ref[:, :LANES] = gq.astype(low)
    g_ref[:, LANES : 2 * LANES] = gk.astype(low)
    g_ref[:, 2 * LANES :] = jnp.where(inside, dv_acc[...], 0.0).astype(low)
    gg = jnp.concatenate([ggq, ggk], axis=0)

    @pl.when(h == 0)
    def _():
        gg_ref[...] = gg

    @pl.when(h > 0)
    def _():
        gg_ref[...] += gg


def attn_bwd(grads, joined, aug, mixed, w_out, cos, sa, sb, gain, head_dim, first, heads):
    tokens = joined.shape[0]
    block = pl.BlockSpec((tokens, 3 * LANES), lambda h, o=None: (0, first + h))
    return kernel(
        functools.partial(attn_bwd_kernel, head_dim),
        "attn_bwd",
        None,
        [*grads, joined, aug, mixed, w_out, cos, sa, sb, gain],
        (heads,),
        [whole(g.shape) for g in grads]
        + [block, block, pl.BlockSpec((tokens, LANES), lambda h, o=None: (0, first + h))]
        + [pl.BlockSpec((LANES, w_out.shape[1]), lambda h, o=None: (first + h, 0))]
        + [whole(cos.shape), whole(cos.shape), whole(cos.shape), whole(gain.shape)],
        [pl.BlockSpec((tokens, 3 * LANES), lambda h, o=None: (0, h)), whole(gain.shape)],
        [shape_of((tokens, heads * 3 * LANES), low), shape_of(gain.shape, wide)],
        scratch=[
            pltpu.VMEM((tokens, LANES), wide),
            pltpu.VMEM((tokens, LANES), wide),
            pltpu.VMEM((LANES, tokens), wide),
            pltpu.VMEM((tokens, LANES), low),
        ],
        megabytes=32,
    )


def project_kernel(product, at, x_ref, w_ref, send_ref, keep_ref):
    value = product(x_ref[...], w_ref[...])
    half = pl.num_programs(0) // 2

    @pl.when(pl.program_id(0) < half)
    def _():
        send_ref[...] = value.astype(low)

    @pl.when(pl.program_id(0) >= half)
    def _():
        keep_ref[...] = value


def project(x, w, rows, product=dot):
    columns = w.shape[1] if product is dot else w.shape[0]
    count = x.shape[0] // rows
    half = count // 2
    return kernel(
        functools.partial(project_kernel, product),
        "project",
        None,
        [x, w],
        (count,),
        [pl.BlockSpec((rows, x.shape[1]), lambda s, o=None: ((s + half) % count, 0)), whole(w.shape)],
        [
            pl.BlockSpec((rows, columns), lambda s, o=None: (jnp.minimum(s, half - 1), 0)),
            pl.BlockSpec((rows, columns), lambda s, o=None: (jnp.maximum(s - half, 0), 0)),
        ],
        [shape_of((half * rows, columns), low), shape_of((half * rows, columns), wide)],
        megabytes=36,
    )


def add_kernel(at, a_ref, b_ref, o_ref):
    o_ref[...] = (a_ref[...].astype(wide) + b_ref[...].astype(wide)).astype(low)


def add_second(a, b):
    rows, columns = a.shape[0] // 2, a.shape[1]
    return kernel(
        add_kernel,
        "add_second",
        None,
        [a, b],
        (1,),
        [pl.BlockSpec((rows, columns), lambda s, o=None: (1, 0))] * 2,
        whole((rows, columns)),
        shape_of((rows, columns), low),
    )


def middle_kernel(live, keep_ref, core_ref, y_ref, tok_ref, mod_ref, hidden_ref, branch_ref, mlp_ref):
    branch = keep_ref[...] + core_ref[...].astype(wide) + y_ref[...].astype(wide)
    gate = mod_ref[2:3, :] * live[0].astype(wide)
    hidden = tok_ref[...].astype(wide) + gate * branch
    hidden_ref[...] = hidden
    branch_ref[...] = branch
    mlp_ref[...] = (hidden * inverse(hidden) * (1.0 + mod_ref[4:5, :]) + mod_ref[3:4, :]).astype(low)


def middle(keep, core, y, tok, modulation, live):
    shape = y.shape
    first = pl.BlockSpec(shape, lambda s, o=None: (0, 0))
    return kernel(
        middle_kernel,
        "middle",
        live,
        [keep, core, y, tok, modulation],
        (1,),
        [first, first, first, first, whole(modulation.shape)],
        [first] * 3,
        [shape_of(shape, wide), shape_of(shape, wide), shape_of(shape, low)],
    )


def middle_back_kernel(live, keep_ref, core_ref, y_ref, hidden_ref, branch_ref, cot_ref, mod_ref, grad_ref, gb_ref, s_ref):
    g_y = keep_ref[...] + core_ref[...].astype(wide) + y_ref[...].astype(wide)
    hidden = hidden_ref[...]
    on = live[0].astype(wide)
    g_v, g_o, g_a = norm_back(hidden, inverse(hidden), mod_ref[4:5, :], g_y)
    grad = cot_ref[...].astype(wide) + g_v
    grad_ref[...] = grad
    gb_ref[...] = (mod_ref[2:3, :] * on * grad).astype(low)
    put_rows(s_ref, r2=on * jnp.sum(grad * branch_ref[...], axis=0, keepdims=True), r3=g_o, r4=g_a)


def middle_back(keep, core, y, hidden, branch, cot, modulation, live):
    shape = y.shape
    first = pl.BlockSpec(shape, lambda s, o=None: (0, 0))
    sums = (8, shape[1])
    return kernel(
        middle_back_kernel,
        "middle_back",
        live,
        [keep, core, y, hidden, branch, cot, modulation],
        (1,),
        [first] * 6 + [whole(modulation.shape)],
        [first, first, whole(sums)],
        [shape_of(shape, wide), shape_of(shape, low), shape_of(sums, wide)],
    )


def result_kernel(live, keep_ref, core_ref, y_ref, hidden_ref, cot_ref, mod_ref, *outs):
    mlp_out = keep_ref[...] + core_ref[...].astype(wide) + y_ref[...].astype(wide)
    on = live[0].astype(wide)
    result = (hidden_ref[...] + mod_ref[5:6, :] * on * mlp_out).astype(low)
    put_rows(outs[-1], r5=on * jnp.sum(cot_ref[...].astype(wide) * mlp_out, axis=0, keepdims=True))
    outs[0][...] = result


def result(keep, core, y, hidden, cot, modulation, live):
    shape = y.shape
    first = pl.BlockSpec(shape, lambda s, o=None: (0, 0))
    sums = (8, shape[1])
    return kernel(
        result_kernel,
        "result",
        live,
        [keep, core, y, hidden, cot, modulation],
        (1,),
        [first] * 5 + [whole(modulation.shape)],
        [first, whole(sums)],
        [shape_of(shape, low), shape_of(sums, wide)],
    )


def last_back_kernel(live, keep_ref, core_ref, y_ref, tok_ref, grad_ref, mod_ref, *outs):
    g_y = keep_ref[...] + core_ref[...].astype(wide) + y_ref[...].astype(wide)
    tok = tok_ref[...].astype(wide)
    g_v, g_o, g_a = norm_back(tok, inverse(tok), mod_ref[1:2, :], g_y)
    grad = (grad_ref[...] + g_v).astype(low)
    put_rows(outs[-1], r0=g_o, r1=g_a)
    outs[0][...] = grad


def last_back(keep, core, y, tok, grad, modulation, live):
    shape = y.shape
    first = pl.BlockSpec(shape, lambda s, o=None: (0, 0))
    sums = (8, shape[1])
    return kernel(
        last_back_kernel,
        "last_back",
        live,
        [keep, core, y, tok, grad, modulation],
        (1,),
        [first] * 5 + [whole(modulation.shape)],
        [first, whole(sums)],
        [shape_of(shape, low), shape_of(sums, wide)],
    )


def feed_forward_kernel(n, live, *refs):
    xs, cots = refs[:n], refs[n : 2 * n]
    mod_ref, up_ref, down_ref, act_ref, gu_ref, gm_ref, send_ref, keep_ref = refs[2 * n :]
    s = pl.program_id(0)
    block = (s + n // 2) % n
    x, cot = pick(block, xs), pick(block, cots)
    w_up = up_ref[...]
    gate_up = dot(x, w_up)
    half = gate_up.shape[1] // 2
    gate, up = gate_up[:, :half], gate_up[:, half:]
    sig = 1.0 / (1.0 + jnp.exp(-gate))
    silu = gate * sig
    act_ref[...] = (silu * up).astype(low)
    grad = (mod_ref[5:6, :] * live[0].astype(wide) * cot.astype(wide)).astype(low)
    gm_ref[...] = grad
    grad_act = dot_t(grad, down_ref[...])
    gu_ref[:, :half] = (grad_act * up * sig * (1.0 + gate * (1.0 - sig))).astype(low)
    gu_ref[:, half:] = (grad_act * silu).astype(low)
    grad_in = dot_t(gu_ref[...], w_up)

    @pl.when(s < n // 2)
    def _():
        send_ref[...] = grad_in.astype(low)

    @pl.when(s >= n // 2)
    def _():
        keep_ref[...] = grad_in


def feed_forward(xs, cots, modulation, w_up, w_down, live):
    n = len(xs)
    rows, width = xs[0].shape
    hidden = w_down.shape[0]
    half = n // 2

    def by_block(columns):
        return pl.BlockSpec((rows, columns), lambda s, o=None: ((s + half) % n, 0))

    return kernel(
        functools.partial(feed_forward_kernel, n),
        "feed_forward",
        live,
        [*xs, *cots, modulation, w_up, w_down],
        (n,),
        [whole(x.shape) for x in (*xs, *cots, modulation, w_up, w_down)],
        [
            by_block(hidden),
            by_block(2 * hidden),
            by_block(width),
            pl.BlockSpec((rows, width), lambda s, o=None: (jnp.minimum(s, half - 1), 0)),
            pl.BlockSpec((rows, width), lambda s, o=None: (jnp.maximum(s - half, 0), 0)),
        ],
        [
            shape_of((n * rows, hidden), low),
            shape_of((n * rows, 2 * hidden), low),
            shape_of((n * rows, width), low),
            shape_of((half * rows, width), low),
            shape_of((half * rows, width), wide),
        ],
        megabytes=48,
    )


def halves_of(acc_ref, at):
    rows = acc_ref.shape[0] // 2
    return [acc_ref[pl.ds(pl.multiple_of(i * rows, 8), rows), :] for i in (1 - at[0], at[0])]


def turned(xs, xt_ref):
    @pl.when(pl.program_id(0) == 0)
    def _():
        rows = xs[0].shape[0]
        for j, x in enumerate(xs):
            xt_ref[:, j * rows : (j + 1) * rows] = x[...].T


def turn_kernel(at, *refs):
    n = len(refs) // 2
    for a, b in zip(refs[:n], refs[n:]):
        b[...] = a[...].T


def turn_blocks(arrays, rows):
    tokens = arrays[0].shape[0]
    return kernel(
        turn_kernel,
        "turn_blocks",
        None,
        arrays,
        (tokens // rows,),
        [pl.BlockSpec((rows, a.shape[1]), lambda s, o=None: (s, 0)) for a in arrays],
        [pl.BlockSpec((a.shape[1], rows), lambda s, o=None: (0, s)) for a in arrays],
        [shape_of((a.shape[1], tokens), a.dtype) for a in arrays],
    )


def grad_part_kernel(n, at, *refs):
    xs, (b_ref, theirs, mine, xt_ref, acc_ref) = refs[:n], refs[n:]
    turned(xs, xt_ref)
    acc_ref[...] = dot(xt_ref[...], b_ref[...])
    for ref, value in zip((theirs, mine), halves_of(acc_ref, at)):
        ref[...] = value.astype(low)


def grad_part(xs, b, at, first, columns, chunk):
    tokens, width = len(xs) * xs[0].shape[0], xs[0].shape[1]
    out = pl.BlockSpec((width // 2, chunk), lambda s, o=None: (0, s))
    return kernel(
        functools.partial(grad_part_kernel, len(xs)),
        "grad_part",
        at,
        [*xs, b],
        (columns // chunk,),
        [whole(x.shape) for x in xs] + [pl.BlockSpec((tokens, chunk), lambda s, o=None: (0, first // chunk + s))],
        [out, out],
        [shape_of((width // 2, columns), low)] * 2,
        scratch=[pltpu.VMEM((width, tokens), low), pltpu.VMEM((width, chunk), wide)],
        megabytes=36,
    )


def grad_last_kernel(n, head_dim, cut, columns, at, *refs):
    xt_ref, mt_ref = refs[:2]
    parts, gbs = refs[2 : 2 + n], refs[2 + n : 2 + 2 * n]
    outs = refs[2 + 2 * n : 6 + 2 * n]
    acc_ref, out_ref = refs[6 + 2 * n :]
    padded = outs[0].shape[1]
    wide_columns = parts[0].shape[1]
    lane = lax.broadcasted_iota(jnp.int32, (wide_columns, padded), 0)
    target = (lane // LANES) * head_dim + lane % LANES
    column = lax.broadcasted_iota(jnp.int32, (wide_columns, padded), 1)
    inside = lane % LANES < head_dim
    per = columns // n
    narrow = sum(
        dot(part[...], jnp.where(inside & (column == target + p * per), 1.0, 0.0).astype(low))
        for p, part in enumerate(parts)
    ).astype(low)
    acc_ref[...] = dot(xt_ref[...], narrow)
    for half, value in enumerate(halves_of(acc_ref, at)):
        outs[half][...] = value[:cut].astype(low)
        outs[2 + half][: value.shape[0] - cut] = value[cut:].astype(low)

    rows = gbs[0].shape[0]
    out_ref[...] = sum(dot(mt_ref[:, j * rows : (j + 1) * rows], gbs[j][...]) for j in range(n))
    for half, value in enumerate(halves_of(out_ref, at)):
        ref = outs[2 + half]
        heads = [value[h * LANES : h * LANES + head_dim] for h in range(value.shape[0] // LANES)]
        value = jnp.concatenate(heads, axis=0)
        length, third = value.shape[0], value.shape[0] // 3
        start = xt_ref.shape[0] // 2 - cut
        spare = jnp.zeros((third, padded - columns), wide)
        ref[start : start + length] = jnp.where(
            lax.broadcasted_iota(jnp.int32, (length, padded), 1) < columns, value[:, :padded], 0.0
        ).astype(low)
        rest = [value[k * third : (k + 1) * third, columns:] for k in range(3)]
        ref[start + length :] = jnp.concatenate(rest + [spare], axis=1).astype(low)


def grad_last(xt, joined, mixed_t, gbs, at, head_dim, cut):
    n = joined.shape[1] // (3 * LANES)
    assert n == len(gbs)
    tokens, part = joined.shape[0], 3 * LANES
    width = xt.shape[0]
    columns = n * 3 * head_dim
    length = mixed_t.shape[0] // LANES * head_dim // 2
    assert gbs[0].shape[1] - columns == columns // 3 and length % 3 == 0
    padded = -(-columns // LANES) * LANES
    shapes = [(cut, padded), (width // 2 - cut + length + length // 3, padded)]
    return kernel(
        functools.partial(grad_last_kernel, n, head_dim, cut, columns),
        "grad_last",
        at,
        [xt, mixed_t, *[joined] * n, *gbs],
        (1,),
        [whole(xt.shape), whole(mixed_t.shape)]
        + [pl.BlockSpec((tokens, part), lambda s, o=None, h=h: (0, h)) for h in range(n)]
        + [whole(b.shape) for b in gbs],
        [whole(a) for a in shapes for _ in range(2)],
        [shape_of(a, low) for a in shapes for _ in range(2)],
        scratch=[
            pltpu.VMEM((width, padded), wide),
            pltpu.VMEM((mixed_t.shape[0], gbs[0].shape[1]), wide),
        ],
        megabytes=50,
    )


def add_halves_kernel(at, a_ref, b_ref, send_ref, keep_ref):
    value = a_ref[...].astype(wide) + b_ref[...].astype(wide)

    @pl.when(pl.program_id(0) == 0)
    def _():
        send_ref[...] = value.astype(low)

    @pl.when(pl.program_id(0) == 1)
    def _():
        keep_ref[...] = value


def add_halves(a, b, at):
    rows, columns = a.shape[0] // 2, a.shape[1]
    block = pl.BlockSpec((rows, columns), lambda s, o=None: (o[s], 0))
    return kernel(
        add_halves_kernel,
        "add_halves",
        at,
        [a, b],
        (2,),
        [block, block],
        [whole((rows, columns))] * 2,
        [shape_of((rows, columns), low), shape_of((rows, columns), wide)],
    )


def join_halves_kernel(at, a_ref, b_ref, o_ref):
    o_ref[...] = jnp.where(pl.program_id(0) == at[1], a_ref[...], b_ref[...])


def join_halves(mine, other, at):
    rows, columns = mine.shape
    return kernel(
        join_halves_kernel,
        "join_halves",
        at,
        [mine, other],
        (2,),
        [whole(mine.shape)] * 2,
        pl.BlockSpec((rows, columns), lambda s, o=None: (s, 0)),
        shape_of((2 * rows, columns), low),
    )


def place_columns(srcs, at, start, step, parts, up_ref):
    width = srcs[0].shape[1]
    piece, count = width // parts, len(srcs)

    def put(d, block):
        for p in range(parts):
            end = (p * count + d) * piece
            up_ref[:, end : end + piece] = block[:, p * piece : (p + 1) * piece]

    for j in range(count):
        block = srcs[j][pl.ds(start, step), :].astype(wide)
        for d in range(count):
            pl.when(at[j] == d)(functools.partial(put, d, block))


def place_first_kernel(parts, at, *refs):
    srcs, up_ref = refs[:-1], refs[-1]
    step = up_ref.shape[0]
    place_columns(srcs, at, pl.multiple_of(pl.program_id(0) * step, 16), step, parts, up_ref)


def place_first(blocks, at, parts):
    count = len(blocks)
    rows, width = blocks[0].shape
    step = 144
    return kernel(
        functools.partial(place_first_kernel, parts),
        "place_first",
        at,
        blocks,
        (rows // step,),
        [whole(b.shape) for b in blocks],
        pl.BlockSpec((step, width * count), lambda s, o=None: (s, 0)),
        shape_of((rows, 2 * width * count), wide),
    )


def place_second_kernel(count, parts, at, *refs):
    srcs, up_ref = refs[:count], refs[-1]
    step = up_ref.shape[0]
    place_columns(srcs, at, pl.multiple_of(pl.program_id(0) * step, 16), step, parts, up_ref)


def place_second(blocks, first, at, parts):
    count = len(blocks)
    width = blocks[0].shape[1]
    rows = first.shape[0]
    step = 144
    return pl.pallas_call(
        functools.partial(place_second_kernel, count, parts),
        grid_spec=pltpu.PrefetchScalarGridSpec(
            num_scalar_prefetch=1,
            grid=(rows // step,),
            in_specs=[whole(b.shape) for b in blocks] + [pl.BlockSpec(memory_space=pl.ANY)],
            out_specs=pl.BlockSpec((step, width * count), lambda s, o: (s, 1)),
        ),
        out_shape=shape_of(first.shape, wide),
        input_output_aliases={count + 1: 0},
        compiler_params=pltpu.CompilerParams(vmem_limit_bytes=32 * 1024 * 1024),
        cost_estimate=pl.CostEstimate(flops=1, bytes_accessed=1, transcendentals=0),
        name="place_second",
    )(at, *blocks, first)


def place_rows_kernel(at, *refs):
    srcs, o_ref = refs[:-1], refs[-1]
    rows = srcs[0].shape[0]
    for j, ref in enumerate(srcs):
        o_ref[pl.ds(pl.multiple_of(at[j] * rows, 8), rows), :] = ref[...].astype(wide)


def place_rows(blocks, at, chunk):
    rows, width = blocks[0].shape
    n = len(blocks)
    return kernel(
        place_rows_kernel,
        "place_rows",
        at,
        blocks,
        (width // chunk,),
        [pl.BlockSpec((rows, chunk), lambda s, o=None: (0, s))] * n,
        pl.BlockSpec((n * rows, chunk), lambda s, o=None: (0, s)),
        shape_of((n * rows, width), wide),
    )


def place_rows_of(srcs, at, halves, head_dim, columns, o_ref):
    count = len(srcs)
    heads = columns // (3 * head_dim) // halves

    def put(d, block):
        for t in range(3):
            for h in range(halves):
                for u in range(heads):
                    end = ((t * halves + h) * count + d) * heads + u
                    start = (h * heads + u) * 3 + t
                    o_ref[:, end * head_dim : (end + 1) * head_dim] = block[
                        :, start * head_dim : (start + 1) * head_dim
                    ]

    for j in range(count):
        block = srcs[j][...].astype(wide)
        for d in range(count):
            pl.when(at[j] == d)(functools.partial(put, d, block))


def place_top_kernel(halves, head_dim, columns, at, *refs):
    place_rows_of(refs[:-1], at, halves, head_dim, columns, refs[-1])


def place_top(blocks, at, halves, head_dim, rows, columns):
    count = len(blocks)
    cut, width = blocks[0].shape
    step = 96
    return kernel(
        functools.partial(place_top_kernel, halves, head_dim, columns),
        "place_top",
        at,
        blocks,
        (cut // step,),
        [pl.BlockSpec((step, width), lambda s, o: (s, 0))] * count,
        pl.BlockSpec((step, columns * count), lambda s, o: (s, 0)),
        shape_of((rows, columns * count), wide),
    )


def place_last_kernel(count, halves, head_dim, columns, at, *refs):
    seconds, lasts = refs[:count], refs[count : 2 * count]
    _, o_ref, out_ref = refs[2 * count :]
    place_rows_of(seconds, at, halves, head_dim, columns, o_ref)

    @pl.when(pl.program_id(0) == 0)
    def _():
        length = out_ref.shape[0] // count
        for j in range(count):
            value = lasts[j][...].astype(wide)
            width, side = columns, columns // 3
            at_row = pl.multiple_of(at[j] * length, 8)
            out_ref[pl.ds(at_row, length), :width] = value[:length, :width]
            rest = [value[length:, k * side : (k + 1) * side] for k in range(3)]
            out_ref[pl.ds(at_row, length), width:] = jnp.concatenate(rest, axis=0)


def place_last(blocks, top, at, halves, head_dim, length, columns):
    count = len(blocks)
    step, width = 96, blocks[0].shape[1]
    rows = top.shape[0]
    last = blocks[0].shape[0] // 2
    steps = last // step
    skip = rows // step - steps
    outs = [top.shape, (count * length, columns // 3 * 4)]
    return pl.pallas_call(
        functools.partial(place_last_kernel, count, halves, head_dim, columns),
        grid_spec=pltpu.PrefetchScalarGridSpec(
            num_scalar_prefetch=1,
            grid=(steps,),
            in_specs=[pl.BlockSpec((step, width), lambda s, o: (s, 0))] * count
            + [pl.BlockSpec((last, width), lambda s, o: (1, 0))] * count
            + [pl.BlockSpec(memory_space=pl.ANY)],
            out_specs=[pl.BlockSpec((step, columns * count), lambda s, o: (skip + s, 0)), whole(outs[1])],
        ),
        out_shape=[shape_of(a, wide) for a in outs],
        input_output_aliases={2 * count + 1: 0},
        compiler_params=pltpu.CompilerParams(vmem_limit_bytes=32 * 1024 * 1024),
        cost_estimate=pl.CostEstimate(flops=1, bytes_accessed=1, transcendentals=0),
        name="place_last",
    )(at, *blocks, *blocks, top)


def program(sizes, tokens, condition, valid, positions, w_qkv, w_out, w_up, w_down, w_ada, qk_gain, cotangent):
    n_img, n_row, n_col = sizes
    images, tile_rows, tile_cols, width = tokens.shape
    assert images == n_row == 4 and n_col == 4
    tile = tile_rows * tile_cols
    own = n_row * tile
    head_dim = qk_gain.shape[1]
    my_heads = width // head_dim // n_col
    me_img, me_row, me_col = lax.axis_index("img"), lax.axis_index("row"), lax.axis_index("col")
    order_col, order_row = block_order(n_col), block_order(n_row)
    halves = 2
    paired = n_img == 2

    def integers(*values):
        return jnp.stack(values).astype(jnp.int32)

    steps = lax.dynamic_index_in_dim(positions, me_row, 1, keepdims=False)
    bit = me_row % 2
    at_col = integers(me_col)
    at_img, at_columns, at_halves, live, at_tables, source, at_image = lax.optimization_barrier(
        (
            integers(me_img if paired else jnp.zeros_like(me_img)),
            integers(*[me_col ^ j for j in order_col]),
            integers(1 - bit, bit),
            lax.dynamic_slice_in_dim(valid, me_row, 1, axis=0),
            jnp.concatenate(
                [
                    integers(steps[0, 1, 0] - steps[0, 0, 0], steps[1, 0, 1] - steps[1, 0, 0]),
                    jnp.arange(n_row, dtype=jnp.int32),
                    integers(*[me_col ^ j for j in order_col]),
                ]
            ),
            integers(*[(me_row ^ k) * n_col + (me_col ^ j) for j in order_col for k in order_row]),
            integers(*[me_row ^ k for k in order_row]),
        )
    )

    def x_swap(v):
        return swap(v, "img", 2, 1)

    def y_swap(v):
        return swap(v, "col", n_col, 2)

    def core_swap(v):
        return swap(v, "col", n_col, 1)

    def z_swaps(parts):
        return [parts[0]] + [swap(p, "row", n_row, k) for p, k in zip(parts[1:], order_row[1:])]

    def over_rows(v):
        return lax.all_to_all(v, "row", split_axis=0, concat_axis=0, tiled=True)

    if paired:
        part_qkv = cut_qkv(w_qkv, at_col, 3 * halves, n_col)
        other_qkv = x_swap(part_qkv)
    else:
        full = cut_qkv(lax.all_gather(w_qkv, "img", axis=0, tiled=True), at_col, 3 * halves, n_col)
        part_qkv, other_qkv = full[: width // 2], full[width // 2 :]
    tok_row = over_rows(after(tokens, part_qkv).reshape(images * tile, width))
    cond = condition.astype(wide)
    silu_cond = jax.nn.silu(cond).astype(low)
    mod_columns = jnp.dot(after(silu_cond, part_qkv), w_ada, preferred_element_type=wide)
    mod_span = mod_columns.shape[1]
    mod_z = z_swaps([lax.dynamic_slice_in_dim(mod_columns, me_row ^ k, 1, axis=0) for k in order_row])
    cos_all, sin_a, sin_b = tables(after(at_tables, mod_columns), n_row, n_col, tile, tile_cols, head_dim)
    gain = after(jnp.pad(qk_gain, ((0, 0), (0, LANES - head_dim))), at_col)
    t = cos_all
    if paired:
        part_up, part_out, part_down = cut_rest(w_up, w_out, w_down, after(at_col, mod_columns), 2 * halves, n_col)
        other_out, other_down = x_swap(part_out), x_swap(part_down)
        other_silu = x_swap(after(silu_cond, mod_columns))
        t = part_down
    mod_row = cat(*[after(m, cos_all, t) for m in mod_z])
    mod_y, mod_core = y_swap(mod_row), core_swap(mod_row)
    t = mod_row
    mod_y, mod_core = lax.optimization_barrier((mod_y, mod_core, t))[:2]
    mod_last = core_swap(mod_y)
    tok_row = after(tok_row, mod_y)
    tok_y, tok_core = y_swap(tok_row), core_swap(tok_row)
    cot_row = over_rows(after(cotangent, tok_row).reshape(images * tile, width))
    modulation = place_modulation([mod_row, mod_y, mod_core, after(mod_last, tok_row)], source).reshape(6, width)
    tok_core = after(tok_core, modulation)
    if paired:
        other_qkv = after(other_qkv, tok_core)
    w_qkv_mine = widen(part_qkv, other_qkv, at_img, head_dim)
    tok_y = after(tok_y, w_qkv_mine)
    if paired:
        other_out, other_down, tok_y, other_silu = lax.optimization_barrier((other_out, other_down, tok_y, other_silu))
        other_up = x_swap(after(part_up, other_down))
    tok_last = core_swap(tok_y)
    toks = [tok_row, tok_y, tok_core, tok_last]

    attn_in, joined = project_qkv(toks, modulation, w_qkv_mine)
    cot_row = after(cot_row, joined)
    cot_y, cot_core = y_swap(cot_row), core_swap(cot_row)
    mixed, aug = attn_fwd(after(joined, cot_row), cos_all, sin_a, sin_b, gain, head_dim)
    if paired:
        w_out_mine = widen_rows(part_out, after(other_out, joined), at_img, head_dim)
    else:

        def cut_rows(w):
            full = lax.all_gather(w, "img", axis=0, tiled=True)
            length = full.shape[0] // (halves * n_col)
            return [
                lax.dynamic_slice_in_dim(full, (h * n_col + me_col) * length, length, axis=0) for h in range(halves)
            ]

        w_out_mine = widen_rows(*cut_rows(w_out), at_img, head_dim)
        w_down_mine = cat(*cut_rows(w_down))
        full_up = lax.all_gather(w_up, "img", axis=0, tiled=True)
        piece = full_up.shape[1] // (2 * halves * n_col)
        w_up_mine = jnp.concatenate(
            [
                lax.dynamic_slice_in_dim(full_up, (p * n_col + me_col) * piece, piece, axis=1)
                for p in range(2 * halves)
            ],
            axis=1,
        )
    cot_y, cot_core, mixed = lax.optimization_barrier((cot_y, cot_core, mixed))
    if paired:
        mixed, other_up = lax.optimization_barrier((mixed, other_up))
    sent, keep = project(mixed, w_out_mine, own)
    got = core_swap(sent)
    cot_last = core_swap(after(cot_y, sent))
    got = after(got, keep)
    sent = add_second(keep, got)
    got_y = y_swap(sent)
    cots = [cot_row, cot_y, cot_core, after(cot_last, sent)]
    t = cots[3]
    if paired:
        w_up_mine, w_down_mine = join(part_up, after(other_up, t), part_down, after(other_down, t), at_img)
        t = w_up_mine
    attn_t, mixed_t = turn_blocks([after(attn_in, t), mixed], own)
    hidden, branch, mlp_own = middle(keep, got, after(got_y, attn_t), tok_row, modulation, live)
    mlp_y, mlp_core = y_swap(mlp_own), core_swap(mlp_own)
    mlp_y, mlp_core = lax.optimization_barrier((mlp_y, mlp_core))
    xs = [mlp_own, mlp_y, mlp_core, core_swap(mlp_y)]

    act, grad_gu, grad_mlp, sent, keep = feed_forward(xs, cots, modulation, w_up_mine, w_down_mine, live)
    got = core_swap(sent)

    class Piece:
        def __init__(self, theirs, mine):
            self.sent = theirs
            self.value, self.got = mine, x_swap(theirs)

        def z_one(self, *earlier):
            self.sent, self.keep = add_halves(self.value, after(self.got, *earlier), at_halves)
            self.got = swap(self.sent, "row", n_row, 1)
            return self.sent

        def z_two(self, *earlier):
            self.sent = (self.keep + after(self.got, *earlier).astype(wide)).astype(low)
            self.got = swap(self.sent, "row", n_row, 2)
            return self.sent

        def z_three(self, *earlier):
            other = after(self.got, *earlier)
            self.keep = (self.sent.astype(wide) + other.astype(wide)).astype(low)
            self.got = swap(self.keep, "row", n_row, 1)
            return self.keep

        def y(self, *earlier):
            self.value = join_halves(self.keep, after(self.got, *earlier), at_halves)
            self.got = y_swap(self.value)
            return self.value

        def rows_in(self, *earlier):
            other = after(self.got, *earlier)
            self.sent = (self.value.astype(wide) + other.astype(wide)).astype(low)
            self.got = over_rows(self.sent)
            return self.sent

        def rows_out(self, *earlier):
            parts = after(self.got, *earlier).reshape(n_row, -1, self.got.shape[1])
            shard = jnp.sum(parts.astype(wide), axis=0).astype(low)
            self.sent = cat(*[shard] * n_row)
            self.got = over_rows(self.sent)
            return self.sent

        def y_rows(self, *earlier):
            self.value = after(self.got, *earlier)
            self.got, self.core = y_swap(self.value), core_swap(self.value)
            return self.value

        def end(self, *earlier):
            self.got, self.value = lax.optimization_barrier((self.got, self.value) + earlier)[:2]
            self.core, self.last = core_swap(self.value), core_swap(self.got)
            return self.got

        def blocks(self, *earlier):
            return [self.value, self.got, after(self.core, *earlier), after(self.last, *earlier)]

    got = after(got, keep)
    sent = add_second(keep, got)
    got_y = y_swap(sent)
    t = sent
    if paired:
        d = Piece(*grad_part([after(act, t)], grad_mlp, at_img, 0, width, 384))
        half_up = grad_gu.shape[1] // 2
        u_one = Piece(*grad_part(xs, after(grad_gu, d.sent), at_img, 0, half_up, 384))
        u_two = Piece(*grad_part(xs, after(grad_gu, u_one.sent), at_img, half_up, half_up, 384))
        t = u_two.sent
    grad_hidden, gb_own, sums_two = middle_back(
        keep, got, after(got_y, t), hidden, branch, cot_row, modulation, live
    )
    gb_y, gb_core = y_swap(gb_own), core_swap(gb_own)
    mlp_sent, mlp_keep = project(after(act, gb_own), w_down_mine, own)
    mlp_got = core_swap(mlp_sent)
    t = mlp_keep
    if paired:
        t = d.z_one(t)
    gb_y, gb_core = lax.optimization_barrier((gb_y, gb_core, t))[:2]
    gb_last = core_swap(gb_y)
    mlp_got = after(mlp_got, gb_y)
    mlp_next = add_second(mlp_keep, mlp_got)
    mlp_y = y_swap(mlp_next)
    gbs = [gb_own, gb_y, gb_core, after(gb_last, mlp_next)]
    joined_back, g_gain = attn_bwd(
        gbs, joined, aug, mixed, w_out_mine, cos_all, sin_a, sin_b, gain, head_dim, 0, my_heads
    )
    t = joined_back
    if paired:
        t = d.z_two(t)
        t = u_one.z_one(t)
    sent, keep = project(after(joined_back, t), w_qkv_mine, own, dot_t)
    got = core_swap(sent)
    t = sent
    if paired:
        rows = width // 2
        length = my_heads * head_dim // halves
        cut = (rows + length + length // 3) // 2
        g = grad_last(attn_t, after(joined_back, t), mixed_t, gbs, at_img, head_dim, cut)
        q_one, q_two = Piece(g[0], g[1]), Piece(g[2], g[3])
        t = g[0]
    got = after(got, t)
    sent = add_second(keep, got)
    got_y = y_swap(sent)
    t = sent
    if paired:
        t = u_two.z_one(t)
        t = d.z_three(t)
    out_own, sums_out = result(mlp_keep, mlp_got, after(mlp_y, t), hidden, cot_row, modulation, live)
    output = over_rows(out_own)
    t = out_own
    if paired:
        t = u_one.z_two(t)
    grad_own, sums_last = last_back(keep, got, after(got_y, t), tok_row, grad_hidden, modulation, live)
    vector = (sums_two + sums_last + sums_out)[:6]
    got = core_swap(vector)
    t = vector
    if paired:
        t = q_one.z_one(t)
        t = q_two.z_one(t)
    vector = vector + after(got, t)
    got = y_swap(vector)
    t = vector
    if paired:
        t = d.y(t)
        t = u_two.z_two(t)
        t = u_one.z_three(t)
        t = d.end(t)
    grad_mod = (vector + after(got, t)).astype(low)
    blocks = grad_mod.reshape(n_row, n_col, mod_span)
    mine = lax.dynamic_slice_in_dim(blocks, at_col[0], 1, axis=1)[:, 0]
    share_z = z_swaps([lax.dynamic_slice_in_dim(mine, me_row ^ k, 1, axis=0) for k in order_row])
    t = mine
    if paired:
        t = u_one.y(t)
        t = q_one.z_two(t)
    output = copied(after(output, t))
    t = output
    if paired:
        sum_down = place_rows(d.blocks(t), at_columns, 384)
        t = u_two.z_three(sum_down)
        t = q_two.z_two(t)
    share_rel = cat(*[after(v, t) for v in share_z])
    pick_image = at_image[None, :] == jnp.arange(images)[:, None]
    share = jnp.sum(jnp.where(pick_image[:, :, None], share_rel.astype(wide)[None], 0.0), axis=1).astype(low)
    back = lax.dot_general(share, w_ada, (((1,), (1,)), ((), ())), preferred_element_type=wide)
    flat = jnp.concatenate([back.reshape(-1), g_gain[:, :head_dim].reshape(-1)]).reshape(1, -1)
    got = swap(flat, "row", n_row, 1)
    t = flat
    if paired:
        other_share = x_swap(share)
        t = u_one.end(t)
        sum_up = place_first(u_one.blocks(t), at_columns, halves)
        t = u_two.y(sum_up)
        t = q_one.z_three(t)
    flat = flat + after(got, t)
    got = swap(flat, "row", n_row, 2)
    t = flat
    if paired:
        t = q_two.z_three(t)
    grad_tokens = over_rows(after(grad_own, t))

    def outer_product(a, b):
        return lax.dot_general(a, b, (((0,), (0,)), ((), ())), preferred_element_type=wide)

    if paired:
        grad_ada = outer_product(silu_cond, share) + outer_product(other_silu, after(other_share, t))
        t = grad_ada
    else:
        grad_ada = outer_product(
            lax.all_gather(silu_cond, "img", axis=0, tiled=True), lax.all_gather(share, "img", axis=0, tiled=True)
        )
    flat = flat + after(got, t)
    got = core_swap(flat)
    t = flat
    if paired:
        t = q_one.y(t)
        t = u_two.end(t)
    flat = flat + after(got, t)
    got = y_swap(flat)
    t = flat
    output = output.reshape(tokens.shape)
    if paired:
        t = q_two.y(t)
        sum_up = place_second(u_two.blocks(t), sum_up, at_columns, halves)
        t = sum_up
    flat = (flat + after(got, t))[0]
    grad_silu = flat[: images * width].reshape(images, width)
    gains = flat[images * width :].reshape(2, head_dim)
    s = 1.0 / (1.0 + jnp.exp(-cond))
    grad_condition = grad_silu * (s * (1.0 + cond * (1.0 - s)))
    if paired:
        gains_other = x_swap(gains)
        t = q_one.end(grad_condition)
        gains = gains + after(gains_other, t)
        columns = 3 * my_heads * head_dim
        top = place_top(q_one.blocks(gains), at_columns, halves, head_dim, rows, columns)
        grad_tokens = after(grad_tokens, top).astype(wide).reshape(tokens.shape)
        t = q_two.end(grad_tokens)
        sum_qkv, sum_out = place_last(q_two.blocks(t), top, at_columns, halves, head_dim, length, columns)
    else:
        gains = lax.psum(gains, "img")
        grad_tokens = grad_tokens.astype(wide).reshape(tokens.shape)

        def weight_grad(a, b):
            return lax.dot_general(a, b, (((0,), (0,)), ((), ())), preferred_element_type=wide).astype(low)

        def reduce_columns(partial, parts):
            summed = lax.psum_scatter(lax.psum(partial, "row"), "img", scatter_dimension=0, tiled=True)
            wholes = lax.all_gather(summed, "col", axis=0)
            rows = wholes.shape[1]
            wholes = wholes.reshape(n_col, rows, parts, -1)
            return jnp.transpose(wholes, (1, 2, 0, 3)).reshape(rows, -1).astype(wide)

        def reduce_rows(partial):
            wholes = lax.all_gather(lax.psum(partial, "row"), "col", axis=0)
            columns = wholes.shape[2]
            wholes = jnp.transpose(wholes.reshape(n_col, halves, -1, columns), (1, 0, 2, 3)).reshape(-1, columns)
            return lax.psum_scatter(wholes, "img", scatter_dimension=0, tiled=True).astype(wide)

        g_qkv = weight_grad(attn_in, joined_back).reshape(width, my_heads, 3, LANES)[..., :head_dim]
        g_qkv = jnp.swapaxes(g_qkv, 1, 2).reshape(width, -1)
        g_out = weight_grad(mixed, cat(*gbs)).reshape(my_heads, LANES, width)[:, :head_dim].reshape(-1, width)
        sum_up = reduce_columns(weight_grad(cat(*xs), grad_gu), 2 * halves)
        sum_down = reduce_rows(weight_grad(act, grad_mlp))
        sum_out = reduce_rows(g_out)
        sum_qkv = reduce_columns(g_qkv, 3 * halves)
    return output, grad_tokens, grad_condition, sum_qkv, sum_out, sum_up, sum_down, grad_ada, gains


def solution(mesh):
    sizes = tuple(mesh.shape[name] for name in ("img", "row", "col"))
    placed = (
        P("img", "row", "col", None),
        P("img", None),
        P("img"),
        P(None, "img", "row", "col"),
        P("img", None),
        P("img", None),
        P("img", None),
        P("img", None),
        P(None, ("row", "col")),
        P(),
        P("img", "row", "col", None),
    )
    return jax.shard_map(
        functools.partial(program, sizes),
        mesh=mesh,
        in_specs=placed,
        out_specs=(
            P("img", "row", "col", None),
            P("img", "row", "col", None),
            P("img", None),
            P("img", None),
            P("img", None),
            P("img", None),
            P("img", None),
            P(None, ("row", "col")),
            P(),
        ),
        check_vma=False,
    )
```

```python
import functools
import math

import jax
import jax.numpy as jnp
from jax import lax
from jax.experimental import pallas as pl
from jax.experimental.pallas import tpu as pltpu
from jax.sharding import PartitionSpec as P

LANES = 128
epsilon = 1e-06
low, wide = jnp.bfloat16, jnp.float32


def bits_of(size):
    return [1 << b for b in reversed(range(size.bit_length() - 1))]


def block_order(size):
    order = [0]
    for bit in bits_of(size):
        order = order + [o ^ bit for o in order]
    return order


def swap(value, axis, size, bit):
    return lax.ppermute(value, axis, [(a, a ^ bit) for a in range(size)])


def after(value, *earlier):
    return lax.optimization_barrier((value,) + earlier)[0]


def cat(*parts):
    return jnp.concatenate(parts, axis=0)


def dot(a, b):
    return jnp.dot(a, b, preferred_element_type=wide)


def dot_t(a, b):
    return lax.dot_general(a, b, (((1,), (1,)), ((), ())), preferred_element_type=wide)


def whole(shape):
    return pl.BlockSpec(shape, lambda *_: (0,) * len(shape))


def shape_of(shape, dtype):
    return jax.ShapeDtypeStruct(shape, dtype)


def kernel(body, name, scalars, args, grid, in_specs, out_specs, out_shape, scratch=(), megabytes=24):
    none = scalars is None
    return pl.pallas_call(
        functools.partial(body, None) if none else body,
        grid_spec=pltpu.PrefetchScalarGridSpec(
            num_scalar_prefetch=0 if none else 1, grid=grid, in_specs=in_specs, out_specs=out_specs, scratch_shapes=scratch
        ),
        out_shape=out_shape,
        compiler_params=pltpu.CompilerParams(vmem_limit_bytes=megabytes * 1024 * 1024),
        cost_estimate=pl.CostEstimate(flops=1, bytes_accessed=1, transcendentals=0),
        name=name,
    )(*([] if none else [scalars]), *args)


def pick(step, refs):
    value = refs[0][...]
    for n in range(1, len(refs)):
        value = jnp.where(step == n, refs[n][...], value)
    return value


def cut_qkv_kernel(parts, count, at, w_ref, o_ref):
    piece = o_ref.shape[1] // parts
    for c in range(count):

        @pl.when(at[0] == c)
        def _():
            for p in range(parts):
                start = (p * count + c) * piece
                o_ref[:, p * piece : (p + 1) * piece] = w_ref[:, start : start + piece]


def cut_qkv(w, at, parts, count):
    rows, width = w.shape
    step = 144
    return kernel(
        functools.partial(cut_qkv_kernel, parts, count),
        "cut_qkv",
        at,
        [w],
        (rows // step,),
        [pl.BlockSpec((step, width), lambda s, o=None: (s, 0))],
        pl.BlockSpec((step, width // count), lambda s, o=None: (s, 0)),
        shape_of((rows, width // count), w.dtype),
    )


def copy_kernel(at, *refs):
    n = len(refs) // 2
    for a, b in zip(refs[:n], refs[n:]):
        b[...] = a[...]


def cut_rest(w_up, w_out, w_down, at, parts, count):
    rows, width = w_up.shape
    piece = width // (parts * count)
    shapes = [(w.shape[0] // count, w.shape[1]) for w in (w_out, w_down)]
    return kernel(
        copy_kernel,
        "cut_rest",
        at,
        [w_up, w_out, w_down],
        (parts,),
        [pl.BlockSpec((rows, piece), lambda p, o=None: (0, p * count + o[0]))]
        + [pl.BlockSpec(s, lambda p, o=None: (o[0], 0)) for s in shapes],
        [pl.BlockSpec((rows, piece), lambda p, o=None: (0, p))] + [whole(s) for s in shapes],
        [shape_of((rows, piece * parts), w_up.dtype)] + [shape_of(s, w_up.dtype) for s in shapes],
    )


def widen_kernel(head_dim, heads, at, mine_ref, other_ref, o_ref):
    src = jnp.where(at[0] == pl.program_id(0), mine_ref[...], other_ref[...])
    none = jnp.zeros((src.shape[0], LANES - head_dim), src.dtype)
    for t in range(3):
        for n in range(heads):
            start, end = (t * heads + n) * head_dim, (n * 3 + t) * LANES
            o_ref[:, end : end + LANES] = jnp.concatenate([src[:, start : start + head_dim], none], axis=1)


def widen(mine, other, at, head_dim):
    rows, width = mine.shape
    out = width // head_dim * LANES
    return kernel(
        functools.partial(widen_kernel, head_dim, width // (3 * head_dim)),
        "widen",
        at,
        [mine, other],
        (2,),
        [whole((rows, width))] * 2,
        pl.BlockSpec((rows, out), lambda h, o=None: (h, 0)),
        shape_of((2 * rows, out), mine.dtype),
    )


def widen_rows_kernel(head_dim, at, mine_ref, other_ref, o_ref):
    src = jnp.where(at[0] == pl.program_id(0), mine_ref[...], other_ref[...]).astype(wide)
    none = jnp.zeros((LANES - head_dim, src.shape[1]), wide)
    for n in range(src.shape[0] // head_dim):
        part = jnp.concatenate([src[n * head_dim : (n + 1) * head_dim], none], axis=0)
        o_ref[n * LANES : (n + 1) * LANES] = part.astype(low)


def widen_rows(mine, other, at, head_dim):
    rows, width = mine.shape
    out = rows // head_dim * LANES
    return kernel(
        functools.partial(widen_rows_kernel, head_dim),
        "widen_rows",
        at,
        [mine, other],
        (2,),
        [whole((rows, width))] * 2,
        pl.BlockSpec((out, width), lambda h, o=None: (h, 0)),
        shape_of((2 * out, width), mine.dtype),
    )


def join_kernel(at, a_ref, b_ref, c_ref, d_ref, x_ref, y_ref):
    mine = at[0] == pl.program_id(0)
    x_ref[...] = jnp.where(mine, a_ref[...], b_ref[...])
    y_ref[...] = jnp.where(mine, c_ref[...], d_ref[...])


def join(mine_up, other_up, mine_down, other_down, at):
    specs = [whole(a.shape) for a in (mine_up, other_up, mine_down, other_down)]
    return kernel(
        join_kernel,
        "join",
        at,
        [mine_up, other_up, mine_down, other_down],
        (2,),
        specs,
        [pl.BlockSpec(a.shape, lambda h, o=None: (h, 0)) for a in (mine_up, mine_down)],
        [shape_of((2 * a.shape[0], a.shape[1]), low) for a in (mine_up, mine_down)],
    )


def copied(a):
    return kernel(copy_kernel, "copied", None, [a], (1,), [whole(a.shape)], whole(a.shape), shape_of(a.shape, a.dtype))


def tables_kernel(n_row, tile, tile_cols, head_dim, at, cos_ref, a_ref, b_ref):
    shape = cos_ref.shape
    pairs = head_dim // 4
    pos = lax.broadcasted_iota(jnp.int32, shape, 0)
    lane = lax.broadcasted_iota(jnp.int32, shape, 1)
    block = pos // tile
    row_block, col_block = block % n_row, block // n_row
    row_at = jnp.zeros(shape, jnp.int32)
    for k in range(n_row):
        row_at = jnp.where(row_block == k, at[2 + k], row_at)
    col_at = jnp.zeros(shape, jnp.int32)
    for j in range(shape[0] // (tile * n_row)):
        col_at = jnp.where(col_block == j, at[2 + n_row + j], col_at)
    inside = pos % tile
    row = (row_at * (tile // tile_cols) + inside // tile_cols) * at[0]
    col = (col_at * tile_cols + inside % tile_cols) * at[1]
    half = 2 * pairs
    within = jnp.where(lane < half, lane, lane - half)
    first = within < pairs
    step = jnp.where(first, within, within - pairs).astype(wide)
    frequency = jnp.exp(step * (-math.log(10000.0) / pairs))
    angle = jnp.where(lane < half, row, col).astype(wide) * frequency
    live = lane < head_dim
    cos, sin = jnp.cos(angle), jnp.sin(angle)
    cos_ref[...] = jnp.where(live, cos, 0.0)
    a_ref[...] = jnp.where(live & first, -sin, 0.0)
    b_ref[...] = jnp.where(live & jnp.logical_not(first), sin, 0.0)


def tables(at, n_row, n_col, tile, tile_cols, head_dim):
    shape = (n_row * n_col * tile, LANES)
    return kernel(
        functools.partial(tables_kernel, n_row, tile, tile_cols, head_dim),
        "tables",
        at,
        [],
        (1,),
        [],
        [whole(shape)] * 3,
        [shape_of(shape, wide)] * 3,
    )


def place_modulation_kernel(at, *refs):
    o_ref = refs[-1]
    rows = refs[0].shape[0]
    for j, ref in enumerate(refs[:-1]):
        for k in range(rows):
            o_ref[pl.ds(at[j * rows + k], 1), :] = ref[k : k + 1, :]


def place_modulation(parts, at):
    rows, width = parts[0].shape
    shape = (rows * len(parts), width)
    return kernel(
        place_modulation_kernel,
        "place_modulation",
        at,
        parts,
        (1,),
        [whole(p.shape) for p in parts],
        whole(shape),
        shape_of(shape, wide),
    )


def inverse(v):
    return lax.rsqrt(jnp.mean(v * v, axis=-1, keepdims=True) + epsilon)


def norm_back(v, inv, stretch, g_y):
    normed = v * inv
    g = g_y * (1.0 + stretch)
    g_v = (g - normed * jnp.mean(g * normed, axis=-1, keepdims=True)) * inv
    return g_v, jnp.sum(g_y, axis=0, keepdims=True), jnp.sum(g_y * normed, axis=0, keepdims=True)


def put_rows(ref, **rows):
    ref[...] = jnp.zeros_like(ref)
    for name, row in rows.items():
        n = int(name[1:])
        ref[n : n + 1, :] = row


def turn(x, cos, sin_a, sin_b, shift):
    return x * cos + pltpu.roll(x, LANES - shift, 1) * sin_a + pltpu.roll(x, shift, 1) * sin_b


def project_qkv_kernel(at, *refs):
    toks, (mod_ref, w_ref, in_ref, joined_ref) = refs[:-4], refs[-4:]
    x = pick(pl.program_id(0), toks).astype(wide)
    attn_in = (x * inverse(x) * (1.0 + mod_ref[1:2, :]) + mod_ref[0:1, :]).astype(low)
    in_ref[...] = attn_in
    joined_ref[...] = dot(attn_in, w_ref[...])


def project_qkv(toks, modulation, w):
    rows, width = toks[0].shape
    n, columns = len(toks), w.shape[1]
    return kernel(
        project_qkv_kernel,
        "project_qkv",
        None,
        [*toks, modulation, w],
        (n,),
        [whole(t.shape) for t in toks] + [whole(modulation.shape), whole(w.shape)],
        [pl.BlockSpec((rows, width), lambda s, o=None: (s, 0)), pl.BlockSpec((rows, columns), lambda s, o=None: (s, 0))],
        [shape_of((n * rows, width), low), shape_of((n * rows, columns), wide)],
    )


def attn_fwd_kernel(head_dim, at, x_ref, cos_ref, a_ref, b_ref, gain_ref, o_ref, aug_ref):
    tokens = x_ref.shape[0]
    pairs, scale = head_dim // 4, head_dim**-0.5 * math.log2(math.e)
    cos, sa, sb = cos_ref[...], a_ref[...], b_ref[...]

    def normed(x):
        return x * lax.rsqrt(jnp.sum(x * x, axis=-1, keepdims=True) * (1.0 / head_dim) + epsilon)

    q = turn(normed(x_ref[:, :LANES]) * gain_ref[0:1, :], cos, sa, sb, pairs) * scale
    k = turn(normed(x_ref[:, LANES : 2 * LANES]) * gain_ref[1:2, :], cos, sa, sb, pairs)
    lane = lax.broadcasted_iota(jnp.int32, (tokens, LANES), 1)
    extra = (lane == head_dim) | (lane == head_dim + 1)
    kk = jnp.where(extra, 1.0, k).astype(low)
    vv = jnp.where(extra, -1.0, x_ref[:, 2 * LANES :]).astype(low)
    aug_ref[:, LANES : 2 * LANES] = kk
    aug_ref[:, 2 * LANES :] = vv
    q_low = q.astype(low)
    rows = 256
    for s in range(tokens // rows):
        span = slice(s * rows, (s + 1) * rows)
        out = dot(jnp.exp2(dot_t(q_low[span], kk)).astype(low), vv)
        total = -out[:, head_dim : head_dim + 1]
        lane_s = lane[span]
        o_ref[span, :] = jnp.where(lane_s < head_dim, out * (1.0 / total), 0.0).astype(low)
        lse = -jnp.log2(total)
        high = lse.astype(low).astype(wide)
        aug = jnp.where(lane_s == head_dim, high, jnp.where(lane_s == head_dim + 1, lse - high, q[span]))
        aug_ref[span, :LANES] = aug.astype(low)


def attn_fwd(joined, cos, sa, sb, gain, head_dim):
    tokens, columns = joined.shape
    heads = columns // (3 * LANES)
    block = pl.BlockSpec((tokens, 3 * LANES), lambda h, o=None: (0, h))
    return kernel(
        functools.partial(attn_fwd_kernel, head_dim),
        "attn_fwd",
        None,
        [joined, cos, sa, sb, gain],
        (heads,),
        [block, whole(cos.shape), whole(cos.shape), whole(cos.shape), whole(gain.shape)],
        [pl.BlockSpec((tokens, LANES), lambda h, o=None: (0, h)), block],
        [shape_of((tokens, heads * LANES), low), shape_of((tokens, columns), low)],
        megabytes=24,
    )


def attn_bwd_kernel(head_dim, at, *refs):
    n = len(refs) - 14
    gbs = refs[:n]
    x_ref, aug_ref, o_ref, w_ref, cos_ref, a_ref, b_ref, gain_ref, g_ref, gg_ref = refs[n : n + 10]
    dk_acc, dv_acc, dq_acc, do_acc = refs[n + 10 :]
    tokens = x_ref.shape[0]
    pairs = head_dim // 4
    h = pl.program_id(0)
    rows = tokens // n
    for j in range(n):
        do_acc[j * rows : (j + 1) * rows, :] = dot_t(gbs[j][...], w_ref[...]).astype(low)
    lane = lax.broadcasted_iota(jnp.int32, (tokens, LANES), 1)
    do_f = do_acc[...].astype(wide)
    delta = jnp.sum(do_f * o_ref[...].astype(wide), axis=-1, keepdims=True)
    high = delta.astype(low).astype(wide)
    do_a = jnp.where(lane == head_dim, high, jnp.where(lane == head_dim + 1, delta - high, do_f)).astype(low)
    qa, ka, va = aug_ref[:, :LANES], aug_ref[:, LANES : 2 * LANES], aug_ref[:, 2 * LANES :]
    ka_t = ka.T
    cols = 256
    for s in range(tokens // cols):
        qs = qa[s * cols : (s + 1) * cols]
        ds = do_a[s * cols : (s + 1) * cols]
        p = jnp.exp2(dot_t(ka, qs))
        grad_s = (p * dot_t(va, ds)).astype(low)
        dv, dk = dot(p.astype(low), ds), dot(grad_s, qs)
        if s == 0:
            dv_acc[...] = dv
            dk_acc[...] = dk
        else:
            dv_acc[...] += dv
            dk_acc[...] += dk
        dq_acc[:, s * cols : (s + 1) * cols] = dot(ka_t, grad_s)
    inside = lane < head_dim
    cos, sa, sb = cos_ref[...], a_ref[...], b_ref[...]

    def back(g, x, gain):
        g = jnp.where(inside, g, 0.0)
        g = g * cos - pltpu.roll(g, LANES - pairs, 1) * sa - pltpu.roll(g, pairs, 1) * sb
        inv = lax.rsqrt(jnp.sum(x * x, axis=-1, keepdims=True) * (1.0 / head_dim) + epsilon)
        normed = x * inv
        gain_part = jnp.sum(g * normed, axis=0, keepdims=True)
        g = g * gain
        return (g - normed * (jnp.sum(g * normed, axis=-1, keepdims=True) * (1.0 / head_dim))) * inv, gain_part

    gq, ggq = back(dq_acc[...].T * (head_dim**-0.5), x_ref[:, :LANES], gain_ref[0:1, :])
    gk, ggk = back(dk_acc[...] * math.log(2.0), x_ref[:, LANES : 2 * LANES], gain_ref[1:2, :])
    g_ref[:, :LANES] = gq.astype(low)
    g_ref[:, LANES : 2 * LANES] = gk.astype(low)
    g_ref[:, 2 * LANES :] = jnp.where(inside, dv_acc[...], 0.0).astype(low)
    gg = jnp.concatenate([ggq, ggk], axis=0)

    @pl.when(h == 0)
    def _():
        gg_ref[...] = gg

    @pl.when(h > 0)
    def _():
        gg_ref[...] += gg


def attn_bwd(grads, joined, aug, mixed, w_out, cos, sa, sb, gain, head_dim, first, heads):
    tokens = joined.shape[0]
    block = pl.BlockSpec((tokens, 3 * LANES), lambda h, o=None: (0, first + h))
    return kernel(
        functools.partial(attn_bwd_kernel, head_dim),
        "attn_bwd",
        None,
        [*grads, joined, aug, mixed, w_out, cos, sa, sb, gain],
        (heads,),
        [whole(g.shape) for g in grads]
        + [block, block, pl.BlockSpec((tokens, LANES), lambda h, o=None: (0, first + h))]
        + [pl.BlockSpec((LANES, w_out.shape[1]), lambda h, o=None: (first + h, 0))]
        + [whole(cos.shape), whole(cos.shape), whole(cos.shape), whole(gain.shape)],
        [pl.BlockSpec((tokens, 3 * LANES), lambda h, o=None: (0, h)), whole(gain.shape)],
        [shape_of((tokens, heads * 3 * LANES), low), shape_of(gain.shape, wide)],
        scratch=[
            pltpu.VMEM((tokens, LANES), wide),
            pltpu.VMEM((tokens, LANES), wide),
            pltpu.VMEM((LANES, tokens), wide),
            pltpu.VMEM((tokens, LANES), low),
        ],
        megabytes=24,
    )


def project_kernel(product, at, x_ref, w_ref, send_ref, keep_ref):
    value = product(x_ref[...], w_ref[...])
    half = pl.num_programs(0) // 2

    @pl.when(pl.program_id(0) < half)
    def _():
        send_ref[...] = value.astype(low)

    @pl.when(pl.program_id(0) >= half)
    def _():
        keep_ref[...] = value


def project(x, w, rows, product=dot):
    columns = w.shape[1] if product is dot else w.shape[0]
    count = x.shape[0] // rows
    half = count // 2
    return kernel(
        functools.partial(project_kernel, product),
        "project",
        None,
        [x, w],
        (count,),
        [pl.BlockSpec((rows, x.shape[1]), lambda s, o=None: ((s + half) % count, 0)), whole(w.shape)],
        [
            pl.BlockSpec((rows, columns), lambda s, o=None: (jnp.minimum(s, half - 1), 0)),
            pl.BlockSpec((rows, columns), lambda s, o=None: (jnp.maximum(s - half, 0), 0)),
        ],
        [shape_of((half * rows, columns), low), shape_of((half * rows, columns), wide)],
        megabytes=24,
    )


def add_kernel(at, a_ref, b_ref, o_ref):
    o_ref[...] = (a_ref[...].astype(wide) + b_ref[...].astype(wide)).astype(low)


def add_second(a, b):
    rows, columns = a.shape[0] // 2, a.shape[1]
    return kernel(
        add_kernel,
        "add_second",
        None,
        [a, b],
        (1,),
        [pl.BlockSpec((rows, columns), lambda s, o=None: (1, 0))] * 2,
        whole((rows, columns)),
        shape_of((rows, columns), low),
    )


def middle_kernel(live, keep_ref, core_ref, y_ref, tok_ref, mod_ref, hidden_ref, branch_ref, mlp_ref):
    branch = keep_ref[...] + core_ref[...].astype(wide) + y_ref[...].astype(wide)
    gate = mod_ref[2:3, :] * live[0].astype(wide)
    hidden = tok_ref[...].astype(wide) + gate * branch
    hidden_ref[...] = hidden
    branch_ref[...] = branch
    mlp_ref[...] = (hidden * inverse(hidden) * (1.0 + mod_ref[4:5, :]) + mod_ref[3:4, :]).astype(low)


def middle(keep, core, y, tok, modulation, live):
    shape = y.shape
    first = pl.BlockSpec(shape, lambda s, o=None: (0, 0))
    return kernel(
        middle_kernel,
        "middle",
        live,
        [keep, core, y, tok, modulation],
        (1,),
        [first, first, first, first, whole(modulation.shape)],
        [first] * 3,
        [shape_of(shape, wide), shape_of(shape, wide), shape_of(shape, low)],
    )


def middle_back_kernel(live, keep_ref, core_ref, y_ref, hidden_ref, branch_ref, cot_ref, mod_ref, grad_ref, gb_ref, s_ref):
    g_y = keep_ref[...] + core_ref[...].astype(wide) + y_ref[...].astype(wide)
    hidden = hidden_ref[...]
    on = live[0].astype(wide)
    g_v, g_o, g_a = norm_back(hidden, inverse(hidden), mod_ref[4:5, :], g_y)
    grad = cot_ref[...].astype(wide) + g_v
    grad_ref[...] = grad
    gb_ref[...] = (mod_ref[2:3, :] * on * grad).astype(low)
    put_rows(s_ref, r2=on * jnp.sum(grad * branch_ref[...], axis=0, keepdims=True), r3=g_o, r4=g_a)


def middle_back(keep, core, y, hidden, branch, cot, modulation, live):
    shape = y.shape
    first = pl.BlockSpec(shape, lambda s, o=None: (0, 0))
    sums = (8, shape[1])
    return kernel(
        middle_back_kernel,
        "middle_back",
        live,
        [keep, core, y, hidden, branch, cot, modulation],
        (1,),
        [first] * 6 + [whole(modulation.shape)],
        [first, first, whole(sums)],
        [shape_of(shape, wide), shape_of(shape, low), shape_of(sums, wide)],
    )


def result_kernel(live, keep_ref, core_ref, y_ref, hidden_ref, cot_ref, mod_ref, *outs):
    mlp_out = keep_ref[...] + core_ref[...].astype(wide) + y_ref[...].astype(wide)
    on = live[0].astype(wide)
    result = (hidden_ref[...] + mod_ref[5:6, :] * on * mlp_out).astype(low)
    put_rows(outs[-1], r5=on * jnp.sum(cot_ref[...].astype(wide) * mlp_out, axis=0, keepdims=True))
    outs[0][...] = result


def result(keep, core, y, hidden, cot, modulation, live):
    shape = y.shape
    first = pl.BlockSpec(shape, lambda s, o=None: (0, 0))
    sums = (8, shape[1])
    return kernel(
        result_kernel,
        "result",
        live,
        [keep, core, y, hidden, cot, modulation],
        (1,),
        [first] * 5 + [whole(modulation.shape)],
        [first, whole(sums)],
        [shape_of(shape, low), shape_of(sums, wide)],
    )


def last_back_kernel(live, keep_ref, core_ref, y_ref, tok_ref, grad_ref, mod_ref, *outs):
    g_y = keep_ref[...] + core_ref[...].astype(wide) + y_ref[...].astype(wide)
    tok = tok_ref[...].astype(wide)
    g_v, g_o, g_a = norm_back(tok, inverse(tok), mod_ref[1:2, :], g_y)
    grad = (grad_ref[...] + g_v).astype(low)
    put_rows(outs[-1], r0=g_o, r1=g_a)
    outs[0][...] = grad


def last_back(keep, core, y, tok, grad, modulation, live):
    shape = y.shape
    first = pl.BlockSpec(shape, lambda s, o=None: (0, 0))
    sums = (8, shape[1])
    return kernel(
        last_back_kernel,
        "last_back",
        live,
        [keep, core, y, tok, grad, modulation],
        (1,),
        [first] * 5 + [whole(modulation.shape)],
        [first, whole(sums)],
        [shape_of(shape, low), shape_of(sums, wide)],
    )


def feed_forward_kernel(n, live, *refs):
    xs, cots = refs[:n], refs[n : 2 * n]
    mod_ref, up_ref, down_ref, act_ref, gu_ref, gm_ref, send_ref, keep_ref = refs[2 * n :]
    s = pl.program_id(0)
    block = (s + n // 2) % n
    x, cot = pick(block, xs), pick(block, cots)
    w_up = up_ref[...]
    gate_up = dot(x, w_up)
    half = gate_up.shape[1] // 2
    gate, up = gate_up[:, :half], gate_up[:, half:]
    sig = 1.0 / (1.0 + jnp.exp(-gate))
    silu = gate * sig
    act_ref[...] = (silu * up).astype(low)
    grad = (mod_ref[5:6, :] * live[0].astype(wide) * cot.astype(wide)).astype(low)
    gm_ref[...] = grad
    grad_act = dot_t(grad, down_ref[...])
    gu_ref[:, :half] = (grad_act * up * sig * (1.0 + gate * (1.0 - sig))).astype(low)
    gu_ref[:, half:] = (grad_act * silu).astype(low)
    grad_in = dot_t(gu_ref[...], w_up)

    @pl.when(s < n // 2)
    def _():
        send_ref[...] = grad_in.astype(low)

    @pl.when(s >= n // 2)
    def _():
        keep_ref[...] = grad_in


def feed_forward(xs, cots, modulation, w_up, w_down, live):
    n = len(xs)
    rows, width = xs[0].shape
    hidden = w_down.shape[0]
    half = n // 2

    def by_block(columns):
        return pl.BlockSpec((rows, columns), lambda s, o=None: ((s + half) % n, 0))

    return kernel(
        functools.partial(feed_forward_kernel, n),
        "feed_forward",
        live,
        [*xs, *cots, modulation, w_up, w_down],
        (n,),
        [whole(x.shape) for x in (*xs, *cots, modulation, w_up, w_down)],
        [
            by_block(hidden),
            by_block(2 * hidden),
            by_block(width),
            pl.BlockSpec((rows, width), lambda s, o=None: (jnp.minimum(s, half - 1), 0)),
            pl.BlockSpec((rows, width), lambda s, o=None: (jnp.maximum(s - half, 0), 0)),
        ],
        [
            shape_of((n * rows, hidden), low),
            shape_of((n * rows, 2 * hidden), low),
            shape_of((n * rows, width), low),
            shape_of((half * rows, width), low),
            shape_of((half * rows, width), wide),
        ],
        megabytes=36,
    )


def halves_of(acc_ref, at):
    rows = acc_ref.shape[0] // 2
    return [acc_ref[pl.ds(pl.multiple_of(i * rows, 8), rows), :] for i in (1 - at[0], at[0])]


def turned(xs, xt_ref):
    @pl.when(pl.program_id(0) == 0)
    def _():
        rows = xs[0].shape[0]
        for j, x in enumerate(xs):
            xt_ref[:, j * rows : (j + 1) * rows] = x[...].T


def turn_kernel(at, *refs):
    n = len(refs) // 2
    for a, b in zip(refs[:n], refs[n:]):
        b[...] = a[...].T


def turn_blocks(arrays, rows):
    tokens = arrays[0].shape[0]
    return kernel(
        turn_kernel,
        "turn_blocks",
        None,
        arrays,
        (tokens // rows,),
        [pl.BlockSpec((rows, a.shape[1]), lambda s, o=None: (s, 0)) for a in arrays],
        [pl.BlockSpec((a.shape[1], rows), lambda s, o=None: (0, s)) for a in arrays],
        [shape_of((a.shape[1], tokens), a.dtype) for a in arrays],
    )


def grad_part_kernel(n, at, *refs):
    xs, (b_ref, theirs, mine, xt_ref, acc_ref) = refs[:n], refs[n:]
    turned(xs, xt_ref)
    acc_ref[...] = dot(xt_ref[...], b_ref[...])
    for ref, value in zip((theirs, mine), halves_of(acc_ref, at)):
        ref[...] = value.astype(low)


def grad_part(xs, b, at, first, columns, chunk):
    tokens, width = len(xs) * xs[0].shape[0], xs[0].shape[1]
    out = pl.BlockSpec((width // 2, chunk), lambda s, o=None: (0, s))
    return kernel(
        functools.partial(grad_part_kernel, len(xs)),
        "grad_part",
        at,
        [*xs, b],
        (columns // chunk,),
        [whole(x.shape) for x in xs] + [pl.BlockSpec((tokens, chunk), lambda s, o=None: (0, first // chunk + s))],
        [out, out],
        [shape_of((width // 2, columns), low)] * 2,
        scratch=[pltpu.VMEM((width, tokens), low), pltpu.VMEM((width, chunk), wide)],
        megabytes=24,
    )


def grad_last_kernel(n, head_dim, cut, columns, at, *refs):
    xt_ref, mt_ref = refs[:2]
    parts, gbs = refs[2 : 2 + n], refs[2 + n : 2 + 2 * n]
    outs = refs[2 + 2 * n : 6 + 2 * n]
    acc_ref, out_ref = refs[6 + 2 * n :]
    padded = outs[0].shape[1]
    wide_columns = parts[0].shape[1]
    lane = lax.broadcasted_iota(jnp.int32, (wide_columns, padded), 0)
    target = (lane // LANES) * head_dim + lane % LANES
    column = lax.broadcasted_iota(jnp.int32, (wide_columns, padded), 1)
    inside = lane % LANES < head_dim
    per = columns // n
    narrow = sum(
        dot(part[...], jnp.where(inside & (column == target + p * per), 1.0, 0.0).astype(low))
        for p, part in enumerate(parts)
    ).astype(low)
    acc_ref[...] = dot(xt_ref[...], narrow)
    for half, value in enumerate(halves_of(acc_ref, at)):
        outs[half][...] = value[:cut].astype(low)
        outs[2 + half][: value.shape[0] - cut] = value[cut:].astype(low)

    rows = gbs[0].shape[0]
    out_ref[...] = sum(dot(mt_ref[:, j * rows : (j + 1) * rows], gbs[j][...]) for j in range(n))
    for half, value in enumerate(halves_of(out_ref, at)):
        ref = outs[2 + half]
        heads = [value[h * LANES : h * LANES + head_dim] for h in range(value.shape[0] // LANES)]
        value = jnp.concatenate(heads, axis=0)
        length, third = value.shape[0], value.shape[0] // 3
        start = xt_ref.shape[0] // 2 - cut
        spare = jnp.zeros((third, padded - columns), wide)
        ref[start : start + length] = jnp.where(
            lax.broadcasted_iota(jnp.int32, (length, padded), 1) < columns, value[:, :padded], 0.0
        ).astype(low)
        rest = [value[k * third : (k + 1) * third, columns:] for k in range(3)]
        ref[start + length :] = jnp.concatenate(rest + [spare], axis=1).astype(low)


def grad_last(xt, joined, mixed_t, gbs, at, head_dim, cut):
    n = joined.shape[1] // (3 * LANES)
    assert n == len(gbs)
    tokens, part = joined.shape[0], 3 * LANES
    width = xt.shape[0]
    columns = n * 3 * head_dim
    length = mixed_t.shape[0] // LANES * head_dim // 2
    assert gbs[0].shape[1] - columns == columns // 3 and length % 3 == 0
    padded = -(-columns // LANES) * LANES
    shapes = [(cut, padded), (width // 2 - cut + length + length // 3, padded)]
    return kernel(
        functools.partial(grad_last_kernel, n, head_dim, cut, columns),
        "grad_last",
        at,
        [xt, mixed_t, *[joined] * n, *gbs],
        (1,),
        [whole(xt.shape), whole(mixed_t.shape)]
        + [pl.BlockSpec((tokens, part), lambda s, o=None, h=h: (0, h)) for h in range(n)]
        + [whole(b.shape) for b in gbs],
        [whole(a) for a in shapes for _ in range(2)],
        [shape_of(a, low) for a in shapes for _ in range(2)],
        scratch=[
            pltpu.VMEM((width, padded), wide),
            pltpu.VMEM((mixed_t.shape[0], gbs[0].shape[1]), wide),
        ],
        megabytes=36,
    )


def add_halves_kernel(at, a_ref, b_ref, send_ref, keep_ref):
    value = a_ref[...].astype(wide) + b_ref[...].astype(wide)

    @pl.when(pl.program_id(0) == 0)
    def _():
        send_ref[...] = value.astype(low)

    @pl.when(pl.program_id(0) == 1)
    def _():
        keep_ref[...] = value


def add_halves(a, b, at):
    rows, columns = a.shape[0] // 2, a.shape[1]
    block = pl.BlockSpec((rows, columns), lambda s, o=None: (o[s], 0))
    return kernel(
        add_halves_kernel,
        "add_halves",
        at,
        [a, b],
        (2,),
        [block, block],
        [whole((rows, columns))] * 2,
        [shape_of((rows, columns), low), shape_of((rows, columns), wide)],
    )


def join_halves_kernel(at, a_ref, b_ref, o_ref):
    o_ref[...] = jnp.where(pl.program_id(0) == at[1], a_ref[...], b_ref[...])


def join_halves(mine, other, at):
    rows, columns = mine.shape
    return kernel(
        join_halves_kernel,
        "join_halves",
        at,
        [mine, other],
        (2,),
        [whole(mine.shape)] * 2,
        pl.BlockSpec((rows, columns), lambda s, o=None: (s, 0)),
        shape_of((2 * rows, columns), low),
    )


def place_columns(srcs, at, start, step, parts, up_ref):
    width = srcs[0].shape[1]
    piece, count = width // parts, len(srcs)

    def put(d, block):
        for p in range(parts):
            end = (p * count + d) * piece
            up_ref[:, end : end + piece] = block[:, p * piece : (p + 1) * piece]

    for j in range(count):
        block = srcs[j][pl.ds(start, step), :].astype(wide)
        for d in range(count):
            pl.when(at[j] == d)(functools.partial(put, d, block))


def place_first_kernel(parts, at, *refs):
    srcs, up_ref = refs[:-1], refs[-1]
    step = up_ref.shape[0]
    place_columns(srcs, at, pl.multiple_of(pl.program_id(0) * step, 16), step, parts, up_ref)


def place_first(blocks, at, parts):
    count = len(blocks)
    rows, width = blocks[0].shape
    step = 144
    return kernel(
        functools.partial(place_first_kernel, parts),
        "place_first",
        at,
        blocks,
        (rows // step,),
        [whole(b.shape) for b in blocks],
        pl.BlockSpec((step, width * count), lambda s, o=None: (s, 0)),
        shape_of((rows, 2 * width * count), wide),
    )


def place_second_kernel(count, parts, at, *refs):
    srcs, up_ref = refs[:count], refs[-1]
    step = up_ref.shape[0]
    place_columns(srcs, at, pl.multiple_of(pl.program_id(0) * step, 16), step, parts, up_ref)


def place_second(blocks, first, at, parts):
    count = len(blocks)
    width = blocks[0].shape[1]
    rows = first.shape[0]
    step = 144
    return pl.pallas_call(
        functools.partial(place_second_kernel, count, parts),
        grid_spec=pltpu.PrefetchScalarGridSpec(
            num_scalar_prefetch=1,
            grid=(rows // step,),
            in_specs=[whole(b.shape) for b in blocks] + [pl.BlockSpec(memory_space=pl.ANY)],
            out_specs=pl.BlockSpec((step, width * count), lambda s, o: (s, 1)),
        ),
        out_shape=shape_of(first.shape, wide),
        input_output_aliases={count + 1: 0},
        compiler_params=pltpu.CompilerParams(vmem_limit_bytes=32 * 1024 * 1024),
        cost_estimate=pl.CostEstimate(flops=1, bytes_accessed=1, transcendentals=0),
        name="place_second",
    )(at, *blocks, first)


def place_rows_kernel(at, *refs):
    srcs, o_ref = refs[:-1], refs[-1]
    rows = srcs[0].shape[0]
    for j, ref in enumerate(srcs):
        o_ref[pl.ds(pl.multiple_of(at[j] * rows, 8), rows), :] = ref[...].astype(wide)


def place_rows(blocks, at, chunk):
    rows, width = blocks[0].shape
    n = len(blocks)
    return kernel(
        place_rows_kernel,
        "place_rows",
        at,
        blocks,
        (width // chunk,),
        [pl.BlockSpec((rows, chunk), lambda s, o=None: (0, s))] * n,
        pl.BlockSpec((n * rows, chunk), lambda s, o=None: (0, s)),
        shape_of((n * rows, width), wide),
    )


def place_rows_of(srcs, at, halves, head_dim, columns, o_ref):
    count = len(srcs)
    heads = columns // (3 * head_dim) // halves

    def put(d, block):
        for t in range(3):
            for h in range(halves):
                for u in range(heads):
                    end = ((t * halves + h) * count + d) * heads + u
                    start = (h * heads + u) * 3 + t
                    o_ref[:, end * head_dim : (end + 1) * head_dim] = block[
                        :, start * head_dim : (start + 1) * head_dim
                    ]

    for j in range(count):
        block = srcs[j][...].astype(wide)
        for d in range(count):
            pl.when(at[j] == d)(functools.partial(put, d, block))


def place_top_kernel(halves, head_dim, columns, at, *refs):
    place_rows_of(refs[:-1], at, halves, head_dim, columns, refs[-1])


def place_top(blocks, at, halves, head_dim, rows, columns):
    count = len(blocks)
    cut, width = blocks[0].shape
    step = 96
    return kernel(
        functools.partial(place_top_kernel, halves, head_dim, columns),
        "place_top",
        at,
        blocks,
        (cut // step,),
        [pl.BlockSpec((step, width), lambda s, o: (s, 0))] * count,
        pl.BlockSpec((step, columns * count), lambda s, o: (s, 0)),
        shape_of((rows, columns * count), wide),
    )


def place_last_kernel(count, halves, head_dim, columns, at, *refs):
    seconds, lasts = refs[:count], refs[count : 2 * count]
    _, o_ref, out_ref = refs[2 * count :]
    place_rows_of(seconds, at, halves, head_dim, columns, o_ref)

    @pl.when(pl.program_id(0) == 0)
    def _():
        length = out_ref.shape[0] // count
        for j in range(count):
            value = lasts[j][...].astype(wide)
            width, side = columns, columns // 3
            at_row = pl.multiple_of(at[j] * length, 8)
            out_ref[pl.ds(at_row, length), :width] = value[:length, :width]
            rest = [value[length:, k * side : (k + 1) * side] for k in range(3)]
            out_ref[pl.ds(at_row, length), width:] = jnp.concatenate(rest, axis=0)


def place_last(blocks, top, at, halves, head_dim, length, columns):
    count = len(blocks)
    step, width = 96, blocks[0].shape[1]
    rows = top.shape[0]
    last = blocks[0].shape[0] // 2
    steps = last // step
    skip = rows // step - steps
    outs = [top.shape, (count * length, columns // 3 * 4)]
    return pl.pallas_call(
        functools.partial(place_last_kernel, count, halves, head_dim, columns),
        grid_spec=pltpu.PrefetchScalarGridSpec(
            num_scalar_prefetch=1,
            grid=(steps,),
            in_specs=[pl.BlockSpec((step, width), lambda s, o: (s, 0))] * count
            + [pl.BlockSpec((last, width), lambda s, o: (1, 0))] * count
            + [pl.BlockSpec(memory_space=pl.ANY)],
            out_specs=[pl.BlockSpec((step, columns * count), lambda s, o: (skip + s, 0)), whole(outs[1])],
        ),
        out_shape=[shape_of(a, wide) for a in outs],
        input_output_aliases={2 * count + 1: 0},
        compiler_params=pltpu.CompilerParams(vmem_limit_bytes=32 * 1024 * 1024),
        cost_estimate=pl.CostEstimate(flops=1, bytes_accessed=1, transcendentals=0),
        name="place_last",
    )(at, *blocks, *blocks, top)


def program(sizes, tokens, condition, valid, positions, w_qkv, w_out, w_up, w_down, w_ada, qk_gain, cotangent):
    n_img, n_row, n_col = sizes
    images, tile_rows, tile_cols, width = tokens.shape
    assert images == n_row == 4 and n_col == 4
    tile = tile_rows * tile_cols
    own = n_row * tile
    head_dim = qk_gain.shape[1]
    my_heads = width // head_dim // n_col
    me_img, me_row, me_col = lax.axis_index("img"), lax.axis_index("row"), lax.axis_index("col")
    order_col, order_row = block_order(n_col), block_order(n_row)
    halves = 2
    paired = n_img == 2

    def integers(*values):
        return jnp.stack(values).astype(jnp.int32)

    steps = lax.dynamic_index_in_dim(positions, me_row, 1, keepdims=False)
    bit = me_row % 2
    at_col = integers(me_col)
    at_img, at_columns, at_halves, live, at_tables, source, at_image = lax.optimization_barrier(
        (
            integers(me_img if paired else jnp.zeros_like(me_img)),
            integers(*[me_col ^ j for j in order_col]),
            integers(1 - bit, bit),
            lax.dynamic_slice_in_dim(valid, me_row, 1, axis=0),
            jnp.concatenate(
                [
                    integers(steps[0, 1, 0] - steps[0, 0, 0], steps[1, 0, 1] - steps[1, 0, 0]),
                    jnp.arange(n_row, dtype=jnp.int32),
                    integers(*[me_col ^ j for j in order_col]),
                ]
            ),
            integers(*[(me_row ^ k) * n_col + (me_col ^ j) for j in order_col for k in order_row]),
            integers(*[me_row ^ k for k in order_row]),
        )
    )

    def x_swap(v):
        return swap(v, "img", 2, 1)

    def y_swap(v):
        return swap(v, "col", n_col, 2)

    def core_swap(v):
        return swap(v, "col", n_col, 1)

    def z_swaps(parts):
        return [parts[0]] + [swap(p, "row", n_row, k) for p, k in zip(parts[1:], order_row[1:])]

    def over_rows(v):
        return lax.all_to_all(v, "row", split_axis=0, concat_axis=0, tiled=True)

    if paired:
        part_qkv = cut_qkv(w_qkv, at_col, 3 * halves, n_col)
        other_qkv = x_swap(part_qkv)
    else:
        full = cut_qkv(lax.all_gather(w_qkv, "img", axis=0, tiled=True), at_col, 3 * halves, n_col)
        part_qkv, other_qkv = full[: width // 2], full[width // 2 :]
    tok_row = over_rows(after(tokens, part_qkv).reshape(images * tile, width))
    cond = condition.astype(wide)
    silu_cond = jax.nn.silu(cond).astype(low)
    mod_columns = jnp.dot(after(silu_cond, part_qkv), w_ada, preferred_element_type=wide)
    mod_span = mod_columns.shape[1]
    mod_z = z_swaps([lax.dynamic_slice_in_dim(mod_columns, me_row ^ k, 1, axis=0) for k in order_row])
    cos_all, sin_a, sin_b = tables(after(at_tables, mod_columns), n_row, n_col, tile, tile_cols, head_dim)
    gain = after(jnp.pad(qk_gain, ((0, 0), (0, LANES - head_dim))), at_col)
    t = cos_all
    if paired:
        part_up, part_out, part_down = cut_rest(w_up, w_out, w_down, after(at_col, mod_columns), 2 * halves, n_col)
        other_out, other_down = x_swap(part_out), x_swap(part_down)
        other_silu = x_swap(after(silu_cond, mod_columns))
        t = part_down
    mod_row = cat(*[after(m, cos_all, t) for m in mod_z])
    mod_y, mod_core = y_swap(mod_row), core_swap(mod_row)
    t = mod_row
    mod_y, mod_core = lax.optimization_barrier((mod_y, mod_core, t))[:2]
    mod_last = core_swap(mod_y)
    tok_row = after(tok_row, mod_y)
    tok_y, tok_core = y_swap(tok_row), core_swap(tok_row)
    cot_row = over_rows(after(cotangent, tok_row).reshape(images * tile, width))
    modulation = place_modulation([mod_row, mod_y, mod_core, after(mod_last, tok_row)], source).reshape(6, width)
    tok_core = after(tok_core, modulation)
    if paired:
        other_qkv = after(other_qkv, tok_core)
    w_qkv_mine = widen(part_qkv, other_qkv, at_img, head_dim)
    tok_y = after(tok_y, w_qkv_mine)
    if paired:
        other_out, other_down, tok_y, other_silu = lax.optimization_barrier((other_out, other_down, tok_y, other_silu))
        other_up = x_swap(after(part_up, other_down))
    tok_last = core_swap(tok_y)
    toks = [tok_row, tok_y, tok_core, tok_last]

    attn_in, joined = project_qkv(toks, modulation, w_qkv_mine)
    cot_row = after(cot_row, joined)
    cot_y, cot_core = y_swap(cot_row), core_swap(cot_row)
    mixed, aug = attn_fwd(after(joined, cot_row), cos_all, sin_a, sin_b, gain, head_dim)
    if paired:
        w_out_mine = widen_rows(part_out, after(other_out, joined), at_img, head_dim)
    else:

        def cut_rows(w):
            full = lax.all_gather(w, "img", axis=0, tiled=True)
            length = full.shape[0] // (halves * n_col)
            return [
                lax.dynamic_slice_in_dim(full, (h * n_col + me_col) * length, length, axis=0) for h in range(halves)
            ]

        w_out_mine = widen_rows(*cut_rows(w_out), at_img, head_dim)
        w_down_mine = cat(*cut_rows(w_down))
        full_up = lax.all_gather(w_up, "img", axis=0, tiled=True)
        piece = full_up.shape[1] // (2 * halves * n_col)
        w_up_mine = jnp.concatenate(
            [
                lax.dynamic_slice_in_dim(full_up, (p * n_col + me_col) * piece, piece, axis=1)
                for p in range(2 * halves)
            ],
            axis=1,
        )
    cot_y, cot_core, mixed = lax.optimization_barrier((cot_y, cot_core, mixed))
    if paired:
        mixed, other_up = lax.optimization_barrier((mixed, other_up))
    sent, keep = project(mixed, w_out_mine, own)
    got = core_swap(sent)
    cot_last = core_swap(after(cot_y, sent))
    got = after(got, keep)
    sent = add_second(keep, got)
    got_y = y_swap(sent)
    cots = [cot_row, cot_y, cot_core, after(cot_last, sent)]
    t = cots[3]
    if paired:
        w_up_mine, w_down_mine = join(part_up, after(other_up, t), part_down, after(other_down, t), at_img)
        t = w_up_mine
    attn_t, mixed_t = turn_blocks([after(attn_in, t), mixed], own)
    hidden, branch, mlp_own = middle(keep, got, after(got_y, attn_t), tok_row, modulation, live)
    mlp_y, mlp_core = y_swap(mlp_own), core_swap(mlp_own)
    mlp_y, mlp_core = lax.optimization_barrier((mlp_y, mlp_core))
    xs = [mlp_own, mlp_y, mlp_core, core_swap(mlp_y)]

    act, grad_gu, grad_mlp, sent, keep = feed_forward(xs, cots, modulation, w_up_mine, w_down_mine, live)
    got = core_swap(sent)

    class Piece:
        def __init__(self, theirs, mine):
            self.sent = theirs
            self.value, self.got = mine, x_swap(theirs)

        def z_one(self, *earlier):
            self.sent, self.keep = add_halves(self.value, after(self.got, *earlier), at_halves)
            self.got = swap(self.sent, "row", n_row, 1)
            return self.sent

        def z_two(self, *earlier):
            self.sent = (self.keep + after(self.got, *earlier).astype(wide)).astype(low)
            self.got = swap(self.sent, "row", n_row, 2)
            return self.sent

        def z_three(self, *earlier):
            other = after(self.got, *earlier)
            self.keep = (self.sent.astype(wide) + other.astype(wide)).astype(low)
            self.got = swap(self.keep, "row", n_row, 1)
            return self.keep

        def y(self, *earlier):
            self.value = join_halves(self.keep, after(self.got, *earlier), at_halves)
            self.got = y_swap(self.value)
            return self.value

        def rows_in(self, *earlier):
            other = after(self.got, *earlier)
            self.sent = (self.value.astype(wide) + other.astype(wide)).astype(low)
            self.got = over_rows(self.sent)
            return self.sent

        def rows_out(self, *earlier):
            parts = after(self.got, *earlier).reshape(n_row, -1, self.got.shape[1])
            shard = jnp.sum(parts.astype(wide), axis=0).astype(low)
            self.sent = cat(*[shard] * n_row)
            self.got = over_rows(self.sent)
            return self.sent

        def y_rows(self, *earlier):
            self.value = after(self.got, *earlier)
            self.got, self.core = y_swap(self.value), core_swap(self.value)
            return self.value

        def end(self, *earlier):
            self.got, self.value = lax.optimization_barrier((self.got, self.value) + earlier)[:2]
            self.core, self.last = core_swap(self.value), core_swap(self.got)
            return self.got

        def blocks(self, *earlier):
            return [self.value, self.got, after(self.core, *earlier), after(self.last, *earlier)]

    got = after(got, keep)
    sent = add_second(keep, got)
    got_y = y_swap(sent)
    t = sent
    if paired:
        d = Piece(*grad_part([after(act, t)], grad_mlp, at_img, 0, width, 384))
        half_up = grad_gu.shape[1] // 2
        u_one = Piece(*grad_part(xs, after(grad_gu, d.sent), at_img, 0, half_up, 384))
        u_two = Piece(*grad_part(xs, after(grad_gu, u_one.sent), at_img, half_up, half_up, 384))
        t = u_two.sent
    grad_hidden, gb_own, sums_two = middle_back(
        keep, got, after(got_y, t), hidden, branch, cot_row, modulation, live
    )
    gb_y, gb_core = y_swap(gb_own), core_swap(gb_own)
    mlp_sent, mlp_keep = project(after(act, gb_own), w_down_mine, own)
    mlp_got = core_swap(mlp_sent)
    t = mlp_keep
    if paired:
        t = d.z_one(t)
    gb_y, gb_core = lax.optimization_barrier((gb_y, gb_core, t))[:2]
    gb_last = core_swap(gb_y)
    mlp_got = after(mlp_got, gb_y)
    mlp_next = add_second(mlp_keep, mlp_got)
    mlp_y = y_swap(mlp_next)
    gbs = [gb_own, gb_y, gb_core, after(gb_last, mlp_next)]
    joined_back, g_gain = attn_bwd(
        gbs, joined, aug, mixed, w_out_mine, cos_all, sin_a, sin_b, gain, head_dim, 0, my_heads
    )
    t = joined_back
    if paired:
        t = d.z_two(t)
        t = u_one.z_one(t)
    sent, keep = project(after(joined_back, t), w_qkv_mine, own, dot_t)
    got = core_swap(sent)
    t = sent
    if paired:
        rows = width // 2
        length = my_heads * head_dim // halves
        cut = (rows + length + length // 3) // 2
        g = grad_last(attn_t, after(joined_back, t), mixed_t, gbs, at_img, head_dim, cut)
        q_one, q_two = Piece(g[0], g[1]), Piece(g[2], g[3])
        t = g[0]
    got = after(got, t)
    sent = add_second(keep, got)
    got_y = y_swap(sent)
    t = sent
    if paired:
        t = u_two.z_one(t)
        t = d.z_three(t)
    out_own, sums_out = result(mlp_keep, mlp_got, after(mlp_y, t), hidden, cot_row, modulation, live)
    output = over_rows(out_own)
    t = out_own
    if paired:
        t = u_one.z_two(t)
    grad_own, sums_last = last_back(keep, got, after(got_y, t), tok_row, grad_hidden, modulation, live)
    vector = (sums_two + sums_last + sums_out)[:6]
    got = core_swap(vector)
    t = vector
    if paired:
        t = q_one.z_one(t)
        t = q_two.z_one(t)
    vector = vector + after(got, t)
    got = y_swap(vector)
    t = vector
    if paired:
        t = d.y(t)
        t = u_two.z_two(t)
        t = u_one.z_three(t)
        t = d.end(t)
    grad_mod = (vector + after(got, t)).astype(low)
    blocks = grad_mod.reshape(n_row, n_col, mod_span)
    mine = lax.dynamic_slice_in_dim(blocks, at_col[0], 1, axis=1)[:, 0]
    share_z = z_swaps([lax.dynamic_slice_in_dim(mine, me_row ^ k, 1, axis=0) for k in order_row])
    t = mine
    if paired:
        t = u_one.y(t)
        t = q_one.z_two(t)
    output = copied(after(output, t))
    t = output
    if paired:
        sum_down = place_rows(d.blocks(t), at_columns, 384)
        t = u_two.z_three(sum_down)
        t = q_two.z_two(t)
    share_rel = cat(*[after(v, t) for v in share_z])
    pick_image = at_image[None, :] == jnp.arange(images)[:, None]
    share = jnp.sum(jnp.where(pick_image[:, :, None], share_rel.astype(wide)[None], 0.0), axis=1).astype(low)
    back = lax.dot_general(share, w_ada, (((1,), (1,)), ((), ())), preferred_element_type=wide)
    flat = jnp.concatenate([back.reshape(-1), g_gain[:, :head_dim].reshape(-1)]).reshape(1, -1)
    got = swap(flat, "row", n_row, 1)
    t = flat
    if paired:
        other_share = x_swap(share)
        t = u_one.end(t)
        sum_up = place_first(u_one.blocks(t), at_columns, halves)
        t = u_two.y(sum_up)
        t = q_one.z_three(t)
    flat = flat + after(got, t)
    got = swap(flat, "row", n_row, 2)
    t = flat
    if paired:
        t = q_two.z_three(t)
    grad_tokens = over_rows(after(grad_own, t))

    def outer_product(a, b):
        return lax.dot_general(a, b, (((0,), (0,)), ((), ())), preferred_element_type=wide)

    if paired:
        grad_ada = outer_product(silu_cond, share) + outer_product(other_silu, after(other_share, t))
        t = grad_ada
    else:
        grad_ada = outer_product(
            lax.all_gather(silu_cond, "img", axis=0, tiled=True), lax.all_gather(share, "img", axis=0, tiled=True)
        )
    flat = flat + after(got, t)
    got = core_swap(flat)
    t = flat
    if paired:
        t = q_one.y(t)
        t = u_two.end(t)
    flat = flat + after(got, t)
    got = y_swap(flat)
    t = flat
    output = output.reshape(tokens.shape)
    if paired:
        t = q_two.y(t)
        sum_up = place_second(u_two.blocks(t), sum_up, at_columns, halves)
        t = sum_up
    flat = (flat + after(got, t))[0]
    grad_silu = flat[: images * width].reshape(images, width)
    gains = flat[images * width :].reshape(2, head_dim)
    s = 1.0 / (1.0 + jnp.exp(-cond))
    grad_condition = grad_silu * (s * (1.0 + cond * (1.0 - s)))
    if paired:
        gains_other = x_swap(gains)
        t = q_one.end(grad_condition)
        gains = gains + after(gains_other, t)
        columns = 3 * my_heads * head_dim
        top = place_top(q_one.blocks(gains), at_columns, halves, head_dim, rows, columns)
        grad_tokens = after(grad_tokens, top).astype(wide).reshape(tokens.shape)
        t = q_two.end(grad_tokens)
        sum_qkv, sum_out = place_last(q_two.blocks(t), top, at_columns, halves, head_dim, length, columns)
    else:
        gains = lax.psum(gains, "img")
        grad_tokens = grad_tokens.astype(wide).reshape(tokens.shape)

        def weight_grad(a, b):
            return lax.dot_general(a, b, (((0,), (0,)), ((), ())), preferred_element_type=wide).astype(low)

        def reduce_columns(partial, parts):
            summed = lax.psum_scatter(lax.psum(partial, "row"), "img", scatter_dimension=0, tiled=True)
            wholes = lax.all_gather(summed, "col", axis=0)
            rows = wholes.shape[1]
            wholes = wholes.reshape(n_col, rows, parts, -1)
            return jnp.transpose(wholes, (1, 2, 0, 3)).reshape(rows, -1).astype(wide)

        def reduce_rows(partial):
            wholes = lax.all_gather(lax.psum(partial, "row"), "col", axis=0)
            columns = wholes.shape[2]
            wholes = jnp.transpose(wholes.reshape(n_col, halves, -1, columns), (1, 0, 2, 3)).reshape(-1, columns)
            return lax.psum_scatter(wholes, "img", scatter_dimension=0, tiled=True).astype(wide)

        g_qkv = weight_grad(attn_in, joined_back).reshape(width, my_heads, 3, LANES)[..., :head_dim]
        g_qkv = jnp.swapaxes(g_qkv, 1, 2).reshape(width, -1)
        g_out = weight_grad(mixed, cat(*gbs)).reshape(my_heads, LANES, width)[:, :head_dim].reshape(-1, width)
        sum_up = reduce_columns(weight_grad(cat(*xs), grad_gu), 2 * halves)
        sum_down = reduce_rows(weight_grad(act, grad_mlp))
        sum_out = reduce_rows(g_out)
        sum_qkv = reduce_columns(g_qkv, 3 * halves)
    return output, grad_tokens, grad_condition, sum_qkv, sum_out, sum_up, sum_down, grad_ada, gains


def solution(mesh):
    sizes = tuple(mesh.shape[name] for name in ("img", "row", "col"))
    placed = (
        P("img", "row", "col", None),
        P("img", None),
        P("img"),
        P(None, "img", "row", "col"),
        P("img", None),
        P("img", None),
        P("img", None),
        P("img", None),
        P(None, ("row", "col")),
        P(),
        P("img", "row", "col", None),
    )
    return jax.shard_map(
        functools.partial(program, sizes),
        mesh=mesh,
        in_specs=placed,
        out_specs=(
            P("img", "row", "col", None),
            P("img", "row", "col", None),
            P("img", None),
            P("img", None),
            P("img", None),
            P("img", None),
            P("img", None),
            P(None, ("row", "col")),
            P(),
        ),
        check_vma=False,
    )
```
